32 devices in a mesh: sub: 8 (over z, y), rhs: 4 (over x, core).
Axes of the slice: x: 2, y: 2, z: 4, core: 2. Of those that a mesh axis runs over, the one named last changes fastest.
Arguments:
- stiffness: float32 [384, 4, 9216], P('sub'), may hold values from -1 to 2, as said below
- precond: float32 [384, 9216], P('sub'), may hold values from -0.625 to 0.625
- rhs_vec: float32 [8, 36864], P('rhs', 'sub'), may hold values from -50 to 50
- cotangent: float32 [8, 36864], P('rhs', 'sub'), may hold values from -6 to 6
- col_index: int32 [384, 4], P('sub'), may hold values from 0 to 59, as said below
- send_rows: int32 [8, 12], P('sub'), may hold values from 0 to 47, as said below
- counts: int32 [8], P('sub'), may hold values from 12 to 48, as said below
Outputs:
- solution: float32 [8, 36864], P('rhs', 'sub')
- grad_precond: float32 [384, 9216], P('sub')
The draws below stay inside these ranges and needn't reach their ends.
Inputs may be any that keep to these rules, and one draw needn't show every extreme that they name: `counts`: at least one subdomain has 48 live block rows. `send_rows`: for subdomain s, entries 0 to 5 are distinct live rows below counts[s] // 2 in increasing order, the first of them 0; entries 6 to 11 are distinct live rows from counts[s] // 2 on in increasing order, the last of them counts[s] - 1. Interface row j of the first group of subdomain s is coupled with interface row j of the second group of subdomain s - 1. `col_index`: index 6 + n is block n of the subdomain; indices below 6 and from 54 on are the blocks received from the previous and the next subdomain. Slot 0 of row n is 6 + n. A slot other than slot 0 that names 6 + n holds a zero block; rows that are not live hold only slot 0's block. `stiffness`: the operator A is symmetric and positive definite.
All inputs are finite; a program needn't handle non-finite values.
Results may differ from the reference program's by a relative error of at most 0.0003.
Values sent between devices are 32-bit elements; how exact they have to be, the bound alone decides.
No kernel may reach another device: no remote copies, remote signals or barrier semaphores. Data moves between devices by JAX's collectives and lax.ppermute only.
A program may use at most 128 MiB of HBM per device.

```python
import jax
import jax.numpy as jnp
from jax import lax

BS = 96
K = 4
NBLK = 48
IF = 6
ITERS = 4
RHS = 8
SUBS = 8
BLOCKS = 384


def layout(key):
    raw_draw = jax.random.randint(jax.random.fold_in(key, 11), (SUBS,), 0, 64)
    cube_val = raw_draw * raw_draw * raw_draw // 4096
    live_rows = NBLK // 4 + (NBLK - NBLK // 4) * cube_val // 64
    heaviest = jax.random.randint(jax.random.fold_in(key, 12), (), 0, SUBS)
    live_rows = jnp.where(jnp.arange(SUBS) == heaviest, NBLK, live_rows).astype(jnp.int32)
    position = jnp.arange(NBLK)[None, :]
    half_mark = (live_rows // 2)[:, None]
    limit = (1 << 16) * NBLK
    scores_left = jax.random.randint(jax.random.fold_in(key, 13), (SUBS, NBLK), 0, 1 << 16) * NBLK + position
    scores_right = jax.random.randint(jax.random.fold_in(key, 14), (SUBS, NBLK), 0, 1 << 16) * NBLK + position
    left_keys = jnp.where(position < half_mark, scores_left, limit + position)
    left_keys = jnp.where(position == 0, -1, left_keys)
    right_ok = (position >= half_mark) & (position < live_rows[:, None])
    right_keys = jnp.where(right_ok, scores_right, limit + position)
    right_keys = jnp.where(position == live_rows[:, None] - 1, -1, right_keys)
    left_pick = jnp.sort(jnp.argsort(left_keys, axis=1)[:, :IF], axis=1)
    right_pick = jnp.sort(jnp.argsort(right_keys, axis=1)[:, :IF], axis=1)
    sending = jnp.concatenate([left_pick, right_pick], axis=1).astype(jnp.int32)
    return (live_rows, sending)


def draw_counts(key, part):
    return layout(key)[0]


def draw_send_rows(key, part):
    return layout(key)[1]


def draw_col_index(key, part):
    live_rows, sending = layout(key)
    row_index = jnp.arange(NBLK)[None, :]
    own_col = jnp.broadcast_to(IF + row_index, (SUBS, NBLK))
    lower_col = jnp.where((row_index >= 1) & (row_index < live_rows[:, None]), own_col - 1, own_col)
    upper_col = jnp.where(row_index + 1 < live_rows[:, None], own_col + 1, own_col)
    sub_ids = jnp.arange(SUBS)[:, None]
    outer_col = own_col.at[sub_ids, sending[:, :IF]].set(jnp.broadcast_to(jnp.arange(IF)[None, :], (SUBS, IF)))
    outer_col = outer_col.at[sub_ids, sending[:, IF:]].set(jnp.broadcast_to(IF + NBLK + jnp.arange(IF)[None, :], (SUBS, IF)))
    column_table = jnp.stack([own_col, lower_col, upper_col, outer_col], axis=2)
    return column_table.reshape(SUBS * NBLK, K).astype(jnp.int32)


def draw_stiffness(key, part):
    live_rows, sending = layout(key)
    entry_bound = 0.8 / (4 * BS - 1)
    centre_raw = jax.random.uniform(jax.random.fold_in(key, 21), (SUBS, NBLK, BS, BS), jnp.float32, -entry_bound, entry_bound)
    centre_raw = 0.5 * (centre_raw + jnp.swapaxes(centre_raw, -1, -2))
    identity = jnp.eye(BS, dtype=jnp.float32)
    diag_vals = jax.random.uniform(jax.random.fold_in(key, 22), (SUBS, NBLK, BS), jnp.float32, 1.0, 2.0)
    centre = centre_raw * (1.0 - identity) + identity * diag_vals[..., None]
    edge_blocks = jax.random.uniform(jax.random.fold_in(key, 23), (SUBS, NBLK, BS, BS), jnp.float32, -entry_bound, entry_bound)
    row_index = jnp.arange(NBLK)[None, :]
    edge_ok = (row_index + 1 < live_rows[:, None]).astype(jnp.float32)
    upper_blk = edge_blocks * edge_ok[..., None, None]
    flipped = jnp.swapaxes(upper_blk, -1, -2)
    lower_blk = jnp.concatenate([jnp.zeros_like(flipped[:, :1]), flipped[:, :-1]], axis=1)
    face_blocks = jax.random.uniform(jax.random.fold_in(key, 24), (SUBS, IF, BS, BS), jnp.float32, -entry_bound, entry_bound)
    has_left = (jnp.arange(SUBS) >= 1).astype(jnp.float32)
    left_blk = face_blocks * has_left[:, None, None, None]
    right_src = jnp.concatenate([face_blocks[1:], jnp.zeros_like(face_blocks[:1])], axis=0)
    right_blk = jnp.swapaxes(right_src, -1, -2)
    sub_ids = jnp.arange(SUBS)[:, None]
    outer_blk = jnp.zeros((SUBS, NBLK, BS, BS), jnp.float32)
    outer_blk = outer_blk.at[sub_ids, sending[:, :IF]].set(left_blk)
    outer_blk = outer_blk.at[sub_ids, sending[:, IF:]].set(right_blk)
    stacked = jnp.stack([centre, lower_blk, upper_blk, outer_blk], axis=2)
    return stacked.reshape(SUBS * NBLK, K, BS * BS)


def draw_rhs_vec(key, part):
    sub_pos = (jnp.arange(BLOCKS * BS) // (NBLK * BS)).astype(jnp.float32)
    spread = jax.random.uniform(jax.random.fold_in(key, 32), (RHS, BLOCKS), jnp.float32, jnp.log(0.5), jnp.log(2.0))
    block_scale = jnp.repeat(jnp.exp(spread), BS, axis=1)
    sub_ramp = 1.0 + 2.0 * sub_pos / max(SUBS - 1, 1)
    base_noise = jnp.clip(jax.random.normal(jax.random.fold_in(key, 31), (RHS, BLOCKS * BS), jnp.float32), -6.0, 6.0)
    return base_noise * sub_ramp[None, :] * block_scale


def level_of(rng, shape, split, smallest, top_value):
    def one(dim, blocks):
        draws = jax.random.uniform(jax.random.fold_in(jax.random.fold_in(rng, 6), dim), (blocks,), jnp.float32, smallest / len(split), top_value / len(split))
        return jnp.repeat(jnp.exp(draws), shape[dim] // blocks).reshape((-1,) + (1,) * (len(shape) - dim - 1))

    loudness = one(*split[0])
    for cut in split[1:]:
        loudness = loudness * one(*cut)
    return loudness


def normal_values(stream_key, extent, width, bound, cuts=(), kind=jnp.bfloat16):
    entries = width * jax.random.normal(stream_key, extent, jnp.float32)
    if cuts:
        entries = entries * level_of(stream_key, extent, cuts, -0.22, 0.18)
    return jnp.clip(entries, -bound, bound).astype(kind)


def setup_inputs(seed: int = 0) -> dict:
    key_of = jax.random.split(jax.random.key(seed), 8)
    return {
        "stiffness": draw_stiffness(jax.random.fold_in(key_of[7], 71), 0),
        "precond": normal_values(key_of[1], (BLOCKS, BS * BS), BS ** -0.5, 0.625, ((0, 8),), jnp.float32),
        "rhs_vec": draw_rhs_vec(jax.random.fold_in(key_of[7], 71), 0),
        "cotangent": normal_values(key_of[3], (RHS, BLOCKS * BS), 1.0, 6.0, ((0, 4), (1, 8)), jnp.float32),
        "col_index": draw_col_index(jax.random.fold_in(key_of[7], 71), 0),
        "send_rows": draw_send_rows(jax.random.fold_in(key_of[7], 71), 0),
        "counts": draw_counts(jax.random.fold_in(key_of[7], 71), 0),
    }


highest = lax.Precision.HIGHEST

def reference(stiffness, precond, rhs_vec, cotangent, col_index, send_rows, counts):
    sub_count = counts.shape[0]
    rhs_count = rhs_vec.shape[0]
    sub_ids = jnp.arange(sub_count)
    blocks = stiffness.reshape(sub_count, NBLK, K, BS, BS)
    columns = col_index.reshape(sub_count, NBLK * K)
    live_mask = (jnp.arange(NBLK)[None, :] < counts[:, None]).astype(rhs_vec.dtype)
    source = rhs_vec.reshape(rhs_count, sub_count, NBLK, BS) * live_mask[None, :, :, None]
    target = cotangent.reshape(rhs_count, sub_count, NBLK, BS)

    def apply_stiff(vector):
        outgoing = vector[:, sub_ids[:, None], send_rows]
        empty_rim = jnp.zeros_like(outgoing[:, :1, :IF])
        from_left = jnp.concatenate([empty_rim, outgoing[:, :-1, IF:]], axis=1)
        from_right = jnp.concatenate([outgoing[:, 1:, :IF], empty_rim], axis=1)
        extended = jnp.concatenate([from_left, vector, from_right], axis=2)
        gathered = extended[:, sub_ids[:, None], columns].reshape(rhs_count, sub_count, NBLK, K, BS)
        return jnp.einsum('snkab,rsnkb->rsna', blocks, gathered, precision=highest)

    def precond_apply(weights, vector):
        projected = jnp.einsum('snab,rsnb->rsna', weights, vector, precision=highest)
        return vector + jnp.einsum('snab,rsna->rsnb', weights, projected, precision=highest)

    def inner_sum(first_vec, second_vec):
        return lax.optimization_barrier(jnp.sum(first_vec * second_vec, axis=(1, 2, 3)))

    def widen(scalars):
        return scalars[:, None, None, None]

    def solve(flat_weights):
        weights = flat_weights.reshape(sub_count, NBLK, BS, BS)
        residual = source
        precon = precond_apply(weights, residual)
        direction = precon
        norm_now = inner_sum(residual, precon)
        solution = jnp.zeros_like(source)
        for iteration in range(ITERS):
            applied = apply_stiff(direction)
            step_len = norm_now / inner_sum(direction, applied)
            solution = solution + widen(step_len) * direction
            residual = residual - widen(step_len) * applied
            if iteration + 1 < ITERS:
                precon = precond_apply(weights, residual)
                norm_next = inner_sum(residual, precon)
                direction = precon + widen(norm_next / norm_now) * direction
                norm_now = norm_next
        return solution
    solution, pullback = jax.vjp(solve, precond)
    gradient, = pullback(target)
    return (solution.reshape(rhs_count, sub_count * NBLK * BS), gradient)
```

```python
import functools

import jax
import jax.numpy as jnp
from jax import lax
from jax.experimental import pallas as pl
from jax.experimental.pallas import tpu as pltpu
from jax.sharding import PartitionSpec as P

BS = 96
K = 4
NBLK = 48
IF = 6
ITERS = 4
LANES = 128
OFF = 8
ROWS = 64
LOW = OFF - IF
HIGH = OFF + NBLK
CHUNK = 8
MIB = 1024 * 1024

highest = lax.Precision.HIGHEST
f32 = jnp.float32


def own(value):
    return value[:, OFF:HIGH]


def lane_ids():
    return lax.broadcasted_iota(jnp.int32, (BS, LANES), 1)


def diagonal():
    return lax.broadcasted_iota(jnp.int32, (BS, LANES), 0) == lane_ids()


def fold(prod):
    return jnp.sum(prod.reshape(BS // 8, 8, prod.shape[-1]), axis=0)


def make_operator(weights):
    gram = lax.dot_general(
        weights, weights, (((0,), (0,)), ((), ())), precision=highest, preferred_element_type=f32
    )
    wide = jnp.concatenate([gram, jnp.zeros((BS, LANES - BS), f32)], axis=1)
    return wide + jnp.where(diagonal(), 1.0, 0.0)


def scatter_apply(blocks, op_ref, x_ref, y_ref, col_ref, column_ref, wait):
    count = x_ref.shape[0]
    y_ref[...] = jnp.zeros_like(y_ref)

    def step(group, carry):
        wait(group)
        base = pl.multiple_of(group * CHUNK, CHUNK)
        tiles = [x_ref[r, pl.ds(base + OFF, CHUNK), :] for r in range(count)]
        for i in range(CHUNK):
            n = group * CHUNK + i
            oper = op_ref[n + OFF]
            images = [jnp.sum(oper * tiles[r][i : i + 1, :], axis=1, keepdims=True) for r in range(count)]
            if column_ref is not None:
                for r in range(column_ref.shape[0]):
                    column_ref[r, :BS, :] = jnp.where(lane_ids() == n + OFF, images[r], column_ref[r, :BS, :])
            for k in range(K):
                block = blocks[n, k]
                slot = col_ref[n, k] + LOW
                for r in range(count):
                    y_ref[r, slot, :, :BS] = y_ref[r, slot, :, :BS] + fold(block * images[r])
        return carry

    lax.fori_loop(0, NBLK // CHUNK, step, 0)


def ghost_images(op_ref, x_ref, g_ref):
    count = x_ref.shape[0]
    mask = diagonal()
    g_ref[...] = jnp.zeros_like(g_ref)
    for first in (LOW, HIGH):
        for j in range(IF):
            slot = first + j
            oper = op_ref[slot]
            for r in range(count):
                image = jnp.sum(oper * x_ref[r, slot : slot + 1, :], axis=1, keepdims=True)
                line = jnp.sum(fold(jnp.where(mask, image, 0.0)), axis=0, keepdims=True)
                g_ref[r, slot : slot + 1, :] = line


def ghost_apply(blocks, g_ref, y_ref, col_ref, list_ref):
    count = g_ref.shape[0]
    mask = diagonal()[:, :BS]

    def step(item, carry):
        for u in range(4):
            entry = list_ref[0, 1 + item * 4 + u]
            n = entry // K
            k = entry % K
            slot = col_ref[n, k] + LOW
            block = blocks[n, k]
            for r in range(count):
                image = jnp.sum(block * g_ref[r, pl.ds(slot, 1), :BS], axis=1, keepdims=True)
                y_ref[r, n + OFF, :, :BS] = y_ref[r, n + OFF, :, :BS] + fold(jnp.where(mask, image, 0.0))
        return carry

    lax.fori_loop(0, (list_ref[0, 0] + 3) // 4, step, 0)


def pack(y_ref, r):
    sub = lax.broadcasted_iota(jnp.int32, (8, LANES), 0)
    groups = []
    for g in range(ROWS // 8):
        total = jnp.zeros((8, LANES), f32)
        for i in range(8):
            line = jnp.sum(y_ref[r, g * 8 + i], axis=0, keepdims=True)
            total = jnp.where(sub == i, line, total)
        groups.append(total)
    return jnp.concatenate(groups, axis=0)


def unpack_columns(column_ref, r):
    return column_ref[r].T[:ROWS]


def messages(up_ref, down_ref, v_ref, h_ref, send_ref):
    for r in range(v_ref.shape[0]):
        for j in range(IF):
            down_ref[r, j : j + 1, :] = v_ref[r, pl.ds(send_ref[0, j] + OFF, 1), :]
            up_ref[r, j : j + 1, :] = v_ref[r, pl.ds(send_ref[0, IF + j] + OFF, 1), :]
            down_ref[r, 8 + j : 9 + j, :] = h_ref[r, LOW + j : LOW + j + 1, :]
            up_ref[r, 8 + j : 9 + j, :] = h_ref[r, HIGH + j : HIGH + j + 1, :]


def complete(v_ref, low_ref, high_ref, send_ref, edge_ref):
    for r in range(v_ref.shape[0]):
        for j in range(IF):
            for part, base, ghost, flag in ((low_ref, 0, LOW, 0), (high_ref, IF, HIGH, 1)):
                at = pl.ds(send_ref[0, base + j] + OFF, 1)
                v_ref[r, at, :] = v_ref[r, at, :] + part[r, 8 + j : 9 + j, :]
                slot = ghost + j
                summed = v_ref[r, slot : slot + 1, :] + part[r, j : j + 1, :]
                v_ref[r, slot : slot + 1, :] = jnp.where(edge_ref[flag] > 0, summed, 0.0)


def tile_sum(first, second):
    prod = first * second
    return jnp.sum(prod.reshape(prod.shape[0] // 8, 8, LANES), axis=0)


def stream(hbm, buffer, sems):
    def copy(group):
        part = pl.ds(group * CHUNK, CHUNK)
        return pltpu.make_async_copy(hbm.at[part], buffer.at[part], sems.at[group])

    for g in range(NBLK // CHUNK):
        copy(g).start()
    return lambda group: copy(group).wait()


def nowait(group):
    return None


def prepare_kernel(weights_ref, op_ref):
    for i in range(weights_ref.shape[0]):
        op_ref[i] = make_operator(weights_ref[i])


def list_kernel(col_ref, list_ref):
    def clear(i, carry):
        list_ref[0, i] = 0
        return carry

    lax.fori_loop(0, list_ref.shape[1], clear, 0)

    def step(i, count):
        col = col_ref[i // K, i % K]
        list_ref[0, 1 + count] = i
        return count + jnp.where((col < IF) | (col >= IF + NBLK), 1, 0)

    count = lax.fori_loop(0, NBLK * K, step, 0)
    list_ref[0, 0] = count
    for u in range(4):
        list_ref[0, 1 + count + u] = 0


def first_kernel(
    col_ref, list_ref, send_ref, edge_ref, count_ref, sigma_ref,
    blocks_hbm, op_own_ref, ghost_w_ref, base_ref,
    ops_ref, zero_ref, v1_ref, b1_ref, v2_ref, up_ref, down_ref, dots_ref,
    blocks, y_ref, column_ref, g_ref, sems,
):
    wait = stream(blocks_hbm, blocks, sems)
    count = v1_ref.shape[0]
    ops_ref[OFF:HIGH] = op_own_ref[...]
    for j in range(IF):
        ops_ref[LOW + j] = make_operator(ghost_w_ref[j])
        ops_ref[HIGH + j] = make_operator(ghost_w_ref[IF + j])
    column_ref[...] = jnp.zeros_like(column_ref)
    row = lax.broadcasted_iota(jnp.int32, (ROWS, LANES), 0)
    dead = (row >= count_ref[0] + OFF) & (row < HIGH)
    for r in range(count):
        zero_ref[r] = jnp.where(dead, 0.0, base_ref[r])
        zero_ref[count + r] = base_ref[count + r]
    scatter_apply(blocks, ops_ref, zero_ref, y_ref, col_ref, column_ref, wait)
    ghost_images(ops_ref, zero_ref, g_ref)
    ghost_apply(blocks, g_ref, y_ref, col_ref, list_ref)
    inner = (row >= OFF) & (row < HIGH)
    for r in range(count):
        v0 = jnp.where(inner, zero_ref[r], 0.0)
        target = jnp.where(inner, zero_ref[count + r], 0.0)
        image = unpack_columns(column_ref, r)
        v1 = jnp.where(inner, pack(y_ref, r) - sigma_ref[r] * v0, 0.0)
        v1_ref[r] = v1
        b1_ref[r] = jnp.where(inner, pack(y_ref, count + r), 0.0)
        dots_ref[r, 0] = tile_sum(v0, image)
        dots_ref[r, 1] = tile_sum(v1, image)
        dots_ref[r, 8] = tile_sum(target, image)
    half = y_ref.at[pl.ds(0, count)]
    scatter_apply(blocks, ops_ref, v1_ref, half, col_ref, column_ref, nowait)
    for r in range(count):
        target = jnp.where(inner, zero_ref[count + r], 0.0)
        image = unpack_columns(column_ref, r)
        dots_ref[r, 2] = tile_sum(v1_ref[r], image)
        dots_ref[r, 9] = tile_sum(target, image)
        v2_ref[r] = pack(y_ref, r) - sigma_ref[r] * v1_ref[r]
        for d in (3, 4, 5, 6, 7, 10, 11):
            dots_ref[r, d] = jnp.zeros((8, LANES), f32)
    messages(up_ref, down_ref, v2_ref, v2_ref, send_ref)


def second_kernel(
    col_ref, list_ref, send_ref, edge_ref, sigma_ref,
    blocks_hbm, ops_ref, zero_ref, v1_ref, v2_in, low_ref, high_ref, dots_in,
    v2_ref, v3_ref, v4_ref, k3_ref, up_ref, down_ref, dots_ref,
    blocks, y_ref, column_ref, g_ref, sems,
):
    wait = stream(blocks_hbm, blocks, sems)
    count = v1_ref.shape[0]
    column_ref[...] = jnp.zeros_like(column_ref)
    v2_ref[...] = v2_in[...]
    complete(v2_ref, low_ref, high_ref, send_ref, edge_ref)
    scatter_apply(blocks, ops_ref, v2_ref, y_ref, col_ref, column_ref, wait)
    ghost_images(ops_ref, v2_ref, g_ref)
    ghost_apply(blocks, g_ref, y_ref, col_ref, list_ref)
    row = lax.broadcasted_iota(jnp.int32, (ROWS, LANES), 0)
    inner = (row >= OFF) & (row < HIGH)
    for r in range(count):
        image = unpack_columns(column_ref, r)
        v3 = jnp.where(inner, pack(y_ref, r) - sigma_ref[r] * v2_ref[r], 0.0)
        v3_ref[r] = v3
        for d in (0, 1, 2, 8, 9):
            dots_ref[r, d] = dots_in[r, d]
        dots_ref[r, 3] = tile_sum(v1_ref[r], image)
        dots_ref[r, 4] = tile_sum(v2_ref[r], image)
        dots_ref[r, 5] = tile_sum(v3, image)
        dots_ref[r, 10] = tile_sum(jnp.where(inner, zero_ref[count + r], 0.0), image)
    scatter_apply(blocks, ops_ref, v3_ref, y_ref, col_ref, column_ref, nowait)
    for r in range(count):
        image = unpack_columns(column_ref, r)
        dots_ref[r, 6] = tile_sum(v3_ref[r], image)
        dots_ref[r, 11] = tile_sum(jnp.where(inner, zero_ref[count + r], 0.0), image)
        dots_ref[r, 7] = jnp.zeros((8, LANES), f32)
        k3_ref[r] = image
        v4_ref[r] = pack(y_ref, r) - sigma_ref[r] * v3_ref[r]
    messages(up_ref, down_ref, v4_ref, v4_ref, send_ref)


def moment_kernel(send_ref, edge_ref, v4_in, k3_ref, low_ref, high_ref, dots_in, v4_ref, dots_ref):
    v4_ref[...] = v4_in[...]
    complete(v4_ref, low_ref, high_ref, send_ref, edge_ref)
    lane = lax.broadcasted_iota(jnp.int32, (8, LANES), 1)
    for r in range(v4_ref.shape[0]):
        total = jnp.zeros((8, LANES), f32)
        for d in range(12):
            part = tile_sum(v4_ref[r], k3_ref[r]) if d == 7 else dots_in[r, d]
            whole = jnp.sum(jnp.sum(part, axis=0, keepdims=True), axis=1, keepdims=True)
            total = jnp.where(lane == d, whole, total)
        dots_ref[r] = total


def third_kernel(
    col_ref, list_ref, blocks_hbm, ops_ref, v4_ref, w5_ref, blocks, y_ref, g_ref, sems
):
    wait = stream(blocks_hbm, blocks, sems)
    scatter_apply(blocks, ops_ref, v4_ref, y_ref, col_ref, None, wait)
    ghost_images(ops_ref, v4_ref, g_ref)
    ghost_apply(blocks, g_ref, y_ref, col_ref, list_ref)
    for r in range(v4_ref.shape[0]):
        w5_ref[r] = pack(y_ref, r)


TARGETS = 10


def fourth_kernel(
    col_ref, send_ref, coef_ref, scale_ref,
    blocks_hbm, ops_ref, zero_ref, v1_ref, v2_ref, v3_ref, v4_ref, w5_ref, b1_ref,
    comb_ref, rho_ref, up_ref, down_ref,
    blocks, y_ref, x_ref, sems,
):
    wait = stream(blocks_hbm, blocks, sems)
    count = v1_ref.shape[0]
    row = lax.broadcasted_iota(jnp.int32, (ROWS, LANES), 0)
    inner = (row >= OFF) & (row < HIGH)
    for r in range(count):
        parts = [zero_ref[r], v1_ref[r], v2_ref[r], v3_ref[r], v4_ref[r], w5_ref[r], zero_ref[count + r], b1_ref[r]]
        parts = [jnp.where(inner, part, 0.0) for part in parts]
        for g in range(TARGETS):
            total = coef_ref[g, 0, r] * parts[0]
            for s in range(1, 8):
                total = total + coef_ref[g, s, r] * parts[s]
            comb_ref[g, r] = total
        x_ref[r] = comb_ref[5, r]
    scatter_apply(blocks, ops_ref, x_ref, y_ref, col_ref, None, wait)
    for r in range(count):
        rho_ref[r] = comb_ref[7, r] - scale_ref[0, r] * pack(y_ref, r)
    messages(up_ref, down_ref, rho_ref, rho_ref, send_ref)


def fifth_kernel(
    col_ref, list_ref, send_ref, edge_ref, scale_ref,
    blocks_hbm, ops_ref, rho_in, comb_ref, low_ref, high_ref,
    zeta_ref, sol_ref,
    blocks, y_ref, rho_ref, column_ref, g_ref, sems,
):
    wait = stream(blocks_hbm, blocks, sems)
    count = rho_in.shape[0]
    column_ref[...] = jnp.zeros_like(column_ref)
    rho_ref[...] = rho_in[...]
    complete(rho_ref, low_ref, high_ref, send_ref, edge_ref)
    scatter_apply(blocks, ops_ref, rho_ref, y_ref, col_ref, None, wait)
    ghost_images(ops_ref, rho_ref, g_ref)
    ghost_apply(blocks, g_ref, y_ref, col_ref, list_ref)
    for r in range(count):
        change = rho_ref[r] - comb_ref[7, r]
        zeta_ref[0, r] = own((comb_ref[8, r] + scale_ref[1, r] * change - scale_ref[2, r] * pack(y_ref, r))[None])[0]
        zeta_ref[1, r] = own((comb_ref[6, r] + change)[None])[0]
    lanes = lane_ids()
    for n in range(NBLK):
        for r in range(count):
            image = jnp.sum(ops_ref[n + OFF] * comb_ref[9, r, n + OFF : n + OFF + 1, :], axis=1, keepdims=True)
            column_ref[r, :BS, :] = jnp.where(lanes == n + OFF, image, column_ref[r, :BS, :])
    for r in range(count):
        sol_ref[r] = own(unpack_columns(column_ref, r)[None])[0]


def total_over(values, axis):
    size = lax.axis_size(axis)
    if size & (size - 1):
        return lax.psum(values, axis)
    step = 1
    while step < size:
        width = min(8, size // step)
        parts = [values]
        for d in range(1, width):
            parts.append(lax.ppermute(values, axis, [(i, i ^ (d * step)) for i in range(size)]))
        while len(parts) > 1:
            parts = [parts[i] + parts[i + 1] for i in range(0, len(parts), 2)]
        values = parts[0]
        step *= width
    return values


def exchange(up, down):
    size = lax.axis_size("sub")
    rising = [(i, i + 1) for i in range(size - 1)]
    falling = [(j, i) for i, j in rising]
    return lax.ppermute(up, "sub", rising), lax.ppermute(down, "sub", falling)


def scalars(moments, products, sigma):
    zero = jnp.zeros_like(sigma)
    one = jnp.ones_like(sigma)

    def quad(poly, shifted):
        total = zero
        for i in range(ITERS):
            for j in range(ITERS):
                pair = poly[i] * poly[j]
                total = total + pair * moments[i + j]
                del pair
        return total

    def inner(first, second):
        total = zero
        for i in range(len(first)):
            for j in range(len(second)):
                if i + j < len(moments):
                    total = total + first[i] * second[j] * moments[i + j]
        return total

    def apply(poly):
        out = [zero] * (len(poly) + 1)
        for j, value in enumerate(poly):
            out[j] = out[j] + sigma * value
            out[j + 1] = out[j + 1] + value
        return out

    def add(first, second, scale):
        size = max(len(first), len(second))
        first = list(first) + [zero] * (size - len(first))
        second = list(second) + [zero] * (size - len(second))
        return [a + scale * b for a, b in zip(first, second)]

    resid = [[one]]
    direc = [[one]]
    image = []
    step, ratio, norm, curv = [], [zero], [moments[0]], []
    for i in range(ITERS):
        image.append(apply(direc[i]))
        curv.append(inner(direc[i], image[i]))
        step.append(norm[i] / curv[i])
        if i + 1 < ITERS:
            resid.append(add(resid[i], image[i], -step[i]))
            norm.append(inner(resid[i + 1], resid[i + 1]))
            ratio.append(norm[i + 1] / norm[i])
            direc.append(add(resid[i + 1], direc[i], ratio[i + 1]))
    cot = []
    for i in range(ITERS):
        total = zero
        for j, value in enumerate(resid[i]):
            total = total + value * products[j]
        cot.append(total)
    along = [cot[0]]
    for i in range(1, ITERS):
        along.append(cot[i] + ratio[i] * along[i - 1])

    def row(poly):
        return list(poly) + [zero] * (8 - len(poly))

    def scaled(first, scale):
        return [scale * a for a in first]

    target = [zero] * 6 + [one, zero]
    resid_rows = [row(poly) for poly in resid]
    image_rows = [row(poly) for poly in image]

    def resid_prod(i):
        return [norm[l] if l == i else zero for l in range(ITERS)]

    def image_prod(i):
        return [norm[i] / step[i] if l == i else (-norm[l] / step[i] if l == i + 1 else zero) for l in range(ITERS)]

    def along_dir(prod, i):
        total = prod[0]
        for l in range(1, i + 1):
            total = prod[l] + ratio[l] * total
        return total

    def operator_prod(prod):
        out = []
        for l in range(ITERS - 1):
            value = (prod[l] - prod[l + 1]) / step[l]
            if l > 0:
                value = value - ratio[l] * (prod[l - 1] - prod[l]) / step[l - 1]
            out.append(value)
        return out + [zero]

    last = ITERS - 1
    step_bar = along[last]
    curv_bar = -step_bar * step[last] / curv[last]
    dir_row = add(scaled(target, step[last]), image_rows[last], 2 * curv_bar)
    dir_prod = add(scaled(cot, step[last]), image_prod(last), 2 * curv_bar)
    norm_bar = step_bar / curv[last]
    rho_row = [zero] * 8
    rho_prod = [zero] * ITERS
    zetas = [None] * ITERS
    rho_rows = []
    for i in (2, 1, 0):
        ratio_bar = along_dir(dir_prod, i)
        full = norm_bar + ratio_bar / norm[i]
        zeta_row = add(dir_row, resid_rows[i + 1], full)
        zetas[i + 1] = zeta_row
        rho_row = add(add(rho_row, zeta_row, one), resid_rows[i + 1], full)
        rho_prod = add(add(rho_prod, dir_prod, one), resid_prod(i + 1), 2 * full)
        rho_rows.append(rho_row)
        step_bar = along[i] - (rho_prod[i] - rho_prod[i + 1]) / step[i]
        curv_bar = -step_bar * step[i] / curv[i]
        if i == 2:
            oper = [zero] * 8
            for k in range(5):
                if k < 4:
                    oper[k] = oper[k] + sigma * rho_row[k]
                    oper[k + 1] = oper[k + 1] + rho_row[k]
                else:
                    oper[5] = oper[5] + rho_row[4]
            oper[7] = rho_row[6]
        else:
            oper = [zero] * 8
        kept = add(scaled(dir_row, ratio[i + 1]), target, step[i])
        kept = add(kept, image_rows[i], 2 * curv_bar)
        dir_row = add(kept, oper, -step[i])
        oper_prod = operator_prod(rho_prod)
        dir_prod = add(add(scaled(dir_prod, ratio[i + 1]), cot, step[i]), image_prod(i), 2 * curv_bar)
        dir_prod = add(dir_prod, oper_prod, -step[i])
        norm_bar = -ratio_bar * norm[i + 1] / (norm[i] * norm[i]) + step_bar / curv[i]
    zetas[0] = add(dir_row, resid_rows[0], norm_bar)
    answer = [zero] * 8
    for i in range(ITERS):
        answer = add(answer, row(direc[i]), step[i])
    combos = [resid_rows[1], resid_rows[2], resid_rows[3], zetas[3], zetas[2], rho_rows[1], zetas[1], rho_rows[2], zetas[0], answer]
    coefs = jnp.stack([jnp.stack(combo) for combo in combos])
    scales = jnp.stack([step[1], ratio[1], step[0]])
    return coefs, scales


def vmem():
    return pl.BlockSpec(memory_space=pltpu.VMEM)


def smem():
    return pl.BlockSpec(memory_space=pltpu.SMEM)


def hbm():
    return pl.BlockSpec(memory_space=pl.ANY)


def shards(stiffness, precond, rhs_vec, cotangent, col_index, send_rows, counts):
    count = rhs_vec.shape[0]
    sub = lax.axis_index("sub")
    size = lax.axis_size("sub")
    edge = jnp.stack([sub > 0, sub + 1 < size]).astype(jnp.int32)
    sending = send_rows[0]
    base = jnp.concatenate([rhs_vec, cotangent], axis=0).reshape(2 * count, NBLK, BS)

    outgoing = jnp.take(base, sending, axis=1).transpose(1, 0, 2).reshape(2 * IF, 2 * count * BS)
    outgoing = jnp.concatenate([jnp.take(precond, sending, axis=0), outgoing], axis=1)
    before, after = exchange(outgoing[IF:], outgoing[:IF])

    diag = stiffness[:, 0, :: BS + 1]
    stats = jnp.stack([jnp.sum(precond * precond), jnp.sum(diag)])
    stats = lax.psum(stats, "sub") / (size * NBLK * BS)
    sigma = jnp.full((count,), (1.0 + stats[0]) * stats[1])

    blocks = stiffness.reshape(NBLK, K, BS, BS)
    weights = precond.reshape(NBLK, BS, BS)
    op_own = pl.pallas_call(
        prepare_kernel,
        grid=(NBLK // CHUNK,),
        in_specs=[pl.BlockSpec((CHUNK, BS, BS), lambda i: (i, 0, 0))],
        out_specs=pl.BlockSpec((CHUNK, BS, LANES), lambda i: (i, 0, 0)),
        out_shape=jax.ShapeDtypeStruct((NBLK, BS, LANES), f32),
        name="prepare",
    )(weights)
    halo_list = pl.pallas_call(
        list_kernel,
        in_specs=[smem()],
        out_specs=smem(),
        out_shape=jax.ShapeDtypeStruct((1, NBLK * K + 8), jnp.int32),
        name="halo_list",
    )(col_index)

    ghosts = jnp.concatenate([before, after], axis=0)
    ghost_w = ghosts[:, : BS * BS].reshape(2 * IF, BS, BS)
    ghost_v = ghosts[:, BS * BS :].reshape(2 * IF, 2 * count, BS).transpose(1, 0, 2)
    pads = jnp.zeros((2 * count, LOW, BS), f32)
    extended = jnp.concatenate([pads, ghost_v[:, :IF], base, ghost_v[:, IF:], pads], axis=1)
    extended = jnp.pad(extended, ((0, 0), (0, 0), (0, LANES - BS)))

    rows = jax.ShapeDtypeStruct((count, ROWS, LANES), f32)
    message = jax.ShapeDtypeStruct((count, 16, LANES), f32)
    dots = jax.ShapeDtypeStruct((count, 12, 8, LANES), f32)
    big = pltpu.VMEM((NBLK, K, BS, BS), f32)
    sems = pltpu.SemaphoreType.DMA((NBLK // CHUNK,))
    partial = lambda r: pltpu.VMEM((r, ROWS, 8, LANES), f32)
    square = pltpu.VMEM((count, LANES, LANES), f32)
    ghost_rows = lambda r: pltpu.VMEM((r, ROWS, LANES), f32)
    params = pltpu.CompilerParams(vmem_limit_bytes=40 * MIB)

    ops, zero, v1, b1, v2, up, down, dot = pl.pallas_call(
        first_kernel,
        in_specs=[smem()] * 6 + [hbm()] + [vmem()] * 3,
        out_specs=[vmem()] * 8,
        out_shape=[
            jax.ShapeDtypeStruct((ROWS, BS, LANES), f32),
            jax.ShapeDtypeStruct((2 * count, ROWS, LANES), f32),
            rows, rows, rows, message, message, dots,
        ],
        scratch_shapes=[big, partial(2 * count), square, ghost_rows(2 * count), sems],
        compiler_params=params,
        name="first",
    )(col_index, halo_list, send_rows, edge, counts, sigma, blocks, op_own, ghost_w, extended)
    low, high = exchange(up, down)

    v2, v3, v4, k3, up, down, dot = pl.pallas_call(
        second_kernel,
        in_specs=[smem()] * 5 + [hbm()] + [vmem()] * 7,
        out_specs=[vmem()] * 7,
        out_shape=[rows, rows, rows, rows, message, message, dots],
        scratch_shapes=[big, partial(count), square, ghost_rows(count), sems],
        compiler_params=params,
        name="second",
    )(col_index, halo_list, send_rows, edge, sigma, blocks, ops, zero, v1, v2, low, high, dot)
    low, high = exchange(up, down)

    v4, dot = pl.pallas_call(
        moment_kernel,
        in_specs=[smem()] * 2 + [vmem()] * 5,
        out_specs=[vmem()] * 2,
        out_shape=[rows, jax.ShapeDtypeStruct((count, 8, LANES), f32)],
        name="moments",
    )(send_rows, edge, v4, k3, low, high, dot)
    sums = total_over(dot[:, 0, :12], "sub")

    w5 = pl.pallas_call(
        third_kernel,
        in_specs=[smem()] * 2 + [hbm()] + [vmem()] * 2,
        out_specs=vmem(),
        out_shape=rows,
        scratch_shapes=[big, partial(count), ghost_rows(count), sems],
        compiler_params=params,
        name="third",
    )(col_index, halo_list, blocks, ops, v4)

    coefs, scales = scalars([sums[:, i] for i in range(8)], [sums[:, 8 + i] for i in range(4)], sigma)

    comb, rho, up, down = pl.pallas_call(
        fourth_kernel,
        in_specs=[smem()] * 4 + [hbm()] + [vmem()] * 8,
        out_specs=[vmem()] * 4,
        out_shape=[jax.ShapeDtypeStruct((TARGETS, count, ROWS, LANES), f32), rows, message, message],
        scratch_shapes=[big, partial(count), ghost_rows(count), sems],
        compiler_params=params,
        name="fourth",
    )(col_index, send_rows, coefs, scales, blocks, ops, zero, v1, v2, v3, v4, w5, b1)
    low, high = exchange(up, down)

    zeta, answer = pl.pallas_call(
        fifth_kernel,
        in_specs=[smem()] * 5 + [hbm()] + [vmem()] * 5,
        out_specs=[vmem()] * 2,
        out_shape=[
            jax.ShapeDtypeStruct((2, count, NBLK, LANES), f32),
            jax.ShapeDtypeStruct((count, NBLK, LANES), f32),
        ],
        scratch_shapes=[big, partial(count), ghost_rows(count), square, ghost_rows(count), sems],
        compiler_params=params,
        name="fifth",
    )(col_index, halo_list, send_rows, edge, scales, blocks, ops, rho, comb, low, high)

    resid = jnp.concatenate([zero[None, :count, OFF:HIGH, :BS], comb[:3, :, OFF:HIGH, :BS]], axis=0)
    adjoint = jnp.concatenate([zeta[..., :BS], comb[4:5, :, OFF:HIGH, :BS], comb[3:4, :, OFF:HIGH, :BS]], axis=0)
    mixed = jnp.einsum("irna,irnb->nab", resid, adjoint, precision=highest)
    mixed = mixed + jnp.swapaxes(mixed, 1, 2)
    grad = jnp.einsum("nab,nbc->nac", weights, mixed, precision=highest)
    grad = lax.psum(grad, "rhs")
    return answer[..., :BS].reshape(count, NBLK * BS), grad.reshape(NBLK, BS * BS)


def solution(mesh):
    in_specs = (
        P("sub", None, None),
        P("sub", None),
        P("rhs", "sub"),
        P("rhs", "sub"),
        P("sub", None),
        P("sub", None),
        P("sub"),
    )
    out_specs = (P("rhs", "sub"), P("sub", None))
    return jax.shard_map(shards, mesh=mesh, in_specs=in_specs, out_specs=out_specs, check_vma=False)
```

```python
import functools

import jax
import jax.numpy as jnp
from jax import lax
from jax.experimental import pallas as pl
from jax.experimental.pallas import tpu as pltpu
from jax.sharding import PartitionSpec as P

BS = 96
K = 4
NBLK = 48
IF = 6
ITERS = 4
EARLY = 16
LATE = 4
CUTS = BS * BS // 128
LANES = 128
OFF = 8
ROWS = 64
LOW = OFF - IF
HIGH = OFF + NBLK
CHUNK = 8
MIB = 1024 * 1024

highest = lax.Precision.HIGHEST
f32 = jnp.float32


def own(value):
    return value[:, OFF:HIGH]


def lane_ids():
    return lax.broadcasted_iota(jnp.int32, (BS, LANES), 1)


def diagonal():
    pos = lax.broadcasted_iota(jnp.int32, (BS, LANES), 0)
    row = (pos & ~31) + 4 * (pos & 7) + ((pos >> 3) & 3)
    return row == lane_ids()


def fold(prod):
    return jnp.sum(prod.reshape(BS // 8, 8, prod.shape[-1]), axis=0)


def unflatten(read):
    lane = lax.broadcasted_iota(jnp.int32, (8, LANES), 1)
    out = []
    for h in range(BS // 32):
        one, two, three = (read(24 * h + m) for m in range(3))
        out.append(jnp.where(lane < BS, one, 0.0))
        mixed = jnp.where(lane < 32, pltpu.roll(one, 32, 1), pltpu.roll(two, 32, 1))
        out.append(jnp.where(lane < BS, mixed, 0.0))
        mixed = jnp.where(lane < 64, pltpu.roll(two, 64, 1), pltpu.roll(three, 64, 1))
        out.append(jnp.where(lane < BS, mixed, 0.0))
        out.append(jnp.where(lane < BS, pltpu.roll(three, 96, 1), 0.0))
    return jnp.concatenate(out, axis=0)


def flatten(block, write):
    lane = lax.broadcasted_iota(jnp.int32, (8, LANES), 1)
    for h in range(BS // 32):
        one, two, three, four = (block[32 * h + 8 * j : 32 * h + 8 * j + 8] for j in range(4))
        two = pltpu.roll(two, 96, 1)
        three = pltpu.roll(three, 64, 1)
        write(24 * h, jnp.where(lane < BS, one, two))
        write(24 * h + 1, jnp.where(lane < 64, two, three))
        write(24 * h + 2, jnp.where(lane < 32, three, pltpu.roll(four, 32, 1)))


def make_operator(weights, gram_ref):
    gram = lax.dot_general(
        weights, weights, (((0,), (0,)), ((), ())), precision=highest, preferred_element_type=f32
    )
    gram_ref[...] = gram[:BS]
    rows = [gram_ref[pl.ds(32 * h + j, 8, stride=4), :] for h in range(BS // 32) for j in range(4)]
    return jnp.concatenate(rows, axis=0) + jnp.where(diagonal(), 1.0, 0.0)


def scatter_apply(blocks, op_ref, x_ref, y_ref, col_ref, column_ref):
    count = x_ref.shape[0]
    y_ref[...] = jnp.zeros_like(y_ref)

    def step(group, carry):
        base = pl.multiple_of(group * CHUNK, CHUNK)
        tiles = [x_ref[r, pl.ds(base + OFF, CHUNK), :] for r in range(count)]
        for i in range(CHUNK):
            n = group * CHUNK + i
            oper = op_ref[n + OFF]
            images = [jnp.sum(oper * tiles[r][i : i + 1, :], axis=1, keepdims=True) for r in range(count)]
            if column_ref is not None:
                for r in range(column_ref.shape[0]):
                    column_ref[r] = jnp.where(lane_ids() == n + OFF, images[r], column_ref[r])
            for k in range(K):
                block = blocks[n, k]
                slot = col_ref[k, n] + LOW
                for r in range(count):
                    y_ref[r, slot] = y_ref[r, slot] + fold(block * images[r])
        return carry

    lax.fori_loop(0, NBLK // CHUNK, step, 0)


def ghost_images(op_ref, x_ref, g_ref):
    count = x_ref.shape[0]
    mask = diagonal()
    g_ref[...] = jnp.zeros_like(g_ref)
    for first in (LOW, HIGH):
        for j in range(IF):
            slot = first + j
            oper = op_ref[slot]
            for r in range(count):
                image = jnp.sum(oper * x_ref[r, slot : slot + 1, :], axis=1, keepdims=True)
                line = jnp.sum(fold(jnp.where(mask, image, 0.0)), axis=0, keepdims=True)
                g_ref[r, slot : slot + 1, :] = line


def ghost_apply(blocks, g_ref, y_ref, col_ref, list_ref):
    count = g_ref.shape[0]
    mask = diagonal()

    def step(item, carry):
        for u in range(4):
            entry = list_ref[0, 1 + item * 4 + u]
            n = entry >> 2
            k = entry & 3
            slot = col_ref[k, n] + LOW
            block = blocks[n, k]
            for r in range(count):
                image = jnp.sum(block * g_ref[r, pl.ds(slot, 1), :], axis=1, keepdims=True)
                y_ref[r, n + OFF] = y_ref[r, n + OFF] + fold(jnp.where(mask, image, 0.0))
        return carry

    lax.fori_loop(0, (list_ref[0, 0] + 3) >> 2, step, 0)


def pack(y_ref, r):
    sub = lax.broadcasted_iota(jnp.int32, (8, LANES), 0)
    groups = []
    for g in range(ROWS // 8):
        total = jnp.zeros((8, LANES), f32)
        for i in range(8):
            line = jnp.sum(y_ref[r, g * 8 + i], axis=0, keepdims=True)
            total = jnp.where(sub == i, line, total)
        groups.append(total)
    return jnp.concatenate(groups, axis=0)


def unpack_columns(column_ref, square_ref, r):
    for h in range(BS // 32):
        for j in range(4):
            start = 32 * h + 8 * j
            square_ref[pl.ds(32 * h + j, 8, stride=4), :] = column_ref[r, start : start + 8, :]
    square_ref[BS:, :] = jnp.zeros((LANES - BS, LANES), f32)
    return square_ref[...].T[:ROWS]


def messages(up_ref, down_ref, v_ref, send_ref, extra_ref=None):
    for r in range(v_ref.shape[0]):
        for j in range(IF):
            low = pl.ds(send_ref[0, j] + OFF, 1)
            high = pl.ds(send_ref[0, IF + j] + OFF, 1)
            down_ref[r, j : j + 1, :] = v_ref[r, low, :]
            up_ref[r, j : j + 1, :] = v_ref[r, high, :]
            down_ref[r, 8 + j : 9 + j, :] = v_ref[r, LOW + j : LOW + j + 1, :]
            up_ref[r, 8 + j : 9 + j, :] = v_ref[r, HIGH + j : HIGH + j + 1, :]
            if extra_ref is not None:
                down_ref[r, 16 + j : 17 + j, :] = extra_ref[r, low, :]
                up_ref[r, 16 + j : 17 + j, :] = extra_ref[r, high, :]


def complete(v_ref, low_ref, high_ref, send_ref, edge_ref):
    for r in range(v_ref.shape[0]):
        for j in range(IF):
            for part, base, ghost, flag in ((low_ref, 0, LOW, 0), (high_ref, IF, HIGH, 1)):
                at = pl.ds(send_ref[0, base + j] + OFF, 1)
                v_ref[r, at, :] = v_ref[r, at, :] + part[r, 8 + j : 9 + j, :]
                slot = ghost + j
                summed = v_ref[r, slot : slot + 1, :] + part[r, j : j + 1, :]
                v_ref[r, slot : slot + 1, :] = jnp.where(edge_ref[flag] > 0, summed, 0.0)


def tile_sum(first, second):
    prod = first * second
    return jnp.sum(prod.reshape(prod.shape[0] // 8, 8, LANES), axis=0)


def whole_sum(tile):
    return jnp.sum(jnp.sum(tile, axis=0, keepdims=True), axis=1, keepdims=True)


def inner_rows():
    row = lax.broadcasted_iota(jnp.int32, (ROWS, LANES), 0)
    return (row >= OFF) & (row < HIGH)


def pack_kernel(send_ref, raw_ref, base_ref, up_ref, down_ref):
    for part, ref in ((0, down_ref), (IF, up_ref)):
        for j in range(IF):
            n = send_ref[0, part + j]
            start = (n >> 3) * (8 * CUTS) + (n & 7)
            for i in range(CUTS // 8):
                ref[j, 8 * i : 8 * i + 8, :] = raw_ref[pl.ds(start + 64 * i, 8, stride=8), :]
            ref[j, CUTS:, :] = jnp.zeros((8, LANES), f32)
            for r in range(base_ref.shape[0]):
                ref[j, CUTS + r : CUTS + r + 1, :] = base_ref[r, pl.ds(n + OFF, 1), :]


def prepare_kernel(col_ref, stiff_ref, raw_ref, blocks_ref, weights_ref, ops_ref, list_ref, stats_ref, gram_ref):
    mask = diagonal()

    def step(group, carry):
        count, squares, traces = carry
        for i in range(CHUNK):
            n = group * CHUNK + i
            for k in range(K):
                block = unflatten(lambda q: stiff_ref[pl.ds(n * (CUTS * K) + 4 * q + k, 8, stride=12), :])
                blocks_ref[n, k] = block
                if k == 0:
                    traces = traces + fold(jnp.where(mask, block, 0.0))
                col = col_ref[k, n]
                list_ref[0, 1 + count] = n * K + k
                count = count + jnp.where((col < IF) | (col >= IF + NBLK), 1, 0)
            weights = unflatten(lambda q: raw_ref[pl.ds(group * (8 * CUTS) + 8 * q + i, 8, stride=24), :])
            weights_ref[n] = weights
            squares = squares + fold(weights * weights)
            ops_ref[n] = make_operator(weights, gram_ref.at[i & 1])
        return count, squares, traces

    blank = jnp.zeros((8, LANES), f32)
    count, squares, traces = lax.fori_loop(0, NBLK // CHUNK, step, (jnp.int32(0), blank, blank))
    list_ref[0, 0] = count
    for u in range(4):
        list_ref[0, 1 + count + u] = 0
    stats_ref[:8] = squares
    stats_ref[8:] = traces


def first_kernel(
    col_ref, list_ref, send_ref, edge_ref, count_ref,
    blocks, op_own_ref, base_ref, low_ref, high_ref,
    ops_ref, zero_ref, a1_ref, b1_ref, a2_ref, k0_ref, k1_ref, up_ref, down_ref,
    y_ref, column_ref, square_ref, g_ref, gram_ref,
):
    count = a1_ref.shape[0]
    ops_ref[OFF:HIGH] = op_own_ref[...]
    zero_ref[...] = base_ref[...]
    for part, first in ((low_ref, LOW), (high_ref, HIGH)):
        for j in range(IF):
            weights = unflatten(lambda q: part[j, pl.ds(q, 8, stride=3), :])
            ops_ref[first + j] = make_operator(weights, gram_ref.at[j & 1])
            for r in range(2 * count):
                zero_ref[r, first + j : first + j + 1, :] = part[j, CUTS + r : CUTS + r + 1, :]
    column_ref[...] = jnp.zeros_like(column_ref)
    row = lax.broadcasted_iota(jnp.int32, (ROWS, LANES), 0)
    dead = (row >= count_ref[0] + OFF) & (row < HIGH)
    for r in range(count):
        zero_ref[r] = jnp.where(dead, 0.0, zero_ref[r])
    scatter_apply(blocks, ops_ref, zero_ref, y_ref, col_ref, column_ref)
    ghost_images(ops_ref, zero_ref, g_ref)
    ghost_apply(blocks, g_ref, y_ref, col_ref, list_ref)
    inner = inner_rows()
    for r in range(count):
        k0_ref[r] = unpack_columns(column_ref, square_ref, r)
        a1_ref[r] = jnp.where(inner, pack(y_ref, r), 0.0)
        b1_ref[r] = jnp.where(inner, pack(y_ref, count + r), 0.0)
    half = y_ref.at[pl.ds(0, count)]
    scatter_apply(blocks, ops_ref, a1_ref, half, col_ref, column_ref)
    for r in range(count):
        k1_ref[r] = unpack_columns(column_ref, square_ref, r)
        a2_ref[r] = pack(y_ref, r)
    messages(up_ref, down_ref, a2_ref, send_ref, a1_ref)


def second_kernel(
    col_ref, list_ref, send_ref, edge_ref,
    blocks, ops_ref, zero_ref, a1_ref, a2_in, k0_ref, k1_ref, low_ref, high_ref, stats_ref,
    v1_ref, v2_ref, v3_ref, v4_ref, k3_ref, dots_ref, sigma_ref, up_ref, down_ref,
    y_ref, column_ref, square_ref, g_ref,
):
    count = a1_ref.shape[0]
    inner = inner_rows()
    squares, traces = stats_ref[0, :8], stats_ref[0, 8:]
    for s in range(1, stats_ref.shape[0]):
        squares = squares + stats_ref[s, :8]
        traces = traces + stats_ref[s, 8:]
    scale = 1.0 / (stats_ref.shape[0] * NBLK * BS)
    sigma = (1.0 + scale * whole_sum(squares)) * (scale * whole_sum(traces))
    sigma_ref[...] = jnp.broadcast_to(sigma, sigma_ref.shape)
    column_ref[...] = jnp.zeros_like(column_ref)
    v2_ref[...] = a2_in[...]
    complete(v2_ref, low_ref, high_ref, send_ref, edge_ref)
    for r in range(count):
        v1_ref[r] = a1_ref[r]
        for part, ghost, flag in ((low_ref, LOW, 0), (high_ref, HIGH, 1)):
            for j in range(IF):
                v1_ref[r, ghost + j : ghost + j + 1, :] = part[r, 16 + j : 17 + j, :]
        v1 = v1_ref[r] - sigma * zero_ref[r]
        v2_ref[r] = v2_ref[r] - sigma * v1_ref[r] - sigma * v1
        v1 = jnp.where(inner, v1, 0.0)
        v1_ref[r] = v1
        v0 = jnp.where(inner, zero_ref[r], 0.0)
        target = jnp.where(inner, zero_ref[count + r], 0.0)
        second = k1_ref[r] - sigma * k0_ref[r]
        dots_ref[r, 0] = tile_sum(v0, k0_ref[r])
        dots_ref[r, 1] = tile_sum(v1, k0_ref[r])
        dots_ref[r, 2] = tile_sum(v1, second)
        dots_ref[r, 8] = tile_sum(target, k0_ref[r])
        dots_ref[r, 9] = tile_sum(target, second)
    scatter_apply(blocks, ops_ref, v2_ref, y_ref, col_ref, column_ref)
    ghost_images(ops_ref, v2_ref, g_ref)
    ghost_apply(blocks, g_ref, y_ref, col_ref, list_ref)
    for r in range(count):
        image = unpack_columns(column_ref, square_ref, r)
        v3 = jnp.where(inner, pack(y_ref, r) - sigma * v2_ref[r], 0.0)
        v3_ref[r] = v3
        dots_ref[r, 3] = tile_sum(v1_ref[r], image)
        dots_ref[r, 4] = tile_sum(jnp.where(inner, v2_ref[r], 0.0), image)
        dots_ref[r, 5] = tile_sum(v3, image)
        dots_ref[r, 10] = tile_sum(jnp.where(inner, zero_ref[count + r], 0.0), image)
    scatter_apply(blocks, ops_ref, v3_ref, y_ref, col_ref, column_ref)
    for r in range(count):
        image = unpack_columns(column_ref, square_ref, r)
        dots_ref[r, 6] = tile_sum(v3_ref[r], image)
        dots_ref[r, 7] = jnp.zeros((8, LANES), f32)
        dots_ref[r, 11] = tile_sum(jnp.where(inner, zero_ref[count + r], 0.0), image)
        k3_ref[r] = image
        v4_ref[r] = pack(y_ref, r) - sigma * v3_ref[r]
    messages(up_ref, down_ref, v4_ref, send_ref)


def moment_kernel(send_ref, edge_ref, v4_in, k3_ref, low_ref, high_ref, dots_in, v4_ref, dots_ref):
    v4_ref[...] = v4_in[...]
    complete(v4_ref, low_ref, high_ref, send_ref, edge_ref)
    lane = lax.broadcasted_iota(jnp.int32, (8, LANES), 1)
    sub = lax.broadcasted_iota(jnp.int32, (8, LANES), 0)
    total = jnp.zeros((8, LANES), f32)
    for r in range(v4_ref.shape[0]):
        for d in range(12):
            part = tile_sum(v4_ref[r], k3_ref[r]) if d == 7 else dots_in[r, d]
            total = jnp.where((lane == d) & (sub == r), whole_sum(part), total)
    dots_ref[...] = total


def third_kernel(col_ref, list_ref, blocks, ops_ref, v4_ref, w5_ref, y_ref, g_ref):
    scatter_apply(blocks, ops_ref, v4_ref, y_ref, col_ref, None)
    ghost_images(ops_ref, v4_ref, g_ref)
    ghost_apply(blocks, g_ref, y_ref, col_ref, list_ref)
    for r in range(v4_ref.shape[0]):
        w5_ref[r] = pack(y_ref, r)


def fourth_kernel(*refs):
    col_ref, send_ref, blocks, ops_ref, zero_ref, v1_ref, v2_ref, v3_ref, v4_ref, w5_ref, b1_ref, sigma_ref = refs[:12]
    parts_refs = refs[12:-9]
    comb_ref, rho_ref, early_ref, scale_ref, up_ref, down_ref, y_ref, x_ref, coef_ref = refs[-9:]
    sums = [part[...] for part in parts_refs]
    while len(sums) > 1:
        sums = [sums[i] + sums[i + 1] for i in range(0, len(sums), 2)]
    sums = sums[0]
    column = lambda d: jnp.broadcast_to(sums[:, d : d + 1], (8, LANES))
    combos, scales = scalars([column(d) for d in range(8)], [column(8 + d) for d in range(4)], sigma_ref[...])
    for g, value in enumerate(scales):
        scale_ref[g] = value
    count = v1_ref.shape[0]
    inner = inner_rows()
    for g, combo in enumerate(combos):
        for s, value in enumerate(combo):
            if value is not None:
                coef_ref[g, s] = value
    for r in range(count):
        parts = [zero_ref[r], v1_ref[r], v2_ref[r], v3_ref[r], v4_ref[r], w5_ref[r], zero_ref[count + r], b1_ref[r]]
        parts = [jnp.where(inner, part, 0.0) for part in parts]
        for g, combo in enumerate(combos):
            total = None
            for s, value in enumerate(combo):
                if value is not None:
                    term = coef_ref[g, s, r : r + 1, :] * parts[s]
                    total = term if total is None else total + term
            if g == 5:
                x_ref[r] = total
            slot = {0: 2, 1: 4, 2: 6, 3: 14, 4: 12}.get(g)
            if slot is None:
                comb_ref[g - 5, r] = total
            else:
                early_ref[pl.ds(slot + r, NBLK, stride=EARLY), :] = total[OFF:HIGH]
        early_ref[pl.ds(r, NBLK, stride=EARLY), :] = parts[0][OFF:HIGH]
        for slot in (8, 10):
            early_ref[pl.ds(slot + r, NBLK, stride=EARLY), :] = jnp.zeros((NBLK, LANES), f32)
    scatter_apply(blocks, ops_ref, x_ref, y_ref, col_ref, None)
    for r in range(count):
        rho_ref[r] = comb_ref[2, r] - scale_ref[0, r : r + 1, :] * pack(y_ref, r)
    messages(up_ref, down_ref, rho_ref, send_ref)


def answer_kernel(ops_ref, comb_ref, sol_ref, column_ref, square_ref):
    column_ref[...] = jnp.zeros_like(column_ref)
    lanes = lane_ids()
    for r in range(sol_ref.shape[0]):
        for n in range(NBLK):
            image = jnp.sum(ops_ref[n + OFF] * comb_ref[4, r, n + OFF : n + OFF + 1, :], axis=1, keepdims=True)
            column_ref[r] = jnp.where(lanes == n, image, column_ref[r])
        sol_ref[r] = unpack_columns(column_ref, square_ref, r)[:NBLK]


def fifth_kernel(
    col_ref, list_ref, send_ref, edge_ref,
    blocks, ops_ref, rho_in, comb_ref, scale_ref, low_ref, high_ref,
    late_ref, y_ref, rho_ref, g_ref,
):
    count = rho_in.shape[0]
    rho_ref[...] = rho_in[...]
    complete(rho_ref, low_ref, high_ref, send_ref, edge_ref)
    scatter_apply(blocks, ops_ref, rho_ref, y_ref, col_ref, None)
    ghost_images(ops_ref, rho_ref, g_ref)
    ghost_apply(blocks, g_ref, y_ref, col_ref, list_ref)
    for r in range(count):
        change = rho_ref[r] - comb_ref[2, r]
        first = comb_ref[3, r] + scale_ref[1, r : r + 1, :] * change - scale_ref[2, r : r + 1, :] * pack(y_ref, r)
        second = comb_ref[1, r] + change
        late_ref[pl.ds(r, NBLK, stride=LATE), :] = first[OFF:HIGH]
        late_ref[pl.ds(2 + r, NBLK, stride=LATE), :] = second[OFF:HIGH]


def split(value):
    high = value.astype(jnp.bfloat16)
    return high, (value - high.astype(f32)).astype(jnp.bfloat16)


def product(first, second, dim):
    (fh, fl), (sh, sl) = split(first), split(second)
    left = jnp.concatenate([fh, fl, fh], axis=dim)
    right = jnp.concatenate([sh, sh, sl], axis=0)
    return lax.dot_general(left, right, (((dim,), (0,)), ((), ())), preferred_element_type=f32)


def grad_kernel(*refs):
    peers = (len(refs) - 2) // 2
    early, late, weights_ref, grad_ref = refs[:peers], refs[peers : 2 * peers], refs[-2], refs[-1]
    sub = lax.broadcasted_iota(jnp.int32, (8, LANES), 0)

    def step(group, carry):
        for i in range(CHUNK):
            n = group * CHUNK + i
            at = pl.multiple_of(n * EARLY, EARLY)
            resid = [ref[pl.ds(at, 8), :] for ref in early]
            zeta = []
            for first, last in zip(early, late):
                pair = last[pl.ds(pl.multiple_of(group * (CHUNK * LATE) + 8 * (i // 2), 8), 8), :]
                if i % 2:
                    pair = pltpu.roll(pair, 4, 0)
                zeta.append(jnp.where(sub < LATE, pair, first[pl.ds(at + 8, 8), :]))
            mixed = product(jnp.concatenate(resid + zeta, axis=0), jnp.concatenate(zeta + resid, axis=0), 0)
            grad = product(weights_ref[n], mixed, 1)

            def write(q, value):
                grad_ref[pl.ds(group * (8 * CUTS) + 8 * q + i, 8, stride=24), :] = value

            flatten(grad, write)
        return carry

    lax.fori_loop(0, NBLK // CHUNK, step, 0)


def parts_over(values, axis):
    size = lax.axis_size(axis)
    if size & (size - 1):
        return [lax.psum(values, axis)]
    step = 1
    parts = [values]
    while step < size:
        if step > 1:
            while len(parts) > 1:
                parts = [parts[i] + parts[i + 1] for i in range(0, len(parts), 2)]
            values = parts[0]
        width = min(8, size // step)
        parts = [values]
        for d in range(1, width):
            parts.append(lax.ppermute(values, axis, [(i, i ^ (d * step)) for i in range(size)]))
        step *= width
    return parts


def all_of(values, axis):
    size = lax.axis_size(axis)
    return [values] + [
        lax.ppermute(values, axis, [(i, (i + d) % size) for i in range(size)]) for d in range(1, size)
    ]


def exchange(up, down):
    size = lax.axis_size("sub")
    rising = [(i, i + 1) for i in range(size - 1)]
    falling = [(j, i) for i, j in rising]
    return lax.ppermute(up, "sub", rising), lax.ppermute(down, "sub", falling)


def plus(first, second):
    if first is None:
        return second
    return first if second is None else first + second


def times(first, second):
    return None if first is None or second is None else first * second


def add(first, second, scale):
    size = max(len(first), len(second))
    first = list(first) + [None] * (size - len(first))
    second = list(second) + [None] * (size - len(second))
    return [plus(a, times(scale, b)) for a, b in zip(first, second)]


def scaled(first, scale):
    return [times(scale, a) for a in first]


def scalars(moments, products, sigma):
    one = jnp.ones_like(sigma)

    def inner(first, second):
        weights = [None] * (len(first) + len(second) - 1)
        for i, a in enumerate(first):
            for j, b in enumerate(second):
                weights[i + j] = plus(weights[i + j], a * b)
        total = None
        for weight, moment in zip(weights, moments):
            total = plus(total, weight * moment)
        return total

    def apply(poly):
        out = [None] * (len(poly) + 1)
        for j, value in enumerate(poly):
            out[j] = plus(out[j], sigma * value)
            out[j + 1] = plus(out[j + 1], value)
        return out

    resid = [[one]]
    direc = [[one]]
    image = []
    step, ratio, norm, curv = [], [None], [moments[0]], []
    for i in range(ITERS):
        image.append(apply(direc[i]))
        curv.append(inner(direc[i], image[i]))
        step.append(norm[i] / curv[i])
        if i + 1 < ITERS:
            resid.append(add(resid[i], image[i], -step[i]))
            norm.append(inner(resid[i + 1], resid[i + 1]))
            ratio.append(norm[i + 1] / norm[i])
            direc.append(add(resid[i + 1], direc[i], ratio[i + 1]))
    cot = []
    for i in range(ITERS):
        total = None
        for j, value in enumerate(resid[i]):
            total = plus(total, value * products[j])
        cot.append(total)
    along = [cot[0]]
    for i in range(1, ITERS):
        along.append(cot[i] + ratio[i] * along[i - 1])

    def row(poly):
        return list(poly) + [None] * (8 - len(poly))

    target = [None] * 6 + [one, None]
    resid_rows = [row(poly) for poly in resid]
    image_rows = [row(poly) for poly in image]
    inverse = [1.0 / value for value in step]

    def resid_prod(i):
        return [norm[l] if l == i else None for l in range(ITERS)]

    def image_prod(i):
        out = [None] * ITERS
        out[i] = norm[i] * inverse[i]
        if i + 1 < ITERS:
            out[i + 1] = -norm[i + 1] * inverse[i]
        return out

    def along_dir(prod, i):
        total = prod[0]
        for l in range(1, i + 1):
            total = plus(prod[l], times(ratio[l], total))
        return total

    def operator_prod(prod):
        out = []
        for l in range(ITERS - 1):
            value = times(add([prod[l]], [prod[l + 1]], -one)[0], inverse[l])
            if l > 0:
                back = times(add([prod[l - 1]], [prod[l]], -one)[0], inverse[l - 1])
                value = add([value], [back], -ratio[l])[0]
            out.append(value)
        return out + [None]

    last = ITERS - 1
    step_bar = along[last]
    curv_bar = -step_bar * step[last] / curv[last]
    dir_row = add(scaled(target, step[last]), image_rows[last], 2 * curv_bar)
    dir_prod = add(scaled(cot, step[last]), image_prod(last), 2 * curv_bar)
    norm_bar = step_bar / curv[last]
    rho_row = [None] * 8
    rho_prod = [None] * ITERS
    zetas = [None] * ITERS
    rho_rows = []
    for i in (2, 1, 0):
        ratio_bar = along_dir(dir_prod, i)
        full = norm_bar + ratio_bar / norm[i]
        zetas[i + 1] = add(dir_row, resid_rows[i + 1], full)
        rho_row = add(add(rho_row, zetas[i + 1], one), resid_rows[i + 1], full)
        rho_prod = add(add(rho_prod, dir_prod, one), resid_prod(i + 1), 2 * full)
        rho_rows.append(rho_row)
        step_bar = along[i] - (rho_prod[i] - rho_prod[i + 1]) * inverse[i]
        curv_bar = -step_bar * step[i] / curv[i]
        oper = [None] * 8
        if i == 2:
            for k in range(5):
                if k < 4:
                    oper[k] = plus(oper[k], times(sigma, rho_row[k]))
                    oper[k + 1] = plus(oper[k + 1], rho_row[k])
                else:
                    oper[5] = plus(oper[5], rho_row[4])
            oper[7] = rho_row[6]
        kept = add(scaled(dir_row, ratio[i + 1]), target, step[i])
        kept = add(kept, image_rows[i], 2 * curv_bar)
        dir_row = add(kept, oper, -step[i])
        dir_prod = add(add(scaled(dir_prod, ratio[i + 1]), cot, step[i]), image_prod(i), 2 * curv_bar)
        dir_prod = add(dir_prod, operator_prod(rho_prod), -step[i])
        norm_bar = step_bar / curv[i] - ratio_bar * norm[i + 1] / (norm[i] * norm[i])
    zetas[0] = add(dir_row, resid_rows[0], norm_bar)
    answer = [None] * 8
    for i in range(ITERS):
        answer = add(answer, row(direc[i]), step[i])
    combos = [resid_rows[1], resid_rows[2], resid_rows[3], zetas[3], zetas[2], rho_rows[1], zetas[1], rho_rows[2], zetas[0], answer]
    return combos, [step[1], ratio[1], step[0]]


def vmem():
    return pl.BlockSpec(memory_space=pltpu.VMEM)


def smem():
    return pl.BlockSpec(memory_space=pltpu.SMEM)


def shards(stiffness, precond, rhs_vec, cotangent, col_index, send_rows, counts):
    count = rhs_vec.shape[0]
    sub = lax.axis_index("sub")
    size = lax.axis_size("sub")
    edge = jnp.stack([sub > 0, sub + 1 < size]).astype(jnp.int32)
    columns = col_index.T
    stiff_cuts = stiffness.reshape(NBLK, K, CUTS, LANES).transpose(0, 2, 1, 3).reshape(NBLK * K * CUTS, LANES)
    weight_cuts = precond.reshape(NBLK // 8, 8, CUTS, LANES).transpose(0, 2, 1, 3).reshape(NBLK * CUTS, LANES)
    base = jnp.concatenate([rhs_vec, cotangent], axis=0).reshape(2 * count, NBLK, BS)
    base = jnp.pad(base, ((0, 0), (OFF, ROWS - HIGH), (0, LANES - BS)))

    def shape(*dims):
        return jax.ShapeDtypeStruct(dims, f32)

    def call(kernel, name, scalars_in, arrays_in, outs, scratch, flops, specs=None):
        return pl.pallas_call(
            kernel,
            in_specs=[smem()] * len(scalars_in) + [vmem()] * len(arrays_in),
            out_specs=specs or [vmem()] * len(outs),
            out_shape=outs,
            scratch_shapes=scratch,
            compiler_params=pltpu.CompilerParams(vmem_limit_bytes=8 * MIB),
            cost_estimate=pl.CostEstimate(flops=flops, bytes_accessed=flops // 2, transcendentals=0),
            name=name,
        )(*scalars_in, *arrays_in)

    rows = shape(count, ROWS, LANES)
    message = shape(count, 16, LANES)
    longer = shape(count, 24, LANES)
    ghost_message = shape(IF, CUTS + 8, LANES)
    partial = lambda r: pltpu.VMEM((r, ROWS, 8, LANES), f32)
    turned = [pltpu.VMEM((count, BS, LANES), f32), pltpu.VMEM((LANES, LANES), f32)]
    held = lambda r: pltpu.VMEM((r, ROWS, LANES), f32)
    grams = pltpu.VMEM((2, BS, LANES), f32)
    work = 4 * MIB

    up, down = call(pack_kernel, "pack", [send_rows], [weight_cuts, base], [ghost_message] * 2, [], MIB)
    low, high = exchange(up, down)

    blocks, weights, op_own, halo_list, stats = call(
        prepare_kernel, "prepare", [columns], [stiff_cuts, weight_cuts],
        [
            shape(NBLK, K, BS, LANES), shape(NBLK, BS, LANES), shape(NBLK, BS, LANES),
            jax.ShapeDtypeStruct((1, NBLK * K + 8), jnp.int32), shape(16, LANES),
        ],
        [grams], 2 * work, [vmem(), vmem(), vmem(), smem(), vmem()],
    )
    stats = lax.all_gather(stats, "sub")

    ops, zero, a1, b1, a2, k0, k1, up, down = call(
        first_kernel, "first", [columns, halo_list, send_rows, edge, counts], [blocks, op_own, base, low, high],
        [shape(ROWS, BS, LANES), shape(2 * count, ROWS, LANES), rows, rows, rows, rows, rows, longer, longer],
        [partial(2 * count), *turned, held(2 * count), grams], 2 * work,
    )
    low, high = exchange(up, down)

    v1, v2, v3, v4, k3, dots, sigma, up, down = call(
        second_kernel, "second", [columns, halo_list, send_rows, edge],
        [blocks, ops, zero, a1, a2, k0, k1, low, high, stats],
        [rows, rows, rows, rows, rows, shape(count, 12, 8, LANES), shape(8, LANES), message, message],
        [partial(count), *turned, held(count)], 2 * work,
    )
    low, high = exchange(up, down)

    v4, dots = call(
        moment_kernel, "moments", [send_rows, edge], [v4, k3, low, high, dots], [rows, shape(8, LANES)], [], MIB
    )
    parts = parts_over(dots, "sub")

    (w5,) = call(
        third_kernel, "third", [columns, halo_list], [blocks, ops, v4], [rows], [partial(count), held(count)], work
    )

    comb, rho, early, scales, up, down = call(
        fourth_kernel, "fourth", [columns, send_rows],
        [blocks, ops, zero, v1, v2, v3, v4, w5, b1, sigma, *parts],
        [shape(5, count, ROWS, LANES), rows, shape(NBLK * EARLY, LANES), shape(3, 8, LANES), message, message],
        [partial(count), held(count), pltpu.VMEM((10, 8, 8, LANES), f32)], work,
    )
    low, high = exchange(up, down)
    early = all_of(early, "rhs")

    (answer,) = call(answer_kernel, "answer", [], [ops, comb], [shape(count, NBLK, LANES)], turned, MIB)

    (late,) = call(
        fifth_kernel, "fifth", [columns, halo_list, send_rows, edge], [blocks, ops, rho, comb, scales, low, high],
        [shape(NBLK * LATE, LANES)], [partial(count), held(count), held(count)], work,
    )
    late = all_of(late, "rhs")

    (grad,) = call(grad_kernel, "grad", [], [*early, *late, weights], [shape(NBLK * CUTS, LANES)], [], work)
    grad = grad.reshape(NBLK // 8, CUTS, 8, LANES).transpose(0, 2, 1, 3).reshape(NBLK, BS * BS)
    return answer[..., :BS].reshape(count, NBLK * BS), grad


def solution(mesh):
    in_specs = (
        P("sub", None, None),
        P("sub", None),
        P("rhs", "sub"),
        P("rhs", "sub"),
        P("sub", None),
        P("sub", None),
        P("sub"),
    )
    out_specs = (P("rhs", "sub"), P("sub", None))
    return jax.shard_map(shards, mesh=mesh, in_specs=in_specs, out_specs=out_specs, check_vma=False)
```

```python
import functools

import jax
import jax.numpy as jnp
from jax import lax
from jax.experimental import pallas as pl
from jax.experimental.pallas import tpu as pltpu
from jax.sharding import PartitionSpec as P

BS = 96
K = 4
NBLK = 48
IF = 6
ITERS = 4
ALL = (0, 1, 2, 3, 4, 5, 6, 7)
USED = ((0, 1), (0, 1, 2), (0, 1, 2, 3), (0, 1, 2, 3, 4, 6), ALL, ALL, ALL, ALL, ALL, (0, 1, 2, 3))
EARLY = 16
LATE = 4
CUTS = BS * BS // 128
LANES = 128
OFF = 8
ROWS = 64
LOW = OFF - IF
HIGH = OFF + NBLK
CHUNK = 8
MIB = 1024 * 1024

highest = lax.Precision.HIGHEST
f32 = jnp.float32


def own(value):
    return value[:, OFF:HIGH]


def lane_ids():
    return lax.broadcasted_iota(jnp.int32, (BS, LANES), 1)


def diagonal():
    pos = lax.broadcasted_iota(jnp.int32, (BS, LANES), 0)
    row = (pos & ~31) + 4 * (pos & 7) + ((pos >> 3) & 3)
    return row == lane_ids()


def fold(prod):
    return jnp.sum(prod.reshape(BS // 8, 8, prod.shape[-1]), axis=0)


def unflatten(read):
    lane = lax.broadcasted_iota(jnp.int32, (8, LANES), 1)
    out = []
    for h in range(BS // 32):
        one, two, three = (read(24 * h + m) for m in range(3))
        out.append(jnp.where(lane < BS, one, 0.0))
        mixed = jnp.where(lane < 32, pltpu.roll(one, 32, 1), pltpu.roll(two, 32, 1))
        out.append(jnp.where(lane < BS, mixed, 0.0))
        mixed = jnp.where(lane < 64, pltpu.roll(two, 64, 1), pltpu.roll(three, 64, 1))
        out.append(jnp.where(lane < BS, mixed, 0.0))
        out.append(jnp.where(lane < BS, pltpu.roll(three, 96, 1), 0.0))
    return jnp.concatenate(out, axis=0)


def flatten(block, write):
    lane = lax.broadcasted_iota(jnp.int32, (8, LANES), 1)
    for h in range(BS // 32):
        one, two, three, four = (block[32 * h + 8 * j : 32 * h + 8 * j + 8] for j in range(4))
        two = pltpu.roll(two, 96, 1)
        three = pltpu.roll(three, 64, 1)
        write(24 * h, jnp.where(lane < BS, one, two))
        write(24 * h + 1, jnp.where(lane < 64, two, three))
        write(24 * h + 2, jnp.where(lane < 32, three, pltpu.roll(four, 32, 1)))


def make_operator(weights, gram_ref):
    gram = lax.dot_general(
        weights, weights, (((0,), (0,)), ((), ())), precision=highest, preferred_element_type=f32
    )
    gram_ref[...] = gram[:BS]
    rows = [gram_ref[pl.ds(32 * h + j, 8, stride=4), :] for h in range(BS // 32) for j in range(4)]
    return jnp.concatenate(rows, axis=0) + jnp.where(diagonal(), 1.0, 0.0)


def scatter_apply(blocks, op_ref, x_ref, y_ref, col_ref, column_ref):
    count = x_ref.shape[0]
    y_ref[...] = jnp.zeros_like(y_ref)

    def step(group, carry):
        base = pl.multiple_of(group * CHUNK, CHUNK)
        tiles = [x_ref[r, pl.ds(base + OFF, CHUNK), :] for r in range(count)]
        for i in range(CHUNK):
            n = group * CHUNK + i
            oper = op_ref[n]
            images = [jnp.sum(oper * tiles[r][i : i + 1, :], axis=1, keepdims=True) for r in range(count)]
            if column_ref is not None:
                for r in range(count):
                    column_ref[r] = jnp.where(lane_ids() == n + OFF, images[r], column_ref[r])
            for k in range(K):
                block = blocks[n, k]
                slot = col_ref[k, n] + LOW
                for r in range(count):
                    y_ref[r, slot] = y_ref[r, slot] + fold(block * images[r])
        return carry

    lax.fori_loop(0, NBLK // CHUNK, step, 0)


def ghost_images(op_ref, x_ref, g_ref):
    count = x_ref.shape[0]
    mask = diagonal()
    g_ref[...] = jnp.zeros_like(g_ref)
    for first, side in ((LOW, 0), (HIGH, IF)):
        for j in range(IF):
            slot = first + j
            oper = op_ref[side + j]
            for r in range(count):
                image = jnp.sum(oper * x_ref[r, slot : slot + 1, :], axis=1, keepdims=True)
                line = jnp.sum(fold(jnp.where(mask, image, 0.0)), axis=0, keepdims=True)
                g_ref[r, slot : slot + 1, :] = line


def ghost_apply(blocks, g_ref, y_ref, col_ref, list_ref):
    count = g_ref.shape[0]
    mask = diagonal()

    def step(item, carry):
        for u in range(4):
            entry = list_ref[0, 1 + item * 4 + u]
            n = entry >> 2
            k = entry & 3
            slot = col_ref[k, n] + LOW
            block = blocks[n, k]
            for r in range(count):
                image = jnp.sum(block * g_ref[r, pl.ds(slot, 1), :], axis=1, keepdims=True)
                y_ref[r, n + OFF] = y_ref[r, n + OFF] + fold(jnp.where(mask, image, 0.0))
        return carry

    lax.fori_loop(0, (list_ref[0, 0] + 3) >> 2, step, 0)


def pack(y_ref, r):
    sub = lax.broadcasted_iota(jnp.int32, (8, LANES), 0)
    groups = []
    for g in range(ROWS // 8):
        total = jnp.zeros((8, LANES), f32)
        for i in range(8):
            line = jnp.sum(y_ref[r, g * 8 + i], axis=0, keepdims=True)
            total = jnp.where(sub == i, line, total)
        groups.append(total)
    return jnp.concatenate(groups, axis=0)


def unpack_columns(column_ref, square_ref, r):
    for h in range(BS // 32):
        for j in range(4):
            start = 32 * h + 8 * j
            square_ref[pl.ds(32 * h + j, 8, stride=4), :] = column_ref[r, start : start + 8, :]
    square_ref[BS:, :] = jnp.zeros((LANES - BS, LANES), f32)
    return square_ref[...].T[:ROWS]


def messages(up_ref, down_ref, v_ref, send_ref, extra_ref=None):
    for r in range(v_ref.shape[0]):
        for j in range(IF):
            low = pl.ds(send_ref[0, j] + OFF, 1)
            high = pl.ds(send_ref[0, IF + j] + OFF, 1)
            down_ref[r, j : j + 1, :] = v_ref[r, low, :]
            up_ref[r, j : j + 1, :] = v_ref[r, high, :]
            down_ref[r, 8 + j : 9 + j, :] = v_ref[r, LOW + j : LOW + j + 1, :]
            up_ref[r, 8 + j : 9 + j, :] = v_ref[r, HIGH + j : HIGH + j + 1, :]
            if extra_ref is not None:
                down_ref[r, 16 + j : 17 + j, :] = extra_ref[r, low, :]
                up_ref[r, 16 + j : 17 + j, :] = extra_ref[r, high, :]


def complete(v_ref, low_ref, high_ref, send_ref, edge_ref):
    for r in range(v_ref.shape[0]):
        for j in range(IF):
            for part, base, ghost, flag in ((low_ref, 0, LOW, 0), (high_ref, IF, HIGH, 1)):
                at = pl.ds(send_ref[0, base + j] + OFF, 1)
                v_ref[r, at, :] = v_ref[r, at, :] + part[r, 8 + j : 9 + j, :]
                slot = ghost + j
                summed = v_ref[r, slot : slot + 1, :] + part[r, j : j + 1, :]
                v_ref[r, slot : slot + 1, :] = jnp.where(edge_ref[flag] > 0, summed, 0.0)


def tile_sum(first, second):
    prod = first * second
    return jnp.sum(prod.reshape(prod.shape[0] // 8, 8, LANES), axis=0)


def whole_sum(tile):
    return jnp.sum(jnp.sum(tile, axis=0, keepdims=True), axis=1, keepdims=True)


def inner_rows():
    row = lax.broadcasted_iota(jnp.int32, (ROWS, LANES), 0)
    return (row >= OFF) & (row < HIGH)


def pack_kernel(send_ref, raw_ref, base_ref, up_ref, down_ref):
    vectors = base_ref.shape[0]
    for part, ref in ((0, down_ref), (IF, up_ref)):
        for j in range(IF):
            n = send_ref[0, part + j]
            start = (n >> 3) * (8 * CUTS) + (n & 7)
            for i in range(CUTS // 8):
                ref[j, 8 * i : 8 * i + 8, :] = raw_ref[pl.ds(start + 64 * i, 8, stride=8), :]
            ref[j, CUTS:, :] = jnp.zeros((8, LANES), f32)
            weights = unflatten(lambda q: raw_ref[pl.ds(start + 8 * q, 8, stride=24), :])
            for r in range(vectors):
                line = base_ref[r, pl.ds(n + OFF, 1), :]
                if r < vectors // 2:
                    ref[j, CUTS + r : CUTS + r + 1, :] = line
                inside = jnp.sum(weights * line, axis=1, keepdims=True)
                image = line + jnp.sum(fold(weights * inside), axis=0, keepdims=True)
                at = CUTS + vectors // 2 + r
                ref[j, at : at + 1, :] = image


def prepare_kernel(
    col_ref, raw_ref, stiff_hbm, blocks_ref, weights_ref, ops_ref, list_ref, stats_ref, gram_ref, stiff_ref, sems
):
    mask = diagonal()
    part = CHUNK * CUTS * K

    def fetch(group):
        at = pl.ds(group * part, part)
        return pltpu.make_async_copy(stiff_hbm.at[at], stiff_ref.at[at], sems.at[group])

    for g in range(NBLK // CHUNK):
        fetch(g).start()

    def step(group, carry):
        count, squares, traces = carry
        fetch(group).wait()
        for i in range(CHUNK):
            n = group * CHUNK + i
            for k in range(K):
                block = unflatten(lambda q: stiff_ref[pl.ds(n * (CUTS * K) + 4 * q + k, 8, stride=12), :])
                blocks_ref[n, k] = block
                if k == 0:
                    traces = traces + fold(jnp.where(mask, block, 0.0))
                col = col_ref[k, n]
                list_ref[0, 1 + count] = n * K + k
                count = count + jnp.where((col < IF) | (col >= IF + NBLK), 1, 0)
            weights = unflatten(lambda q: raw_ref[pl.ds(group * (8 * CUTS) + 8 * q + i, 8, stride=24), :])
            weights_ref[n] = weights
            squares = squares + fold(weights * weights)
            ops_ref[n] = make_operator(weights, gram_ref.at[i & 1])
        return count, squares, traces

    blank = jnp.zeros((8, LANES), f32)
    count, squares, traces = lax.fori_loop(0, NBLK // CHUNK, step, (jnp.int32(0), blank, blank))
    list_ref[0, 0] = count
    for u in range(4):
        list_ref[0, 1 + count + u] = 0
    stats_ref[:8] = squares
    stats_ref[8:] = traces


def first_kernel(
    col_ref, list_ref, send_ref, count_ref,
    blocks, op_ref, base_ref, low_ref, high_ref,
    zero_ref, a1_ref, a2_ref, up_ref, down_ref,
    y_ref, g_ref,
):
    count = a1_ref.shape[0]
    zero_ref[...] = base_ref[...]
    g_ref[...] = jnp.zeros_like(g_ref)
    row = lax.broadcasted_iota(jnp.int32, (ROWS, LANES), 0)
    dead = (row >= count_ref[0] + OFF) & (row < HIGH)
    for r in range(count):
        zero_ref[r] = jnp.where(dead, 0.0, zero_ref[r])
        for part, first in ((low_ref, LOW), (high_ref, HIGH)):
            for j in range(IF):
                at = slice(first + j, first + j + 1)
                zero_ref[r, at, :] = part[j, CUTS + r : CUTS + r + 1, :]
                g_ref[r, at, :] = part[j, CUTS + count + r : CUTS + count + r + 1, :]
    scatter_apply(blocks, op_ref, zero_ref.at[pl.ds(0, count)], y_ref, col_ref, None)
    ghost_apply(blocks, g_ref, y_ref, col_ref, list_ref)
    inner = inner_rows()
    for r in range(count):
        a1_ref[r] = jnp.where(inner, pack(y_ref, r), 0.0)
    scatter_apply(blocks, op_ref, a1_ref, y_ref, col_ref, None)
    for r in range(count):
        a2_ref[r] = pack(y_ref, r)
    messages(up_ref, down_ref, a2_ref, send_ref, a1_ref)


def operator_rows(op_ref, x_ref, out_ref, column_ref, square_ref):
    column_ref[...] = jnp.zeros_like(column_ref)
    lanes = lane_ids()
    for r in range(column_ref.shape[0]):
        for n in range(NBLK):
            image = jnp.sum(op_ref[n] * x_ref[r, n + OFF : n + OFF + 1, :], axis=1, keepdims=True)
            column_ref[r] = jnp.where(lanes == n + OFF, image, column_ref[r])
        out_ref[r] = unpack_columns(column_ref, square_ref, r)


def ghost_kernel(op_ref, zero_ref, a1_ref, low_ref, high_ref, gop_ref, k0_ref, k1_ref, gram_ref, column_ref, square_ref):
    for part, first in ((low_ref, 0), (high_ref, IF)):
        for j in range(IF):
            weights = unflatten(lambda q: part[j, pl.ds(q, 8, stride=3), :])
            gop_ref[first + j] = make_operator(weights, gram_ref.at[j & 1])
    operator_rows(op_ref, zero_ref, k0_ref, column_ref, square_ref)
    operator_rows(op_ref, a1_ref, k1_ref, column_ref, square_ref)


def target_kernel(col_ref, list_ref, blocks, op_ref, zero_ref, low_ref, high_ref, b1_ref, y_ref, g_ref):
    count = b1_ref.shape[0]
    g_ref[...] = jnp.zeros_like(g_ref)
    for r in range(count):
        for part, first in ((low_ref, LOW), (high_ref, HIGH)):
            for j in range(IF):
                g_ref[r, first + j : first + j + 1, :] = part[j, CUTS + 2 * count + r : CUTS + 2 * count + r + 1, :]
    scatter_apply(blocks, op_ref, zero_ref.at[pl.ds(count, count)], y_ref, col_ref, None)
    ghost_apply(blocks, g_ref, y_ref, col_ref, list_ref)
    inner = inner_rows()
    for r in range(count):
        b1_ref[r] = jnp.where(inner, pack(y_ref, r), 0.0)


def second_kernel(
    col_ref, list_ref, send_ref, edge_ref,
    blocks, ops_ref, gop_ref, zero_ref, a1_ref, a2_in, k0_ref, k1_ref, low_ref, high_ref, stats_ref,
    v1_ref, v2_ref, v3_ref, v4_ref, k3_ref, dots_ref, sigma_ref, up_ref, down_ref,
    y_ref, column_ref, square_ref, g_ref,
):
    count = a1_ref.shape[0]
    inner = inner_rows()
    squares, traces = stats_ref[0, :8], stats_ref[0, 8:]
    for s in range(1, stats_ref.shape[0]):
        squares = squares + stats_ref[s, :8]
        traces = traces + stats_ref[s, 8:]
    scale = 1.0 / (stats_ref.shape[0] * NBLK * BS)
    sigma = (1.0 + scale * whole_sum(squares)) * (scale * whole_sum(traces))
    sigma_ref[...] = jnp.broadcast_to(sigma, sigma_ref.shape)
    column_ref[...] = jnp.zeros_like(column_ref)
    v2_ref[...] = a2_in[...]
    complete(v2_ref, low_ref, high_ref, send_ref, edge_ref)
    for r in range(count):
        v1_ref[r] = a1_ref[r]
        for part, ghost, flag in ((low_ref, LOW, 0), (high_ref, HIGH, 1)):
            for j in range(IF):
                v1_ref[r, ghost + j : ghost + j + 1, :] = part[r, 16 + j : 17 + j, :]
        v1 = v1_ref[r] - sigma * zero_ref[r]
        v2_ref[r] = v2_ref[r] - sigma * v1_ref[r] - sigma * v1
        v1 = jnp.where(inner, v1, 0.0)
        v1_ref[r] = v1
        v0 = jnp.where(inner, zero_ref[r], 0.0)
        target = jnp.where(inner, zero_ref[count + r], 0.0)
        second = k1_ref[r] - sigma * k0_ref[r]
        dots_ref[r, 0] = tile_sum(v0, k0_ref[r])
        dots_ref[r, 1] = tile_sum(v1, k0_ref[r])
        dots_ref[r, 2] = tile_sum(v1, second)
        dots_ref[r, 8] = tile_sum(target, k0_ref[r])
        dots_ref[r, 9] = tile_sum(target, second)
    scatter_apply(blocks, ops_ref, v2_ref, y_ref, col_ref, column_ref)
    ghost_images(gop_ref, v2_ref, g_ref)
    ghost_apply(blocks, g_ref, y_ref, col_ref, list_ref)
    for r in range(count):
        image = unpack_columns(column_ref, square_ref, r)
        v3 = jnp.where(inner, pack(y_ref, r) - sigma * v2_ref[r], 0.0)
        v3_ref[r] = v3
        dots_ref[r, 3] = tile_sum(v1_ref[r], image)
        dots_ref[r, 4] = tile_sum(jnp.where(inner, v2_ref[r], 0.0), image)
        dots_ref[r, 5] = tile_sum(v3, image)
        dots_ref[r, 10] = tile_sum(jnp.where(inner, zero_ref[count + r], 0.0), image)
    scatter_apply(blocks, ops_ref, v3_ref, y_ref, col_ref, column_ref)
    for r in range(count):
        image = unpack_columns(column_ref, square_ref, r)
        dots_ref[r, 6] = tile_sum(v3_ref[r], image)
        dots_ref[r, 7] = jnp.zeros((8, LANES), f32)
        dots_ref[r, 11] = tile_sum(jnp.where(inner, zero_ref[count + r], 0.0), image)
        k3_ref[r] = image
        v4_ref[r] = pack(y_ref, r) - sigma * v3_ref[r]
    messages(up_ref, down_ref, v4_ref, send_ref)


def moment_kernel(send_ref, edge_ref, v4_in, k3_ref, low_ref, high_ref, dots_in, b1_ref, v4_ref, dots_ref):
    del b1_ref
    v4_ref[...] = v4_in[...]
    complete(v4_ref, low_ref, high_ref, send_ref, edge_ref)
    lane = lax.broadcasted_iota(jnp.int32, (8, LANES), 1)
    sub = lax.broadcasted_iota(jnp.int32, (8, LANES), 0)
    total = jnp.zeros((8, LANES), f32)
    for r in range(v4_ref.shape[0]):
        for d in range(12):
            part = tile_sum(v4_ref[r], k3_ref[r]) if d == 7 else dots_in[r, d]
            total = jnp.where((lane == d) & (sub == r), whole_sum(part), total)
    dots_ref[...] = total


def third_kernel(col_ref, list_ref, blocks, ops_ref, gop_ref, v4_ref, w5_ref, y_ref, g_ref):
    scatter_apply(blocks, ops_ref, v4_ref, y_ref, col_ref, None)
    ghost_images(gop_ref, v4_ref, g_ref)
    ghost_apply(blocks, g_ref, y_ref, col_ref, list_ref)
    for r in range(v4_ref.shape[0]):
        w5_ref[r] = pack(y_ref, r)


def combine(coef_ref, parts, g, r):
    total = None
    for s in USED[g]:
        term = coef_ref[g, s, r : r + 1, :] * parts[s]
        total = term if total is None else total + term
    return total


def sources(zero_ref, stored, r, count):
    v1_ref, v2_ref, v3_ref, v4_ref, w5_ref, b1_ref = stored
    parts = [zero_ref[r], v1_ref[r], v2_ref[r], v3_ref[r], v4_ref[r], w5_ref[r], zero_ref[count + r], b1_ref[r]]
    inner = inner_rows()
    return [jnp.where(inner, part, 0.0) for part in parts]


def fourth_kernel(col_ref, send_ref, blocks, ops_ref, sums_ref, sigma_ref, zero_ref, *refs):
    stored, (first_ref, base_ref, rho_ref, coef_ref, scale_ref, up_ref, down_ref, y_ref) = refs[:6], refs[6:]
    sums = [sums_ref[s] for s in range(sums_ref.shape[0])]
    while len(sums) > 1:
        sums = [sum(sums[i : i + 2]) for i in range(0, len(sums), 2)]
    sums = sums[0]
    column = lambda d: jnp.broadcast_to(sums[:, d : d + 1], (8, LANES))
    combos, scales = scalars([column(d) for d in range(8)], [column(8 + d) for d in range(4)], sigma_ref[...])
    for g, value in enumerate(scales):
        scale_ref[g] = value
    for g, combo in enumerate(combos):
        for s, value in enumerate(combo):
            if s in USED[g]:
                coef_ref[g, s] = value
    count = rho_ref.shape[0]
    for r in range(count):
        parts = sources(zero_ref, stored, r, count)
        first_ref[r] = combine(coef_ref, parts, 5, r)
        base_ref[r] = combine(coef_ref, parts, 7, r)
    scatter_apply(blocks, ops_ref, first_ref, y_ref, col_ref, None)
    for r in range(count):
        rho_ref[r] = base_ref[r] - scale_ref[0, r : r + 1, :] * pack(y_ref, r)
    messages(up_ref, down_ref, rho_ref, send_ref)


def combine_kernel(ops_ref, coef_ref, zero_ref, *refs):
    stored, (early_ref, zeta_ref, sol_ref, x_ref, column_ref, square_ref) = refs[:6], refs[6:]
    count = zeta_ref.shape[1]
    for r in range(count):
        parts = sources(zero_ref, stored, r, count)
        early_ref[pl.ds(r, NBLK, stride=EARLY), :] = parts[0][OFF:HIGH]
        for g, slot in ((0, 2), (1, 4), (2, 6), (4, 12), (3, 14)):
            early_ref[pl.ds(slot + r, NBLK, stride=EARLY), :] = combine(coef_ref, parts, g, r)[OFF:HIGH]
        for slot in (8, 10):
            early_ref[pl.ds(slot + r, NBLK, stride=EARLY), :] = jnp.zeros((NBLK, LANES), f32)
        zeta_ref[0, r] = combine(coef_ref, parts, 8, r)
        zeta_ref[1, r] = combine(coef_ref, parts, 6, r)
        x_ref[r] = combine(coef_ref, parts, 9, r)
    operator_rows(ops_ref, x_ref, sol_ref, column_ref, square_ref)


def fifth_kernel(
    col_ref, list_ref, send_ref, edge_ref,
    blocks, ops_ref, gop_ref, rho_in, base_ref, zeta_ref, scale_ref, low_ref, high_ref,
    late_ref, y_ref, rho_ref, g_ref,
):
    count = rho_in.shape[0]
    rho_ref[...] = rho_in[...]
    complete(rho_ref, low_ref, high_ref, send_ref, edge_ref)
    scatter_apply(blocks, ops_ref, rho_ref, y_ref, col_ref, None)
    ghost_images(gop_ref, rho_ref, g_ref)
    ghost_apply(blocks, g_ref, y_ref, col_ref, list_ref)
    for r in range(count):
        change = rho_ref[r] - base_ref[r]
        first = zeta_ref[0, r] + scale_ref[1, r : r + 1, :] * change - scale_ref[2, r : r + 1, :] * pack(y_ref, r)
        second = zeta_ref[1, r] + change
        late_ref[pl.ds(r, NBLK, stride=LATE), :] = first[OFF:HIGH]
        late_ref[pl.ds(2 + r, NBLK, stride=LATE), :] = second[OFF:HIGH]


def split(value):
    high = value.astype(jnp.bfloat16)
    return high, (value - high.astype(f32)).astype(jnp.bfloat16)


def product(first, second, dim):
    (fh, fl), (sh, sl) = split(first), split(second)
    left = jnp.concatenate([fh, fl, fh], axis=dim)
    right = jnp.concatenate([sh, sh, sl], axis=0)
    return lax.dot_general(left, right, (((dim,), (0,)), ((), ())), preferred_element_type=f32)


def mixed_kernel(*refs):
    early, mixed_ref = refs[:-1], refs[-1]

    def step(group, carry):
        for i in range(CHUNK):
            at = pl.multiple_of((group * CHUNK + i) * EARLY, EARLY)
            resid = [ref[pl.ds(at, 8), :] for ref in early]
            zeta = [ref[pl.ds(at + 8, 8), :] for ref in early]
            left = jnp.concatenate(resid + zeta, axis=0)
            right = jnp.concatenate(zeta + resid, axis=0)
            mixed_ref[group * CHUNK + i] = product(left, right, 0)
        return carry

    lax.fori_loop(0, NBLK // CHUNK, step, 0)


def grad_kernel(*refs):
    peers = (len(refs) - 3) // 2
    early, late, mixed_ref, weights_ref, grad_ref = refs[:peers], refs[peers : 2 * peers], *refs[-3:]
    upper = lax.broadcasted_iota(jnp.int32, (8, LANES), 0) < LATE

    def join(tiles):
        out = []
        for q in range(0, len(tiles), 2):
            other = pltpu.roll(tiles[q + 1], LATE, 0) if q + 1 < len(tiles) else jnp.zeros((8, LANES), f32)
            out.append(jnp.where(upper, tiles[q], other))
        return out

    def step(group, carry):
        for i in range(CHUNK):
            n = group * CHUNK + i
            at = pl.multiple_of(n * EARLY, EARLY)
            pair = pl.ds(pl.multiple_of(group * (CHUNK * LATE) + 8 * (i // 2), 8), 8)
            resid = join([ref[pl.ds(at, 8), :] for ref in early])
            zeta = [ref[pair, :] for ref in late]
            zeta = join([pltpu.roll(tile, LATE, 0) for tile in zeta] if i % 2 else zeta)
            left = jnp.concatenate(resid + zeta, axis=0)
            right = jnp.concatenate(zeta + resid, axis=0)
            grad = product(weights_ref[n], mixed_ref[n] + product(left, right, 0), 1)

            def write(q, value):
                grad_ref[pl.ds(group * (8 * CUTS) + 8 * q + i, 8, stride=24), :] = value

            flatten(grad, write)
        return carry

    lax.fori_loop(0, NBLK // CHUNK, step, 0)


def from_all(values, axis):
    size = lax.axis_size(axis)
    return lax.all_to_all(jnp.broadcast_to(values[None], (size, *values.shape)), axis, 0, 0)


def all_of(values, axis):
    size = lax.axis_size(axis)
    return [values] + [
        lax.ppermute(values, axis, [(i, (i + d) % size) for i in range(size)]) for d in range(1, size)
    ]


def exchange(up, down):
    size = lax.axis_size("sub")
    rising = [(i, i + 1) for i in range(size - 1)]
    falling = [(j, i) for i, j in rising]
    return lax.ppermute(up, "sub", rising), lax.ppermute(down, "sub", falling)


def plus(first, second):
    if first is None:
        return second
    return first if second is None else first + second


def times(first, second):
    return None if first is None or second is None else first * second


def add(first, second, scale):
    size = max(len(first), len(second))
    first = list(first) + [None] * (size - len(first))
    second = list(second) + [None] * (size - len(second))
    return [plus(a, times(scale, b)) for a, b in zip(first, second)]


def scaled(first, scale):
    return [times(scale, a) for a in first]


def scalars(moments, products, sigma):
    one = jnp.ones_like(sigma)

    def inner(first, second):
        weights = [None] * (len(first) + len(second) - 1)
        for i, a in enumerate(first):
            for j, b in enumerate(second):
                weights[i + j] = plus(weights[i + j], a * b)
        total = None
        for weight, moment in zip(weights, moments):
            total = plus(total, weight * moment)
        return total

    def apply(poly):
        out = [None] * (len(poly) + 1)
        for j, value in enumerate(poly):
            out[j] = plus(out[j], sigma * value)
            out[j + 1] = plus(out[j + 1], value)
        return out

    resid = [[one]]
    direc = [[one]]
    image = []
    step, ratio, norm, curv = [], [None], [moments[0]], []
    for i in range(ITERS):
        image.append(apply(direc[i]))
        curv.append(inner(direc[i], image[i]))
        step.append(norm[i] / curv[i])
        if i + 1 < ITERS:
            resid.append(add(resid[i], image[i], -step[i]))
            norm.append(inner(resid[i + 1], resid[i + 1]))
            ratio.append(norm[i + 1] / norm[i])
            direc.append(add(resid[i + 1], direc[i], ratio[i + 1]))
    cot = []
    for i in range(ITERS):
        total = None
        for j, value in enumerate(resid[i]):
            total = plus(total, value * products[j])
        cot.append(total)
    along = [cot[0]]
    for i in range(1, ITERS):
        along.append(cot[i] + ratio[i] * along[i - 1])

    def row(poly):
        return list(poly) + [None] * (8 - len(poly))

    target = [None] * 6 + [one, None]
    resid_rows = [row(poly) for poly in resid]
    image_rows = [row(poly) for poly in image]
    inverse = [1.0 / value for value in step]

    def resid_prod(i):
        return [norm[l] if l == i else None for l in range(ITERS)]

    def image_prod(i):
        out = [None] * ITERS
        out[i] = norm[i] * inverse[i]
        if i + 1 < ITERS:
            out[i + 1] = -norm[i + 1] * inverse[i]
        return out

    def along_dir(prod, i):
        total = prod[0]
        for l in range(1, i + 1):
            total = plus(prod[l], times(ratio[l], total))
        return total

    def operator_prod(prod):
        out = []
        for l in range(ITERS - 1):
            value = times(add([prod[l]], [prod[l + 1]], -one)[0], inverse[l])
            if l > 0:
                back = times(add([prod[l - 1]], [prod[l]], -one)[0], inverse[l - 1])
                value = add([value], [back], -ratio[l])[0]
            out.append(value)
        return out + [None]

    last = ITERS - 1
    step_bar = along[last]
    curv_bar = -step_bar * step[last] / curv[last]
    dir_row = add(scaled(target, step[last]), image_rows[last], 2 * curv_bar)
    dir_prod = add(scaled(cot, step[last]), image_prod(last), 2 * curv_bar)
    norm_bar = step_bar / curv[last]
    rho_row = [None] * 8
    rho_prod = [None] * ITERS
    zetas = [None] * ITERS
    rho_rows = []
    for i in (2, 1, 0):
        ratio_bar = along_dir(dir_prod, i)
        full = norm_bar + ratio_bar / norm[i]
        zetas[i + 1] = add(dir_row, resid_rows[i + 1], full)
        rho_row = add(add(rho_row, zetas[i + 1], one), resid_rows[i + 1], full)
        rho_prod = add(add(rho_prod, dir_prod, one), resid_prod(i + 1), 2 * full)
        rho_rows.append(rho_row)
        step_bar = along[i] - (rho_prod[i] - rho_prod[i + 1]) * inverse[i]
        curv_bar = -step_bar * step[i] / curv[i]
        oper = [None] * 8
        if i == 2:
            for k in range(5):
                if k < 4:
                    oper[k] = plus(oper[k], times(sigma, rho_row[k]))
                    oper[k + 1] = plus(oper[k + 1], rho_row[k])
                else:
                    oper[5] = plus(oper[5], rho_row[4])
            oper[7] = rho_row[6]
        kept = add(scaled(dir_row, ratio[i + 1]), target, step[i])
        kept = add(kept, image_rows[i], 2 * curv_bar)
        dir_row = add(kept, oper, -step[i])
        dir_prod = add(add(scaled(dir_prod, ratio[i + 1]), cot, step[i]), image_prod(i), 2 * curv_bar)
        dir_prod = add(dir_prod, operator_prod(rho_prod), -step[i])
        norm_bar = step_bar / curv[i] - ratio_bar * norm[i + 1] / (norm[i] * norm[i])
    zetas[0] = add(dir_row, resid_rows[0], norm_bar)
    answer = [None] * 8
    for i in range(ITERS):
        answer = add(answer, row(direc[i]), step[i])
    combos = [resid_rows[1], resid_rows[2], resid_rows[3], zetas[3], zetas[2], rho_rows[1], zetas[1], rho_rows[2], zetas[0], answer]
    return combos, [step[1], ratio[1], step[0]]


def vmem():
    return pl.BlockSpec(memory_space=pltpu.VMEM)


def hbm():
    return pl.BlockSpec(memory_space=pltpu.HBM)


def smem():
    return pl.BlockSpec(memory_space=pltpu.SMEM)


def shards(stiffness, precond, rhs_vec, cotangent, col_index, send_rows, counts):
    count = rhs_vec.shape[0]
    sub = lax.axis_index("sub")
    size = lax.axis_size("sub")
    edge = jnp.stack([sub > 0, sub + 1 < size]).astype(jnp.int32)
    columns = col_index.T
    stiff_cuts = stiffness.reshape(NBLK, K, CUTS, LANES).transpose(0, 2, 1, 3).reshape(NBLK * K * CUTS, LANES)
    weight_cuts = precond.reshape(NBLK // 8, 8, CUTS, LANES).transpose(0, 2, 1, 3).reshape(NBLK * CUTS, LANES)
    base = jnp.concatenate([rhs_vec, cotangent], axis=0).reshape(2 * count, NBLK, BS)
    base = jnp.pad(base, ((0, 0), (OFF, ROWS - HIGH), (0, LANES - BS)))

    def shape(*dims):
        return jax.ShapeDtypeStruct(dims, f32)

    def call(kernel, name, scalars_in, arrays_in, outs, scratch, flops, specs=None, limit=8, in_specs=None):
        return pl.pallas_call(
            kernel,
            in_specs=in_specs or [smem()] * len(scalars_in) + [vmem()] * len(arrays_in),
            out_specs=specs or [vmem()] * len(outs),
            out_shape=outs,
            scratch_shapes=scratch,
            compiler_params=pltpu.CompilerParams(vmem_limit_bytes=limit * MIB),
            cost_estimate=pl.CostEstimate(flops=flops, bytes_accessed=flops // 2, transcendentals=0),
            name=name,
        )(*scalars_in, *arrays_in)

    rows = shape(count, ROWS, LANES)
    message = shape(count, 16, LANES)
    longer = shape(count, 24, LANES)
    ghost_message = shape(IF, CUTS + 8, LANES)
    partial = lambda r: pltpu.VMEM((r, ROWS, 8, LANES), f32)
    turned = [pltpu.VMEM((count, BS, LANES), f32), pltpu.VMEM((LANES, LANES), f32)]
    held = lambda r: pltpu.VMEM((r, ROWS, LANES), f32)
    grams = pltpu.VMEM((2, BS, LANES), f32)
    work = 4 * MIB

    up, down = call(pack_kernel, "pack", [send_rows], [weight_cuts, base], [ghost_message] * 2, [], MIB)
    near, far = exchange(up, down)

    blocks, weights, ops, halo_list, stats = call(
        prepare_kernel, "prepare", [columns], [weight_cuts, stiff_cuts],
        [
            shape(NBLK, K, BS, LANES), shape(NBLK, BS, LANES), shape(NBLK, BS, LANES),
            jax.ShapeDtypeStruct((1, NBLK * K + 8), jnp.int32), shape(16, LANES),
        ],
        [grams, pltpu.VMEM((NBLK * K * CUTS, LANES), f32), pltpu.SemaphoreType.DMA((NBLK // CHUNK,))],
        2 * work, [vmem(), vmem(), vmem(), smem(), vmem()], 16, [smem(), vmem(), hbm()],
    )
    stats = from_all(stats, "sub")

    zero, a1, a2, up, down = call(
        first_kernel, "first", [columns, halo_list, send_rows, counts], [blocks, ops, base, near, far],
        [shape(2 * count, ROWS, LANES), rows, rows, longer, longer],
        [partial(count), held(count)], 2 * work,
    )
    low, high = exchange(up, down)

    gops, k0, k1 = call(
        ghost_kernel, "ghosts", [], [ops, zero, a1, near, far],
        [shape(2 * IF, BS, LANES), rows, rows], [grams, *turned], work,
    )

    v1, v2, v3, v4, k3, dots, sigma, up, down = call(
        second_kernel, "second", [columns, halo_list, send_rows, edge],
        [blocks, ops, gops, zero, a1, a2, k0, k1, low, high, stats],
        [rows, rows, rows, rows, rows, shape(count, 12, 8, LANES), shape(8, LANES), message, message],
        [partial(count), *turned, held(count)], 2 * work,
    )
    low, high = exchange(up, down)

    zero, v3 = lax.optimization_barrier((zero, v3))
    (b1,) = call(
        target_kernel, "target", [columns, halo_list], [blocks, ops, zero, near, far], [rows],
        [partial(count), held(count)], work,
    )

    v4, dots = call(
        moment_kernel, "moments", [send_rows, edge], [v4, k3, low, high, dots, b1], [rows, shape(8, LANES)], [], MIB
    )
    sums = from_all(dots, "sub")

    (w5,) = call(
        third_kernel, "third", [columns, halo_list], [blocks, ops, gops, v4], [rows],
        [partial(count), held(count)], work,
    )

    stored = [zero, v1, v2, v3, v4, w5, b1]
    first, fixed, rho, coefs, scales, up, down = call(
        fourth_kernel, "fourth", [columns, send_rows], [blocks, ops, sums, sigma, *stored],
        [rows, rows, rows, shape(10, 8, 8, LANES), shape(3, 8, LANES), message, message], [partial(count)], work,
    )
    low, high = exchange(up, down)

    early, zeta, answer = call(
        combine_kernel, "combine", [], [ops, coefs, *stored],
        [shape(NBLK * EARLY, LANES), shape(2, count, ROWS, LANES), rows], [held(count), *turned], MIB,
    )
    early = all_of(early, "rhs")

    (late,) = call(
        fifth_kernel, "fifth", [columns, halo_list, send_rows, edge],
        [blocks, ops, gops, rho, fixed, zeta, scales, low, high],
        [shape(NBLK * LATE, LANES)], [partial(count), held(count), held(count)], work,
    )
    late = all_of(late, "rhs")

    (mixed,) = call(mixed_kernel, "mixed", [], early, [shape(NBLK, LANES, LANES)], [], work)
    (grad,) = call(grad_kernel, "grad", [], [*early, *late, mixed, weights], [shape(NBLK * CUTS, LANES)], [], work)
    grad = grad.reshape(NBLK // 8, CUTS, 8, LANES).transpose(0, 2, 1, 3).reshape(NBLK, BS * BS)
    return answer[:, OFF:HIGH, :BS].reshape(count, NBLK * BS), grad


def solution(mesh):
    in_specs = (
        P("sub", None, None),
        P("sub", None),
        P("rhs", "sub"),
        P("rhs", "sub"),
        P("sub", None),
        P("sub", None),
        P("sub"),
    )
    out_specs = (P("rhs", "sub"), P("sub", None))
    return jax.shard_map(shards, mesh=mesh, in_specs=in_specs, out_specs=out_specs, check_vma=False)
```

```python
import functools

import jax
import jax.numpy as jnp
from jax import lax
from jax.experimental import pallas as pl
from jax.experimental.pallas import tpu as pltpu
from jax.sharding import PartitionSpec as P

BS = 96
K = 4
NBLK = 48
IF = 6
ITERS = 4
ALL = (0, 1, 2, 3, 4, 5, 6, 7)
USED = ((0, 1), (0, 1, 2), (0, 1, 2, 3), (0, 1, 2, 3, 4, 6), ALL, ALL, ALL, ALL, ALL, (0, 1, 2, 3))
EARLY = 16
LATE = 4
CUTS = BS * BS // 128
LANES = 128
OFF = 8
ROWS = 64
LOW = OFF - IF
HIGH = OFF + NBLK
CHUNK = 8
MIB = 1024 * 1024

highest = lax.Precision.HIGHEST
f32 = jnp.float32


def own(value):
    return value[:, OFF:HIGH]


def lane_ids():
    return lax.broadcasted_iota(jnp.int32, (BS, LANES), 1)


def diagonal():
    pos = lax.broadcasted_iota(jnp.int32, (BS, LANES), 0)
    row = (pos & ~31) + 4 * (pos & 7) + ((pos >> 3) & 3)
    return row == lane_ids()


def fold(prod):
    return jnp.sum(prod.reshape(BS // 8, 8, prod.shape[-1]), axis=0)


def unflatten(read):
    lane = lax.broadcasted_iota(jnp.int32, (8, LANES), 1)
    out = []
    for h in range(BS // 32):
        one, two, three = (read(24 * h + m) for m in range(3))
        out.append(jnp.where(lane < BS, one, 0.0))
        mixed = jnp.where(lane < 32, pltpu.roll(one, 32, 1), pltpu.roll(two, 32, 1))
        out.append(jnp.where(lane < BS, mixed, 0.0))
        mixed = jnp.where(lane < 64, pltpu.roll(two, 64, 1), pltpu.roll(three, 64, 1))
        out.append(jnp.where(lane < BS, mixed, 0.0))
        out.append(jnp.where(lane < BS, pltpu.roll(three, 96, 1), 0.0))
    return jnp.concatenate(out, axis=0)


def flatten(block, write):
    lane = lax.broadcasted_iota(jnp.int32, (8, LANES), 1)
    for h in range(BS // 32):
        one, two, three, four = (block[32 * h + 8 * j : 32 * h + 8 * j + 8] for j in range(4))
        two = pltpu.roll(two, 96, 1)
        three = pltpu.roll(three, 64, 1)
        write(24 * h, jnp.where(lane < BS, one, two))
        write(24 * h + 1, jnp.where(lane < 64, two, three))
        write(24 * h + 2, jnp.where(lane < 32, three, pltpu.roll(four, 32, 1)))


def make_operator(weights, gram_ref):
    gram = lax.dot_general(
        weights, weights, (((0,), (0,)), ((), ())), precision=highest, preferred_element_type=f32
    )
    gram_ref[...] = gram[:BS]
    rows = [gram_ref[pl.ds(32 * h + j, 8, stride=4), :] for h in range(BS // 32) for j in range(4)]
    return jnp.concatenate(rows, axis=0) + jnp.where(diagonal(), 1.0, 0.0)


def scatter_apply(blocks, op_ref, x_ref, y_ref, col_ref, column_ref):
    count = x_ref.shape[0]
    y_ref[...] = jnp.zeros_like(y_ref)

    def step(group, carry):
        base = pl.multiple_of(group * CHUNK, CHUNK)
        tiles = [x_ref[r, pl.ds(base + OFF, CHUNK), :] for r in range(count)]
        for i in range(CHUNK):
            n = group * CHUNK + i
            oper = op_ref[n]
            images = [jnp.sum(oper * tiles[r][i : i + 1, :], axis=1, keepdims=True) for r in range(count)]
            if column_ref is not None:
                for r in range(count):
                    column_ref[r] = jnp.where(lane_ids() == n + OFF, images[r], column_ref[r])
            for k in range(K):
                block = blocks[n, k]
                slot = col_ref[k, n] + LOW
                for r in range(count):
                    y_ref[r, slot] = y_ref[r, slot] + fold(block * images[r])
        return carry

    lax.fori_loop(0, NBLK // CHUNK, step, 0)


def ghost_images(op_ref, x_ref, g_ref):
    count = x_ref.shape[0]
    mask = diagonal()
    g_ref[...] = jnp.zeros_like(g_ref)
    for first, side in ((LOW, 0), (HIGH, IF)):
        for j in range(IF):
            slot = first + j
            oper = op_ref[side + j]
            for r in range(count):
                image = jnp.sum(oper * x_ref[r, slot : slot + 1, :], axis=1, keepdims=True)
                line = jnp.sum(fold(jnp.where(mask, image, 0.0)), axis=0, keepdims=True)
                g_ref[r, slot : slot + 1, :] = line


def ghost_apply(blocks, g_ref, y_ref, col_ref, list_ref):
    count = g_ref.shape[0]
    mask = diagonal()

    def step(item, carry):
        for u in range(4):
            entry = list_ref[0, 1 + item * 4 + u]
            n = entry >> 2
            k = entry & 3
            slot = col_ref[k, n] + LOW
            block = blocks[n, k]
            for r in range(count):
                image = jnp.sum(block * g_ref[r, pl.ds(slot, 1), :], axis=1, keepdims=True)
                y_ref[r, n + OFF] = y_ref[r, n + OFF] + fold(jnp.where(mask, image, 0.0))
        return carry

    lax.fori_loop(0, (list_ref[0, 0] + 3) >> 2, step, 0)


def pack(y_ref, r):
    sub = lax.broadcasted_iota(jnp.int32, (8, LANES), 0)
    groups = []
    for g in range(ROWS // 8):
        total = jnp.zeros((8, LANES), f32)
        for i in range(8):
            line = jnp.sum(y_ref[r, g * 8 + i], axis=0, keepdims=True)
            total = jnp.where(sub == i, line, total)
        groups.append(total)
    return jnp.concatenate(groups, axis=0)


def unpack_columns(column_ref, square_ref, r):
    for h in range(BS // 32):
        for j in range(4):
            start = 32 * h + 8 * j
            square_ref[pl.ds(32 * h + j, 8, stride=4), :] = column_ref[r, start : start + 8, :]
    square_ref[BS:, :] = jnp.zeros((LANES - BS, LANES), f32)
    return square_ref[...].T[:ROWS]


def messages(up_ref, down_ref, v_ref, send_ref, extra_ref=None):
    for r in range(v_ref.shape[0]):
        for j in range(IF):
            low = pl.ds(send_ref[0, j] + OFF, 1)
            high = pl.ds(send_ref[0, IF + j] + OFF, 1)
            down_ref[r, j : j + 1, :] = v_ref[r, low, :]
            up_ref[r, j : j + 1, :] = v_ref[r, high, :]
            down_ref[r, 8 + j : 9 + j, :] = v_ref[r, LOW + j : LOW + j + 1, :]
            up_ref[r, 8 + j : 9 + j, :] = v_ref[r, HIGH + j : HIGH + j + 1, :]
            if extra_ref is not None:
                down_ref[r, 16 + j : 17 + j, :] = extra_ref[r, low, :]
                up_ref[r, 16 + j : 17 + j, :] = extra_ref[r, high, :]


def complete(v_ref, low_ref, high_ref, send_ref, edge_ref):
    for r in range(v_ref.shape[0]):
        for j in range(IF):
            for part, base, ghost, flag in ((low_ref, 0, LOW, 0), (high_ref, IF, HIGH, 1)):
                at = pl.ds(send_ref[0, base + j] + OFF, 1)
                v_ref[r, at, :] = v_ref[r, at, :] + part[r, 8 + j : 9 + j, :]
                slot = ghost + j
                summed = v_ref[r, slot : slot + 1, :] + part[r, j : j + 1, :]
                v_ref[r, slot : slot + 1, :] = jnp.where(edge_ref[flag] > 0, summed, 0.0)


def tile_sum(first, second):
    prod = first * second
    return jnp.sum(prod.reshape(prod.shape[0] // 8, 8, LANES), axis=0)


def whole_sum(tile):
    return jnp.sum(jnp.sum(tile, axis=0, keepdims=True), axis=1, keepdims=True)


def inner_rows():
    row = lax.broadcasted_iota(jnp.int32, (ROWS, LANES), 0)
    return (row >= OFF) & (row < HIGH)


def pack_kernel(send_ref, raw_ref, base_ref, up_ref, down_ref):
    vectors = base_ref.shape[0]
    for part, ref in ((0, down_ref), (IF, up_ref)):
        for j in range(IF):
            n = send_ref[0, part + j]
            start = (n >> 3) * (8 * CUTS) + (n & 7)
            for i in range(CUTS // 8):
                ref[j, 8 * i : 8 * i + 8, :] = raw_ref[pl.ds(start + 64 * i, 8, stride=8), :]
            ref[j, CUTS:, :] = jnp.zeros((8, LANES), f32)
            weights = unflatten(lambda q: raw_ref[pl.ds(start + 8 * q, 8, stride=24), :])
            for r in range(vectors):
                line = base_ref[r, pl.ds(n + OFF, 1), :]
                ref[j, CUTS + r : CUTS + r + 1, :] = line
                if r < vectors // 2:
                    inside = jnp.sum(weights * line, axis=1, keepdims=True)
                    image = line + jnp.sum(fold(weights * inside), axis=0, keepdims=True)
                    at = CUTS + vectors + r
                    ref[j, at : at + 1, :] = image


def operator_kernel(raw_ref, weights_ref, ops_ref, squares_ref, gram_ref):
    def step(group, squares):
        for i in range(CHUNK):
            n = group * CHUNK + i
            weights = unflatten(lambda q: raw_ref[pl.ds(group * (8 * CUTS) + 8 * q + i, 8, stride=24), :])
            weights_ref[n] = weights
            squares = squares + fold(weights * weights)
            ops_ref[n] = make_operator(weights, gram_ref.at[i & 1])
        return squares

    squares_ref[...] = lax.fori_loop(0, NBLK // CHUNK, step, jnp.zeros((8, LANES), f32))


def blocks_kernel(col_ref, stiff_ref, squares_ref, blocks_ref, list_ref, stats_ref):
    mask = diagonal()

    def step(group, carry):
        count, traces = carry
        for i in range(CHUNK):
            n = group * CHUNK + i
            for k in range(K):
                block = unflatten(lambda q: stiff_ref[pl.ds(n * (CUTS * K) + 4 * q + k, 8, stride=12), :])
                blocks_ref[n, k] = block
                if k == 0:
                    traces = traces + fold(jnp.where(mask, block, 0.0))
                col = col_ref[k, n]
                list_ref[0, 1 + count] = n * K + k
                count = count + jnp.where((col < IF) | (col >= IF + NBLK), 1, 0)
        return count, traces

    count, traces = lax.fori_loop(0, NBLK // CHUNK, step, (jnp.int32(0), jnp.zeros((8, LANES), f32)))
    list_ref[0, 0] = count
    for u in range(4):
        list_ref[0, 1 + count + u] = 0
    stats_ref[:8] = squares_ref[...]
    stats_ref[8:] = traces


def first_kernel(
    col_ref, list_ref, send_ref, count_ref,
    blocks, op_ref, base_ref, low_ref, high_ref,
    zero_ref, a1_ref, a2_ref, up_ref, down_ref,
    y_ref, g_ref,
):
    count = a1_ref.shape[0]
    zero_ref[...] = base_ref[...]
    g_ref[...] = jnp.zeros_like(g_ref)
    row = lax.broadcasted_iota(jnp.int32, (ROWS, LANES), 0)
    dead = (row >= count_ref[0] + OFF) & (row < HIGH)
    for r in range(count):
        zero_ref[r] = jnp.where(dead, 0.0, zero_ref[r])
        for part, first in ((low_ref, LOW), (high_ref, HIGH)):
            for j in range(IF):
                at = slice(first + j, first + j + 1)
                for s in (r, count + r):
                    zero_ref[s, at, :] = part[j, CUTS + s : CUTS + s + 1, :]
                g_ref[r, at, :] = part[j, CUTS + 2 * count + r : CUTS + 2 * count + r + 1, :]
    scatter_apply(blocks, op_ref, zero_ref.at[pl.ds(0, count)], y_ref, col_ref, None)
    ghost_apply(blocks, g_ref, y_ref, col_ref, list_ref)
    inner = inner_rows()
    for r in range(count):
        a1_ref[r] = jnp.where(inner, pack(y_ref, r), 0.0)
    scatter_apply(blocks, op_ref, a1_ref, y_ref, col_ref, None)
    for r in range(count):
        a2_ref[r] = pack(y_ref, r)
    messages(up_ref, down_ref, a2_ref, send_ref, a1_ref)


def operator_rows(op_ref, x_ref, out_ref, column_ref, square_ref):
    column_ref[...] = jnp.zeros_like(column_ref)
    lanes = lane_ids()
    for r in range(column_ref.shape[0]):
        for n in range(NBLK):
            image = jnp.sum(op_ref[n] * x_ref[r, n + OFF : n + OFF + 1, :], axis=1, keepdims=True)
            column_ref[r] = jnp.where(lanes == n + OFF, image, column_ref[r])
        out_ref[r] = unpack_columns(column_ref, square_ref, r)


def ghost_kernel(op_ref, zero_ref, a1_ref, low_ref, high_ref, gop_ref, k0_ref, k1_ref, gram_ref, column_ref, square_ref):
    for part, first in ((low_ref, 0), (high_ref, IF)):
        for j in range(IF):
            weights = unflatten(lambda q: part[j, pl.ds(q, 8, stride=3), :])
            gop_ref[first + j] = make_operator(weights, gram_ref.at[j & 1])
    operator_rows(op_ref, zero_ref, k0_ref, column_ref, square_ref)
    operator_rows(op_ref, a1_ref, k1_ref, column_ref, square_ref)


def target_kernel(col_ref, list_ref, blocks, op_ref, gop_ref, zero_ref, b1_ref, y_ref, g_ref):
    count = b1_ref.shape[0]
    target = zero_ref.at[pl.ds(count, count)]
    scatter_apply(blocks, op_ref, target, y_ref, col_ref, None)
    ghost_images(gop_ref, target, g_ref)
    ghost_apply(blocks, g_ref, y_ref, col_ref, list_ref)
    inner = inner_rows()
    for r in range(count):
        b1_ref[r] = jnp.where(inner, pack(y_ref, r), 0.0)


def second_kernel(
    col_ref, list_ref, send_ref, edge_ref,
    blocks, ops_ref, gop_ref, zero_ref, a1_ref, a2_in, k0_ref, k1_ref, low_ref, high_ref, stats_ref,
    v1_ref, v2_ref, v3_ref, v4_ref, k3_ref, dots_ref, sigma_ref, up_ref, down_ref,
    y_ref, column_ref, square_ref, g_ref,
):
    count = a1_ref.shape[0]
    inner = inner_rows()
    squares, traces = stats_ref[0, :8], stats_ref[0, 8:]
    for s in range(1, stats_ref.shape[0]):
        squares = squares + stats_ref[s, :8]
        traces = traces + stats_ref[s, 8:]
    scale = 1.0 / (lax.axis_size("sub") * NBLK * BS)
    sigma = (1.0 + scale * whole_sum(squares)) * (scale * whole_sum(traces))
    sigma_ref[...] = jnp.broadcast_to(sigma, sigma_ref.shape)
    column_ref[...] = jnp.zeros_like(column_ref)
    v2_ref[...] = a2_in[...]
    complete(v2_ref, low_ref, high_ref, send_ref, edge_ref)
    for r in range(count):
        v1_ref[r] = a1_ref[r]
        for part, ghost, flag in ((low_ref, LOW, 0), (high_ref, HIGH, 1)):
            for j in range(IF):
                v1_ref[r, ghost + j : ghost + j + 1, :] = part[r, 16 + j : 17 + j, :]
        v1 = v1_ref[r] - sigma * zero_ref[r]
        v2_ref[r] = v2_ref[r] - sigma * v1_ref[r] - sigma * v1
        v1 = jnp.where(inner, v1, 0.0)
        v1_ref[r] = v1
        v0 = jnp.where(inner, zero_ref[r], 0.0)
        target = jnp.where(inner, zero_ref[count + r], 0.0)
        second = k1_ref[r] - sigma * k0_ref[r]
        dots_ref[r, 0] = tile_sum(v0, k0_ref[r])
        dots_ref[r, 1] = tile_sum(v1, k0_ref[r])
        dots_ref[r, 2] = tile_sum(v1, second)
        dots_ref[r, 8] = tile_sum(target, k0_ref[r])
        dots_ref[r, 9] = tile_sum(target, second)
    scatter_apply(blocks, ops_ref, v2_ref, y_ref, col_ref, column_ref)
    ghost_images(gop_ref, v2_ref, g_ref)
    ghost_apply(blocks, g_ref, y_ref, col_ref, list_ref)
    for r in range(count):
        image = unpack_columns(column_ref, square_ref, r)
        v3 = jnp.where(inner, pack(y_ref, r) - sigma * v2_ref[r], 0.0)
        v3_ref[r] = v3
        dots_ref[r, 3] = tile_sum(v1_ref[r], image)
        dots_ref[r, 4] = tile_sum(jnp.where(inner, v2_ref[r], 0.0), image)
        dots_ref[r, 5] = tile_sum(v3, image)
        dots_ref[r, 10] = tile_sum(jnp.where(inner, zero_ref[count + r], 0.0), image)
    scatter_apply(blocks, ops_ref, v3_ref, y_ref, col_ref, column_ref)
    for r in range(count):
        image = unpack_columns(column_ref, square_ref, r)
        dots_ref[r, 6] = tile_sum(v3_ref[r], image)
        dots_ref[r, 7] = jnp.zeros((8, LANES), f32)
        dots_ref[r, 11] = tile_sum(jnp.where(inner, zero_ref[count + r], 0.0), image)
        k3_ref[r] = image
        v4_ref[r] = pack(y_ref, r) - sigma * v3_ref[r]
    messages(up_ref, down_ref, v4_ref, send_ref)


def moment_kernel(send_ref, edge_ref, v4_in, k3_ref, low_ref, high_ref, dots_in, b1_ref, v4_ref, dots_ref):
    del b1_ref
    v4_ref[...] = v4_in[...]
    complete(v4_ref, low_ref, high_ref, send_ref, edge_ref)
    lane = lax.broadcasted_iota(jnp.int32, (8, LANES), 1)
    sub = lax.broadcasted_iota(jnp.int32, (8, LANES), 0)
    total = jnp.zeros((8, LANES), f32)
    for r in range(v4_ref.shape[0]):
        for d in range(12):
            part = tile_sum(v4_ref[r], k3_ref[r]) if d == 7 else dots_in[r, d]
            total = jnp.where((lane == d) & (sub == r), whole_sum(part), total)
    dots_ref[...] = total


def third_kernel(col_ref, list_ref, blocks, ops_ref, gop_ref, v4_ref, w5_ref, y_ref, g_ref):
    scatter_apply(blocks, ops_ref, v4_ref, y_ref, col_ref, None)
    ghost_images(gop_ref, v4_ref, g_ref)
    ghost_apply(blocks, g_ref, y_ref, col_ref, list_ref)
    for r in range(v4_ref.shape[0]):
        w5_ref[r] = pack(y_ref, r)


def combine(coef_ref, parts, g, r):
    total = None
    for s in USED[g]:
        term = coef_ref[g, s, r : r + 1, :] * parts[s]
        total = term if total is None else total + term
    return total


def sources(zero_ref, stored, r, count):
    v1_ref, v2_ref, v3_ref, v4_ref, w5_ref, b1_ref = stored
    parts = [zero_ref[r], v1_ref[r], v2_ref[r], v3_ref[r], v4_ref[r], w5_ref[r], zero_ref[count + r], b1_ref[r]]
    inner = inner_rows()
    return [jnp.where(inner, part, 0.0) for part in parts]


def fourth_kernel(col_ref, send_ref, blocks, ops_ref, sigma_ref, zero_ref, *refs):
    stored, sums = refs[:6], [part[...] for part in refs[6:-8]]
    first_ref, base_ref, rho_ref, coef_ref, scale_ref, up_ref, down_ref, y_ref = refs[-8:]
    while len(sums) > 1:
        sums = [sums[i] + sums[i + 1] for i in range(0, len(sums), 2)]
    sums = sums[0]
    column = lambda d: jnp.broadcast_to(sums[:, d : d + 1], (8, LANES))
    combos, scales = scalars([column(d) for d in range(8)], [column(8 + d) for d in range(4)], sigma_ref[...])
    for g, value in enumerate(scales):
        scale_ref[g] = value
    for g, combo in enumerate(combos):
        for s, value in enumerate(combo):
            if s in USED[g]:
                coef_ref[g, s] = value
    count = rho_ref.shape[0]
    for r in range(count):
        parts = sources(zero_ref, stored, r, count)
        first_ref[r] = combine(coef_ref, parts, 5, r)
        base_ref[r] = combine(coef_ref, parts, 7, r)
    scatter_apply(blocks, ops_ref, first_ref, y_ref, col_ref, None)
    for r in range(count):
        rho_ref[r] = base_ref[r] - scale_ref[0, r : r + 1, :] * pack(y_ref, r)
    messages(up_ref, down_ref, rho_ref, send_ref)


def early_kernel(coef_ref, zero_ref, *refs):
    stored, early_ref = refs[:6], refs[6]
    count = zero_ref.shape[0] // 2
    for r in range(count):
        parts = sources(zero_ref, stored, r, count)
        early_ref[pl.ds(r, NBLK, stride=EARLY), :] = parts[0][OFF:HIGH]
        for g, slot in ((0, 2), (1, 4), (2, 6), (4, 12), (3, 14)):
            early_ref[pl.ds(slot + r, NBLK, stride=EARLY), :] = combine(coef_ref, parts, g, r)[OFF:HIGH]
        for slot in (8, 10):
            early_ref[pl.ds(slot + r, NBLK, stride=EARLY), :] = jnp.zeros((NBLK, LANES), f32)


def answer_kernel(ops_ref, coef_ref, zero_ref, *refs):
    stored, (zeta_ref, sol_ref, x_ref, column_ref, square_ref) = refs[:6], refs[6:]
    count = zeta_ref.shape[1]
    for r in range(count):
        parts = sources(zero_ref, stored, r, count)
        zeta_ref[0, r] = combine(coef_ref, parts, 8, r)
        zeta_ref[1, r] = combine(coef_ref, parts, 6, r)
        x_ref[r] = combine(coef_ref, parts, 9, r)
    operator_rows(ops_ref, x_ref, sol_ref, column_ref, square_ref)


def fifth_kernel(
    col_ref, list_ref, send_ref, edge_ref,
    blocks, ops_ref, gop_ref, rho_in, base_ref, zeta_ref, scale_ref, low_ref, high_ref,
    late_ref, y_ref, rho_ref, g_ref,
):
    count = rho_in.shape[0]
    rho_ref[...] = rho_in[...]
    complete(rho_ref, low_ref, high_ref, send_ref, edge_ref)
    scatter_apply(blocks, ops_ref, rho_ref, y_ref, col_ref, None)
    ghost_images(gop_ref, rho_ref, g_ref)
    ghost_apply(blocks, g_ref, y_ref, col_ref, list_ref)
    for r in range(count):
        change = rho_ref[r] - base_ref[r]
        first = zeta_ref[0, r] + scale_ref[1, r : r + 1, :] * change - scale_ref[2, r : r + 1, :] * pack(y_ref, r)
        second = zeta_ref[1, r] + change
        late_ref[pl.ds(r, NBLK, stride=LATE), :] = first[OFF:HIGH]
        late_ref[pl.ds(2 + r, NBLK, stride=LATE), :] = second[OFF:HIGH]


def split(value):
    high = value.astype(jnp.bfloat16)
    return high, (value - high.astype(f32)).astype(jnp.bfloat16)


def product(first, second, dim):
    (fh, fl), (sh, sl) = split(first), split(second)
    left = jnp.concatenate([fh, fl, fh], axis=dim)
    right = jnp.concatenate([sh, sh, sl], axis=0)
    return lax.dot_general(left, right, (((dim,), (0,)), ((), ())), preferred_element_type=f32)


def mixed_kernel(*refs):
    early, mixed_ref = refs[:-1], refs[-1]

    def step(group, carry):
        for i in range(CHUNK):
            at = pl.multiple_of((group * CHUNK + i) * EARLY, EARLY)
            resid = [ref[pl.ds(at, 8), :] for ref in early]
            zeta = [ref[pl.ds(at + 8, 8), :] for ref in early]
            left = jnp.concatenate(resid + zeta, axis=0)
            right = jnp.concatenate(zeta + resid, axis=0)
            mixed_ref[group * CHUNK + i] = product(left, right, 0)
        return carry

    lax.fori_loop(0, NBLK // CHUNK, step, 0)


def grad_kernel(*refs):
    peers = (len(refs) - 3) // 2
    early, late, mixed_ref, weights_ref, grad_ref = refs[:peers], refs[peers : 2 * peers], *refs[-3:]
    upper = lax.broadcasted_iota(jnp.int32, (8, LANES), 0) < LATE

    def join(tiles):
        out = []
        for q in range(0, len(tiles), 2):
            other = pltpu.roll(tiles[q + 1], LATE, 0) if q + 1 < len(tiles) else jnp.zeros((8, LANES), f32)
            out.append(jnp.where(upper, tiles[q], other))
        return out

    def step(group, carry):
        for i in range(CHUNK):
            n = group * CHUNK + i
            at = pl.multiple_of(n * EARLY, EARLY)
            pair = pl.ds(pl.multiple_of(group * (CHUNK * LATE) + 8 * (i // 2), 8), 8)
            resid = join([ref[pl.ds(at, 8), :] for ref in early])
            zeta = [ref[pair, :] for ref in late]
            zeta = join([pltpu.roll(tile, LATE, 0) for tile in zeta] if i % 2 else zeta)
            left = jnp.concatenate(resid + zeta, axis=0)
            right = jnp.concatenate(zeta + resid, axis=0)
            grad = product(weights_ref[n], mixed_ref[n] + product(left, right, 0), 1)

            def write(q, value):
                grad_ref[pl.ds(group * (8 * CUTS) + 8 * q + i, 8, stride=24), :] = value

            flatten(grad, write)
        return carry

    lax.fori_loop(0, NBLK // CHUNK, step, 0)


def parts_over(values, axis, most):
    size = lax.axis_size(axis)
    if size & (size - 1):
        return [lax.psum(values, axis)]
    parts = [values]
    step = 1
    while step < size:
        while len(parts) > 1:
            parts = [parts[i] + parts[i + 1] for i in range(0, len(parts), 2)]
        width = min(most, size // step)
        for d in range(1, width):
            parts.append(lax.ppermute(parts[0], axis, [(i, i ^ (d * step)) for i in range(size)]))
        step *= width
    return parts


def widening(parts, axis, step, most):
    if step is None:
        return parts, None
    size = lax.axis_size(axis)
    if size & (size - 1):
        return [lax.psum(parts[0], axis)], None
    step = step or 1
    while len(parts) > 1:
        parts = [parts[i] + parts[i + 1] for i in range(0, len(parts), 2)]
    width = min(most, size // step)
    total = parts[0]
    parts = [total] + [lax.ppermute(total, axis, [(i, i ^ (d * step)) for i in range(size)]) for d in range(1, width)]
    step *= width
    return parts, step if step < size else None


def all_of(values, axis):
    size = lax.axis_size(axis)
    return [values] + [
        lax.ppermute(values, axis, [(i, (i + d) % size) for i in range(size)]) for d in range(1, size)
    ]


def exchange(up, down):
    size = lax.axis_size("sub")
    rising = [(i, i + 1) for i in range(size - 1)]
    falling = [(j, i) for i, j in rising]
    return lax.ppermute(up, "sub", rising), lax.ppermute(down, "sub", falling)


def plus(first, second):
    if first is None:
        return second
    return first if second is None else first + second


def times(first, second):
    return None if first is None or second is None else first * second


def add(first, second, scale):
    size = max(len(first), len(second))
    first = list(first) + [None] * (size - len(first))
    second = list(second) + [None] * (size - len(second))
    return [plus(a, times(scale, b)) for a, b in zip(first, second)]


def scaled(first, scale):
    return [times(scale, a) for a in first]


def scalars(moments, products, sigma):
    one = jnp.ones_like(sigma)

    def inner(first, second):
        weights = [None] * (len(first) + len(second) - 1)
        for i, a in enumerate(first):
            for j, b in enumerate(second):
                weights[i + j] = plus(weights[i + j], a * b)
        total = None
        for weight, moment in zip(weights, moments):
            total = plus(total, weight * moment)
        return total

    def apply(poly):
        out = [None] * (len(poly) + 1)
        for j, value in enumerate(poly):
            out[j] = plus(out[j], sigma * value)
            out[j + 1] = plus(out[j + 1], value)
        return out

    resid = [[one]]
    direc = [[one]]
    image = []
    step, ratio, norm, curv = [], [None], [moments[0]], []
    for i in range(ITERS):
        image.append(apply(direc[i]))
        curv.append(inner(direc[i], image[i]))
        step.append(norm[i] / curv[i])
        if i + 1 < ITERS:
            resid.append(add(resid[i], image[i], -step[i]))
            norm.append(inner(resid[i + 1], resid[i + 1]))
            ratio.append(norm[i + 1] / norm[i])
            direc.append(add(resid[i + 1], direc[i], ratio[i + 1]))
    cot = []
    for i in range(ITERS):
        total = None
        for j, value in enumerate(resid[i]):
            total = plus(total, value * products[j])
        cot.append(total)
    along = [cot[0]]
    for i in range(1, ITERS):
        along.append(cot[i] + ratio[i] * along[i - 1])

    def row(poly):
        return list(poly) + [None] * (8 - len(poly))

    target = [None] * 6 + [one, None]
    resid_rows = [row(poly) for poly in resid]
    image_rows = [row(poly) for poly in image]
    inverse = [1.0 / value for value in step]

    def resid_prod(i):
        return [norm[l] if l == i else None for l in range(ITERS)]

    def image_prod(i):
        out = [None] * ITERS
        out[i] = norm[i] * inverse[i]
        if i + 1 < ITERS:
            out[i + 1] = -norm[i + 1] * inverse[i]
        return out

    def along_dir(prod, i):
        total = prod[0]
        for l in range(1, i + 1):
            total = plus(prod[l], times(ratio[l], total))
        return total

    def operator_prod(prod):
        out = []
        for l in range(ITERS - 1):
            value = times(add([prod[l]], [prod[l + 1]], -one)[0], inverse[l])
            if l > 0:
                back = times(add([prod[l - 1]], [prod[l]], -one)[0], inverse[l - 1])
                value = add([value], [back], -ratio[l])[0]
            out.append(value)
        return out + [None]

    last = ITERS - 1
    step_bar = along[last]
    curv_bar = -step_bar * step[last] / curv[last]
    dir_row = add(scaled(target, step[last]), image_rows[last], 2 * curv_bar)
    dir_prod = add(scaled(cot, step[last]), image_prod(last), 2 * curv_bar)
    norm_bar = step_bar / curv[last]
    rho_row = [None] * 8
    rho_prod = [None] * ITERS
    zetas = [None] * ITERS
    rho_rows = []
    for i in (2, 1, 0):
        ratio_bar = along_dir(dir_prod, i)
        full = norm_bar + ratio_bar / norm[i]
        zetas[i + 1] = add(dir_row, resid_rows[i + 1], full)
        rho_row = add(add(rho_row, zetas[i + 1], one), resid_rows[i + 1], full)
        rho_prod = add(add(rho_prod, dir_prod, one), resid_prod(i + 1), 2 * full)
        rho_rows.append(rho_row)
        step_bar = along[i] - (rho_prod[i] - rho_prod[i + 1]) * inverse[i]
        curv_bar = -step_bar * step[i] / curv[i]
        oper = [None] * 8
        if i == 2:
            for k in range(5):
                if k < 4:
                    oper[k] = plus(oper[k], times(sigma, rho_row[k]))
                    oper[k + 1] = plus(oper[k + 1], rho_row[k])
                else:
                    oper[5] = plus(oper[5], rho_row[4])
            oper[7] = rho_row[6]
        kept = add(scaled(dir_row, ratio[i + 1]), target, step[i])
        kept = add(kept, image_rows[i], 2 * curv_bar)
        dir_row = add(kept, oper, -step[i])
        dir_prod = add(add(scaled(dir_prod, ratio[i + 1]), cot, step[i]), image_prod(i), 2 * curv_bar)
        dir_prod = add(dir_prod, operator_prod(rho_prod), -step[i])
        norm_bar = step_bar / curv[i] - ratio_bar * norm[i + 1] / (norm[i] * norm[i])
    zetas[0] = add(dir_row, resid_rows[0], norm_bar)
    answer = [None] * 8
    for i in range(ITERS):
        answer = add(answer, row(direc[i]), step[i])
    combos = [resid_rows[1], resid_rows[2], resid_rows[3], zetas[3], zetas[2], rho_rows[1], zetas[1], rho_rows[2], zetas[0], answer]
    return combos, [step[1], ratio[1], step[0]]


def vmem():
    return pl.BlockSpec(memory_space=pltpu.VMEM)


def hbm():
    return pl.BlockSpec(memory_space=pltpu.HBM)


def smem():
    return pl.BlockSpec(memory_space=pltpu.SMEM)


def shards(stiffness, precond, rhs_vec, cotangent, col_index, send_rows, counts):
    count = rhs_vec.shape[0]
    sub = lax.axis_index("sub")
    size = lax.axis_size("sub")
    edge = jnp.stack([sub > 0, sub + 1 < size]).astype(jnp.int32)
    columns = col_index.T
    stiff_cuts = stiffness.reshape(NBLK, K, CUTS, LANES).transpose(0, 2, 1, 3).reshape(NBLK * K * CUTS, LANES)
    weight_cuts = precond.reshape(NBLK // 8, 8, CUTS, LANES).transpose(0, 2, 1, 3).reshape(NBLK * CUTS, LANES)
    base = jnp.concatenate([rhs_vec, cotangent], axis=0).reshape(2 * count, NBLK, BS)
    base = jnp.pad(base, ((0, 0), (OFF, ROWS - HIGH), (0, LANES - BS)))

    def shape(*dims):
        return jax.ShapeDtypeStruct(dims, f32)

    def call(kernel, name, scalars_in, arrays_in, outs, scratch, expected, specs=None):
        return pl.pallas_call(
            kernel,
            in_specs=[smem()] * len(scalars_in) + [vmem()] * len(arrays_in),
            out_specs=specs or [vmem()] * len(outs),
            out_shape=outs,
            scratch_shapes=scratch,
            compiler_params=pltpu.CompilerParams(vmem_limit_bytes=8 * MIB),
            cost_estimate=pl.CostEstimate(flops=MIB, bytes_accessed=int(expected * 3.2e6), transcendentals=0),
            name=name,
        )(*scalars_in, *arrays_in)

    rows = shape(count, ROWS, LANES)
    message = shape(count, 16, LANES)
    longer = shape(count, 24, LANES)
    ghost_message = shape(IF, CUTS + 8, LANES)
    partial = lambda r: pltpu.VMEM((r, ROWS, 8, LANES), f32)
    turned = [pltpu.VMEM((count, BS, LANES), f32), pltpu.VMEM((LANES, LANES), f32)]
    held = lambda r: pltpu.VMEM((r, ROWS, LANES), f32)
    grams = pltpu.VMEM((2, BS, LANES), f32)

    up, down = call(pack_kernel, "pack", [send_rows], [weight_cuts, base], [ghost_message] * 2, [], 2)
    near, far = exchange(up, down)

    weights, ops, squares = call(
        operator_kernel, "operators", [], [weight_cuts],
        [shape(NBLK, BS, LANES), shape(NBLK, BS, LANES), shape(8, LANES)], [grams], 4,
    )
    blocks, halo_list, stats = call(
        blocks_kernel, "blocks", [columns], [stiff_cuts, squares],
        [shape(NBLK, K, BS, LANES), jax.ShapeDtypeStruct((1, NBLK * K + 8), jnp.int32), shape(16, LANES)],
        [], 5, [vmem(), smem(), vmem()],
    )
    stats, waiting = widening([stats], "sub", 0, 2)

    zero, a1, a2, up, down = call(
        first_kernel, "first", [columns, halo_list, send_rows, counts], [blocks, ops, base, near, far],
        [shape(2 * count, ROWS, LANES), rows, rows, longer, longer],
        [partial(count), held(count)], 6,
    )
    stats, a2 = lax.optimization_barrier((stats, a2))
    while waiting is not None:
        stats, waiting = widening(stats, "sub", waiting, 4)
    low, high = exchange(up, down)
    stats = jnp.stack(stats)

    gops, k0, k1 = call(
        ghost_kernel, "ghosts", [], [ops, zero, a1, near, far],
        [shape(2 * IF, BS, LANES), rows, rows], [grams, *turned], 3,
    )

    v1, v2, v3, v4, k3, dots, sigma, up, down = call(
        second_kernel, "second", [columns, halo_list, send_rows, edge],
        [blocks, ops, gops, zero, a1, a2, k0, k1, low, high, stats],
        [rows, rows, rows, rows, rows, shape(count, 12, 8, LANES), shape(8, LANES), message, message],
        [partial(count), *turned, held(count)], 7,
    )
    low, high = exchange(up, down)

    zero, v3 = lax.optimization_barrier((zero, v3))
    (b1,) = call(
        target_kernel, "target", [columns, halo_list], [blocks, ops, gops, zero], [rows],
        [partial(count), held(count)], 3,
    )

    v4, dots = call(
        moment_kernel, "moments", [send_rows, edge], [v4, k3, low, high, dots, b1], [rows, shape(8, LANES)], [], 0.8
    )
    sums = parts_over(dots, "sub", 8)

    (w5,) = call(
        third_kernel, "third", [columns, halo_list], [blocks, ops, gops, v4], [rows],
        [partial(count), held(count)], 4,
    )

    stored = [zero, v1, v2, v3, v4, w5, b1]
    first, fixed, rho, coefs, scales, up, down = call(
        fourth_kernel, "fourth", [columns, send_rows], [blocks, ops, sigma, *stored, *sums],
        [rows, rows, rows, shape(10, 8, 8, LANES), shape(3, 8, LANES), message, message], [partial(count)], 3,
    )
    (early,) = call(early_kernel, "early", [], [coefs, *stored], [shape(NBLK * EARLY, LANES)], [], 0.5)
    size = lax.axis_size("rhs")
    early = [early]
    if size == 4:
        early.append(lax.ppermute(early[0], "rhs", [(i, i ^ 2) for i in range(size)]))
    low, high = exchange(up, down)

    zeta, answer = call(
        answer_kernel, "answer", [], [ops, coefs, *stored],
        [shape(2, count, ROWS, LANES), rows], [held(count), *turned], 1.5,
    )
    early, low, high, zeta = lax.optimization_barrier((early, low, high, zeta))
    if size == 4:
        early = early + [lax.ppermute(part, "rhs", [(i, i ^ 1) for i in range(size)]) for part in early]
    else:
        early = all_of(early[0], "rhs")

    (late,) = call(
        fifth_kernel, "fifth", [columns, halo_list, send_rows, edge],
        [blocks, ops, gops, rho, fixed, zeta, scales, low, high],
        [shape(NBLK * LATE, LANES)], [partial(count), held(count), held(count)], 4,
    )
    if size == 4:
        late = [late] + [lax.ppermute(late, "rhs", [(i, i ^ d) for i in range(size)]) for d in (2, 1, 3)]
    else:
        late = all_of(late, "rhs")

    (mixed,) = call(mixed_kernel, "mixed", [], early, [shape(NBLK, LANES, LANES)], [], 3)
    (grad,) = call(grad_kernel, "grad", [], [*early, *late, mixed, weights], [shape(NBLK * CUTS, LANES)], [], 10)
    grad = grad.reshape(NBLK // 8, CUTS, 8, LANES).transpose(0, 2, 1, 3).reshape(NBLK, BS * BS)
    return answer[:, OFF:HIGH, :BS].reshape(count, NBLK * BS), grad


def solution(mesh):
    in_specs = (
        P("sub", None, None),
        P("sub", None),
        P("rhs", "sub"),
        P("rhs", "sub"),
        P("sub", None),
        P("sub", None),
        P("sub"),
    )
    out_specs = (P("rhs", "sub"), P("sub", None))
    return jax.shard_map(shards, mesh=mesh, in_specs=in_specs, out_specs=out_specs, check_vma=False)
```

```python
import functools

import jax
import jax.numpy as jnp
from jax import lax
from jax.experimental import pallas as pl
from jax.experimental.pallas import tpu as pltpu
from jax.sharding import PartitionSpec as P

BS = 96
K = 4
NBLK = 48
IF = 6
ITERS = 4
ALL = (0, 1, 2, 3, 4, 5, 6, 7)
USED = ((0, 1), (0, 1, 2), (0, 1, 2, 3), (0, 1, 2, 3, 4, 6), ALL, ALL, ALL, ALL, ALL, (0, 1, 2, 3))
EARLY = 16
LATE = 4
CUTS = BS * BS // 128
PITCH = CUTS + 1
LANES = 128
OFF = 8
ROWS = 64
LOW = OFF - IF
HIGH = OFF + NBLK
CHUNK = 8
MIB = 1024 * 1024

highest = lax.Precision.HIGHEST
f32 = jnp.float32


def own(value):
    return value[:, OFF:HIGH]


def lane_ids():
    return lax.broadcasted_iota(jnp.int32, (BS, LANES), 1)


def diagonal():
    pos = lax.broadcasted_iota(jnp.int32, (BS, LANES), 0)
    row = (pos & ~31) + 4 * (pos & 7) + ((pos >> 3) & 3)
    return row == lane_ids()


def fold(prod):
    return jnp.sum(prod.reshape(BS // 8, 8, prod.shape[-1]), axis=0)


def unflatten(read):
    lane = lax.broadcasted_iota(jnp.int32, (8, LANES), 1)
    out = []
    for h in range(BS // 32):
        one, two, three = (read(24 * h + m) for m in range(3))
        out.append(jnp.where(lane < BS, one, 0.0))
        mixed = jnp.where(lane < 32, pltpu.roll(one, 32, 1), pltpu.roll(two, 32, 1))
        out.append(jnp.where(lane < BS, mixed, 0.0))
        mixed = jnp.where(lane < 64, pltpu.roll(two, 64, 1), pltpu.roll(three, 64, 1))
        out.append(jnp.where(lane < BS, mixed, 0.0))
        out.append(jnp.where(lane < BS, pltpu.roll(three, 96, 1), 0.0))
    return jnp.concatenate(out, axis=0)


def flatten(block, write):
    lane = lax.broadcasted_iota(jnp.int32, (8, LANES), 1)
    for h in range(BS // 32):
        one, two, three, four = (block[32 * h + 8 * j : 32 * h + 8 * j + 8] for j in range(4))
        two = pltpu.roll(two, 96, 1)
        three = pltpu.roll(three, 64, 1)
        write(24 * h, jnp.where(lane < BS, one, two))
        write(24 * h + 1, jnp.where(lane < 64, two, three))
        write(24 * h + 2, jnp.where(lane < 32, three, pltpu.roll(four, 32, 1)))


def make_operator(weights, gram_ref):
    gram = lax.dot_general(
        weights, weights, (((0,), (0,)), ((), ())), precision=highest, preferred_element_type=f32
    )
    gram_ref[...] = gram[:BS]
    rows = [gram_ref[pl.ds(32 * h + j, 8, stride=4), :] for h in range(BS // 32) for j in range(4)]
    return jnp.concatenate(rows, axis=0) + jnp.where(diagonal(), 1.0, 0.0)


def scatter_apply(blocks, op_ref, x_ref, y_ref, col_ref, column_ref):
    count = x_ref.shape[0]
    y_ref[...] = jnp.zeros_like(y_ref)

    def step(group, carry):
        base = pl.multiple_of(group * CHUNK, CHUNK)
        tiles = [x_ref[r, pl.ds(base + OFF, CHUNK), :] for r in range(count)]
        for i in range(CHUNK):
            n = group * CHUNK + i
            oper = op_ref[n]
            images = [jnp.sum(oper * tiles[r][i : i + 1, :], axis=1, keepdims=True) for r in range(count)]
            if column_ref is not None:
                for r in range(count):
                    column_ref[r] = jnp.where(lane_ids() == n + OFF, images[r], column_ref[r])
            for k in range(K):
                block = blocks[n, k]
                slot = col_ref[k, n] + LOW
                for r in range(count):
                    y_ref[r, slot] = y_ref[r, slot] + fold(block * images[r])
        return carry

    lax.fori_loop(0, NBLK // CHUNK, step, 0)


def ghost_images(op_ref, x_ref, g_ref):
    count = x_ref.shape[0]
    mask = diagonal()
    g_ref[...] = jnp.zeros_like(g_ref)
    for first, side in ((LOW, 0), (HIGH, IF)):
        for j in range(IF):
            slot = first + j
            oper = op_ref[side + j]
            for r in range(count):
                image = jnp.sum(oper * x_ref[r, slot : slot + 1, :], axis=1, keepdims=True)
                line = jnp.sum(fold(jnp.where(mask, image, 0.0)), axis=0, keepdims=True)
                g_ref[r, slot : slot + 1, :] = line


def ghost_apply(blocks, g_ref, y_ref, col_ref, list_ref):
    count = g_ref.shape[0]
    mask = diagonal()

    def step(item, carry):
        for u in range(4):
            entry = list_ref[0, 1 + item * 4 + u]
            n = entry >> 2
            k = entry & 3
            slot = col_ref[k, n] + LOW
            block = blocks[n, k]
            for r in range(count):
                image = jnp.sum(block * g_ref[r, pl.ds(slot, 1), :], axis=1, keepdims=True)
                y_ref[r, n + OFF] = y_ref[r, n + OFF] + fold(jnp.where(mask, image, 0.0))
        return carry

    lax.fori_loop(0, (list_ref[0, 0] + 3) >> 2, step, 0)


def pack(y_ref, r):
    sub = lax.broadcasted_iota(jnp.int32, (8, LANES), 0)
    groups = []
    for g in range(ROWS // 8):
        total = jnp.zeros((8, LANES), f32)
        for i in range(8):
            line = jnp.sum(y_ref[r, g * 8 + i], axis=0, keepdims=True)
            total = jnp.where(sub == i, line, total)
        groups.append(total)
    return jnp.concatenate(groups, axis=0)


def unpack_columns(column_ref, square_ref, r):
    for h in range(BS // 32):
        for j in range(4):
            start = 32 * h + 8 * j
            square_ref[pl.ds(32 * h + j, 8, stride=4), :] = column_ref[r, start : start + 8, :]
    square_ref[BS:, :] = jnp.zeros((LANES - BS, LANES), f32)
    return square_ref[...].T[:ROWS]


def messages(up_ref, down_ref, v_ref, send_ref, extra_ref=None):
    for r in range(v_ref.shape[0]):
        for j in range(IF):
            low = pl.ds(send_ref[0, j] + OFF, 1)
            high = pl.ds(send_ref[0, IF + j] + OFF, 1)
            down_ref[r, j : j + 1, :] = v_ref[r, low, :]
            up_ref[r, j : j + 1, :] = v_ref[r, high, :]
            down_ref[r, 8 + j : 9 + j, :] = v_ref[r, LOW + j : LOW + j + 1, :]
            up_ref[r, 8 + j : 9 + j, :] = v_ref[r, HIGH + j : HIGH + j + 1, :]
            if extra_ref is not None:
                down_ref[r, 16 + j : 17 + j, :] = extra_ref[r, low, :]
                up_ref[r, 16 + j : 17 + j, :] = extra_ref[r, high, :]


def complete(v_ref, low_ref, high_ref, send_ref, edge_ref):
    for r in range(v_ref.shape[0]):
        for j in range(IF):
            for part, base, ghost, flag in ((low_ref, 0, LOW, 0), (high_ref, IF, HIGH, 1)):
                at = pl.ds(send_ref[0, base + j] + OFF, 1)
                v_ref[r, at, :] = v_ref[r, at, :] + part[r, 8 + j : 9 + j, :]
                slot = ghost + j
                summed = v_ref[r, slot : slot + 1, :] + part[r, j : j + 1, :]
                v_ref[r, slot : slot + 1, :] = jnp.where(edge_ref[flag] > 0, summed, 0.0)


def tile_sum(first, second):
    prod = first * second
    return jnp.sum(prod.reshape(prod.shape[0] // 8, 8, LANES), axis=0)


def whole_sum(tile):
    return jnp.sum(jnp.sum(tile, axis=0, keepdims=True), axis=1, keepdims=True)


def inner_rows():
    row = lax.broadcasted_iota(jnp.int32, (ROWS, LANES), 0)
    return (row >= OFF) & (row < HIGH)


def pack_kernel(send_ref, raw_ref, stiff_ref, base_ref, up_ref, down_ref):
    vectors = base_ref.shape[0]
    flat = lax.broadcasted_iota(jnp.int32, (CUTS, LANES), 0) * LANES
    flat = (flat + lax.broadcasted_iota(jnp.int32, (CUTS, LANES), 1)).astype(f32)
    step = float(BS + 1)
    mask = jnp.where(flat - step * jnp.floor((flat + 0.5) * (1.0 / step)) == 0.0, 1.0, 0.0)

    def gather(group, carry):
        squares, traces = carry
        for i in range(CUTS):
            tile = raw_ref[pl.ds(pl.multiple_of(group * (8 * CUTS) + 8 * i, 8), 8), :]
            squares = squares + tile * tile
        for i in range(0, CHUNK, 2):
            start = (group * CHUNK + i) * (CUTS * K)
            for q in range(0, CUTS, 8):
                traces = traces + mask[q : q + 8] * stiff_ref[pl.ds(start + K * q, 8, stride=K), :]
        return squares, traces

    blank = jnp.zeros((8, LANES), f32)
    squares, traces = lax.fori_loop(0, NBLK // CHUNK, gather, (blank, blank))
    squares = jnp.sum(squares, axis=0, keepdims=True)
    traces = 2.0 * jnp.sum(traces, axis=0, keepdims=True)
    for part, ref in ((0, down_ref), (IF, up_ref)):
        for j in range(IF):
            n = send_ref[0, part + j]
            start = (n >> 3) * (8 * CUTS) + (n & 7)
            for i in range(CUTS // 8):
                ref[j, 8 * i : 8 * i + 8, :] = raw_ref[pl.ds(start + 64 * i, 8, stride=8), :]
            ref[j, CUTS:, :] = jnp.zeros((8, LANES), f32)
            weights = unflatten(lambda q: raw_ref[pl.ds(start + 8 * q, 8, stride=24), :])
            for r in range(vectors):
                line = base_ref[r, pl.ds(n + OFF, 1), :]
                ref[j, CUTS + r : CUTS + r + 1, :] = line
                if r < vectors // 2:
                    inside = jnp.sum(weights * line, axis=1, keepdims=True)
                    image = line + jnp.sum(fold(weights * inside), axis=0, keepdims=True)
                    at = CUTS + vectors + r
                    ref[j, at : at + 1, :] = image
        ref[0, CUTS + 6 : CUTS + 7, :] = squares
        ref[0, CUTS + 7 : CUTS + 8, :] = traces


def operator_kernel(raw_ref, weights_ref, ops_ref, gram_ref, turn_ref):
    def step(group, carry):
        for q in range(CUTS):
            tile = raw_ref[pl.ds(pl.multiple_of(group * (8 * CUTS) + 8 * q, 8), 8), :]
            turn_ref[pl.ds(q, 8, stride=PITCH), :] = tile
        for i in range(CHUNK):
            n = group * CHUNK + i
            weights = unflatten(lambda q: turn_ref[pl.ds(PITCH * i + q, 8, stride=3), :])
            weights_ref[n] = weights
            ops_ref[n] = make_operator(weights, gram_ref.at[i & 1])
        return carry

    lax.fori_loop(0, NBLK // CHUNK, step, 0)


def blocks_kernel(col_ref, stiff_ref, blocks_ref, list_ref):
    def step(group, count):
        for i in range(CHUNK):
            n = group * CHUNK + i
            for k in range(K):
                blocks_ref[n, k] = unflatten(lambda q: stiff_ref[pl.ds(n * (CUTS * K) + 4 * q + k, 8, stride=12), :])
                col = col_ref[k, n]
                list_ref[0, 1 + count] = n * K + k
                count = count + jnp.where((col < IF) | (col >= IF + NBLK), 1, 0)
        return count

    count = lax.fori_loop(0, NBLK // CHUNK, step, jnp.int32(0))
    list_ref[0, 0] = count
    for u in range(4):
        list_ref[0, 1 + count + u] = 0


def first_kernel(
    col_ref, list_ref, send_ref, count_ref,
    blocks, op_ref, base_ref, low_ref, high_ref,
    zero_ref, a1_ref, a2_ref, up_ref, down_ref,
    y_ref, g_ref,
):
    count = a1_ref.shape[0]
    zero_ref[...] = base_ref[...]
    g_ref[...] = jnp.zeros_like(g_ref)
    row = lax.broadcasted_iota(jnp.int32, (ROWS, LANES), 0)
    dead = (row >= count_ref[0] + OFF) & (row < HIGH)
    for r in range(count):
        zero_ref[r] = jnp.where(dead, 0.0, zero_ref[r])
        for part, first in ((low_ref, LOW), (high_ref, HIGH)):
            for j in range(IF):
                at = slice(first + j, first + j + 1)
                for s in (r, count + r):
                    zero_ref[s, at, :] = part[j, CUTS + s : CUTS + s + 1, :]
                g_ref[r, at, :] = part[j, CUTS + 2 * count + r : CUTS + 2 * count + r + 1, :]
    scatter_apply(blocks, op_ref, zero_ref.at[pl.ds(0, count)], y_ref, col_ref, None)
    ghost_apply(blocks, g_ref, y_ref, col_ref, list_ref)
    inner = inner_rows()
    for r in range(count):
        a1_ref[r] = jnp.where(inner, pack(y_ref, r), 0.0)
    scatter_apply(blocks, op_ref, a1_ref, y_ref, col_ref, None)
    for r in range(count):
        a2_ref[r] = pack(y_ref, r)
    messages(up_ref, down_ref, a2_ref, send_ref, a1_ref)


def operator_rows(op_ref, x_ref, out_ref, column_ref, square_ref):
    column_ref[...] = jnp.zeros_like(column_ref)
    lanes = lane_ids()
    for r in range(column_ref.shape[0]):
        for n in range(NBLK):
            image = jnp.sum(op_ref[n] * x_ref[r, n + OFF : n + OFF + 1, :], axis=1, keepdims=True)
            column_ref[r] = jnp.where(lanes == n + OFF, image, column_ref[r])
        out_ref[r] = unpack_columns(column_ref, square_ref, r)


def ghost_kernel(op_ref, zero_ref, a1_ref, low_ref, high_ref, gop_ref, k0_ref, k1_ref, gram_ref, column_ref, square_ref):
    for part, first in ((low_ref, 0), (high_ref, IF)):
        for j in range(IF):
            weights = unflatten(lambda q: part[j, pl.ds(q, 8, stride=3), :])
            gop_ref[first + j] = make_operator(weights, gram_ref.at[j & 1])
    operator_rows(op_ref, zero_ref, k0_ref, column_ref, square_ref)
    operator_rows(op_ref, a1_ref, k1_ref, column_ref, square_ref)


def target_kernel(col_ref, list_ref, blocks, op_ref, gop_ref, zero_ref, b1_ref, y_ref, g_ref):
    count = b1_ref.shape[0]
    target = zero_ref.at[pl.ds(count, count)]
    scatter_apply(blocks, op_ref, target, y_ref, col_ref, None)
    ghost_images(gop_ref, target, g_ref)
    ghost_apply(blocks, g_ref, y_ref, col_ref, list_ref)
    inner = inner_rows()
    for r in range(count):
        b1_ref[r] = jnp.where(inner, pack(y_ref, r), 0.0)


def second_kernel(
    col_ref, list_ref, send_ref, edge_ref,
    blocks, ops_ref, gop_ref, zero_ref, a1_ref, a2_in, k0_ref, k1_ref, low_ref, high_ref, stats_ref,
    v1_ref, v2_ref, v3_ref, v4_ref, k3_ref, dots_ref, sigma_ref, up_ref, down_ref,
    y_ref, column_ref, square_ref, g_ref,
):
    count = a1_ref.shape[0]
    inner = inner_rows()
    squares, traces = stats_ref[0, :1], stats_ref[0, 1:]
    for s in range(1, stats_ref.shape[0]):
        squares = squares + stats_ref[s, :1]
        traces = traces + stats_ref[s, 1:]
    scale = 1.0 / (lax.axis_size("sub") * NBLK * BS)
    sigma = (1.0 + scale * whole_sum(squares)) * (scale * whole_sum(traces))
    sigma_ref[...] = jnp.broadcast_to(sigma, sigma_ref.shape)
    column_ref[...] = jnp.zeros_like(column_ref)
    v2_ref[...] = a2_in[...]
    complete(v2_ref, low_ref, high_ref, send_ref, edge_ref)
    for r in range(count):
        v1_ref[r] = a1_ref[r]
        for part, ghost, flag in ((low_ref, LOW, 0), (high_ref, HIGH, 1)):
            for j in range(IF):
                v1_ref[r, ghost + j : ghost + j + 1, :] = part[r, 16 + j : 17 + j, :]
        v1 = v1_ref[r] - sigma * zero_ref[r]
        v2_ref[r] = v2_ref[r] - sigma * v1_ref[r] - sigma * v1
        v1 = jnp.where(inner, v1, 0.0)
        v1_ref[r] = v1
        v0 = jnp.where(inner, zero_ref[r], 0.0)
        target = jnp.where(inner, zero_ref[count + r], 0.0)
        second = k1_ref[r] - sigma * k0_ref[r]
        dots_ref[r, 0] = tile_sum(v0, k0_ref[r])
        dots_ref[r, 1] = tile_sum(v1, k0_ref[r])
        dots_ref[r, 2] = tile_sum(v1, second)
        dots_ref[r, 8] = tile_sum(target, k0_ref[r])
        dots_ref[r, 9] = tile_sum(target, second)
    scatter_apply(blocks, ops_ref, v2_ref, y_ref, col_ref, column_ref)
    ghost_images(gop_ref, v2_ref, g_ref)
    ghost_apply(blocks, g_ref, y_ref, col_ref, list_ref)
    for r in range(count):
        image = unpack_columns(column_ref, square_ref, r)
        v3 = jnp.where(inner, pack(y_ref, r) - sigma * v2_ref[r], 0.0)
        v3_ref[r] = v3
        dots_ref[r, 3] = tile_sum(v1_ref[r], image)
        dots_ref[r, 4] = tile_sum(jnp.where(inner, v2_ref[r], 0.0), image)
        dots_ref[r, 5] = tile_sum(v3, image)
        dots_ref[r, 10] = tile_sum(jnp.where(inner, zero_ref[count + r], 0.0), image)
    scatter_apply(blocks, ops_ref, v3_ref, y_ref, col_ref, column_ref)
    for r in range(count):
        image = unpack_columns(column_ref, square_ref, r)
        dots_ref[r, 6] = tile_sum(v3_ref[r], image)
        dots_ref[r, 7] = jnp.zeros((8, LANES), f32)
        dots_ref[r, 11] = tile_sum(jnp.where(inner, zero_ref[count + r], 0.0), image)
        k3_ref[r] = image
        v4_ref[r] = pack(y_ref, r) - sigma * v3_ref[r]
    messages(up_ref, down_ref, v4_ref, send_ref)


def moment_kernel(send_ref, edge_ref, v4_in, k3_ref, low_ref, high_ref, dots_in, v4_ref, dots_ref):
    v4_ref[...] = v4_in[...]
    complete(v4_ref, low_ref, high_ref, send_ref, edge_ref)
    lane = lax.broadcasted_iota(jnp.int32, (8, LANES), 1)
    sub = lax.broadcasted_iota(jnp.int32, (8, LANES), 0)
    total = jnp.zeros((8, LANES), f32)
    for r in range(v4_ref.shape[0]):
        for d in range(12):
            part = tile_sum(v4_ref[r], k3_ref[r]) if d == 7 else dots_in[r, d]
            total = jnp.where((lane == d) & (sub == r), whole_sum(part), total)
    dots_ref[...] = total


def third_kernel(col_ref, list_ref, blocks, ops_ref, gop_ref, v4_ref, w5_ref, y_ref, g_ref):
    scatter_apply(blocks, ops_ref, v4_ref, y_ref, col_ref, None)
    ghost_images(gop_ref, v4_ref, g_ref)
    ghost_apply(blocks, g_ref, y_ref, col_ref, list_ref)
    for r in range(v4_ref.shape[0]):
        w5_ref[r] = pack(y_ref, r)


def combine(coef_ref, parts, g, r):
    total = None
    for s in USED[g]:
        term = coef_ref[g, s, r : r + 1, :] * parts[s]
        total = term if total is None else total + term
    return total


def sources(zero_ref, stored, r, count):
    v1_ref, v2_ref, v3_ref, v4_ref, w5_ref, b1_ref = stored
    parts = [zero_ref[r], v1_ref[r], v2_ref[r], v3_ref[r], v4_ref[r], w5_ref[r], zero_ref[count + r], b1_ref[r]]
    inner = inner_rows()
    return [jnp.where(inner, part, 0.0) for part in parts]


def fourth_kernel(col_ref, send_ref, blocks, ops_ref, sigma_ref, zero_ref, *refs):
    stored, sums = refs[:6], [part[...] for part in refs[6:-8]]
    first_ref, base_ref, rho_ref, coef_ref, scale_ref, up_ref, down_ref, y_ref = refs[-8:]
    while len(sums) > 1:
        sums = [sums[i] + sums[i + 1] for i in range(0, len(sums), 2)]
    sums = sums[0]
    column = lambda d: jnp.broadcast_to(sums[:, d : d + 1], (8, LANES))
    combos, scales = scalars([column(d) for d in range(8)], [column(8 + d) for d in range(4)], sigma_ref[...])
    for g, value in enumerate(scales):
        scale_ref[g] = value
    for g, combo in enumerate(combos):
        for s, value in enumerate(combo):
            if s in USED[g]:
                coef_ref[g, s] = value
    count = rho_ref.shape[0]
    for r in range(count):
        parts = sources(zero_ref, stored, r, count)
        first_ref[r] = combine(coef_ref, parts, 5, r)
        base_ref[r] = combine(coef_ref, parts, 7, r)
    scatter_apply(blocks, ops_ref, first_ref, y_ref, col_ref, None)
    for r in range(count):
        rho_ref[r] = base_ref[r] - scale_ref[0, r : r + 1, :] * pack(y_ref, r)
    messages(up_ref, down_ref, rho_ref, send_ref)


def early_kernel(coef_ref, zero_ref, *refs):
    stored, early_ref = refs[:6], refs[6]
    count = zero_ref.shape[0] // 2
    for r in range(count):
        parts = sources(zero_ref, stored, r, count)
        early_ref[pl.ds(r, NBLK, stride=EARLY), :] = parts[0][OFF:HIGH]
        for g, slot in ((0, 2), (1, 4), (2, 6), (4, 12), (3, 14)):
            early_ref[pl.ds(slot + r, NBLK, stride=EARLY), :] = combine(coef_ref, parts, g, r)[OFF:HIGH]
        for slot in (8, 10):
            early_ref[pl.ds(slot + r, NBLK, stride=EARLY), :] = jnp.zeros((NBLK, LANES), f32)


def answer_kernel(ops_ref, coef_ref, zero_ref, *refs):
    stored, (zeta_ref, sol_ref, x_ref, column_ref, square_ref) = refs[:6], refs[6:]
    count = zeta_ref.shape[1]
    for r in range(count):
        parts = sources(zero_ref, stored, r, count)
        zeta_ref[0, r] = combine(coef_ref, parts, 8, r)
        zeta_ref[1, r] = combine(coef_ref, parts, 6, r)
        x_ref[r] = combine(coef_ref, parts, 9, r)
    operator_rows(ops_ref, x_ref, sol_ref, column_ref, square_ref)


def fifth_kernel(
    col_ref, list_ref, send_ref, edge_ref,
    blocks, ops_ref, gop_ref, rho_in, base_ref, zeta_ref, scale_ref, low_ref, high_ref,
    late_ref, y_ref, rho_ref, g_ref,
):
    count = rho_in.shape[0]
    rho_ref[...] = rho_in[...]
    complete(rho_ref, low_ref, high_ref, send_ref, edge_ref)
    scatter_apply(blocks, ops_ref, rho_ref, y_ref, col_ref, None)
    ghost_images(gop_ref, rho_ref, g_ref)
    ghost_apply(blocks, g_ref, y_ref, col_ref, list_ref)
    for r in range(count):
        change = rho_ref[r] - base_ref[r]
        first = zeta_ref[0, r] + scale_ref[1, r : r + 1, :] * change - scale_ref[2, r : r + 1, :] * pack(y_ref, r)
        second = zeta_ref[1, r] + change
        late_ref[pl.ds(r, NBLK, stride=LATE), :] = first[OFF:HIGH]
        late_ref[pl.ds(2 + r, NBLK, stride=LATE), :] = second[OFF:HIGH]


def split(value):
    high = value.astype(jnp.bfloat16)
    return high, (value - high.astype(f32)).astype(jnp.bfloat16)


def product(first, second, dim):
    (fh, fl), (sh, sl) = split(first), split(second)
    left = jnp.concatenate([fh, fl, fh], axis=dim)
    right = jnp.concatenate([sh, sh, sl], axis=0)
    return lax.dot_general(left, right, (((dim,), (0,)), ((), ())), preferred_element_type=f32)


def mixed_kernel(*refs):
    early, mixed_ref = refs[:-1], refs[-1]

    def step(group, carry):
        for i in range(CHUNK):
            at = pl.multiple_of((group * CHUNK + i) * EARLY, EARLY)
            resid = [ref[pl.ds(at, 8), :] for ref in early]
            zeta = [ref[pl.ds(at + 8, 8), :] for ref in early]
            left = jnp.concatenate(resid + zeta, axis=0)
            right = jnp.concatenate(zeta + resid, axis=0)
            mixed_ref[group * CHUNK + i] = product(left, right, 0)
        return carry

    lax.fori_loop(0, NBLK // CHUNK, step, 0)


def grad_kernel(*refs):
    peers = (len(refs) - 4) // 2
    early, late, mixed_ref, weights_ref, grad_ref, turn_ref = refs[:peers], refs[peers : 2 * peers], *refs[-4:]
    group = pl.program_id(0)
    upper = lax.broadcasted_iota(jnp.int32, (8, LANES), 0) < LATE

    def join(tiles):
        out = []
        for q in range(0, len(tiles), 2):
            other = pltpu.roll(tiles[q + 1], LATE, 0) if q + 1 < len(tiles) else jnp.zeros((8, LANES), f32)
            out.append(jnp.where(upper, tiles[q], other))
        return out

    for i in range(CHUNK):
        n = group * CHUNK + i
        at = pl.multiple_of(n * EARLY, EARLY)
        pair = pl.ds(pl.multiple_of(group * (CHUNK * LATE) + 8 * (i // 2), 8), 8)
        resid = join([ref[pl.ds(at, 8), :] for ref in early])
        zeta = [ref[pair, :] for ref in late]
        zeta = join([pltpu.roll(tile, LATE, 0) for tile in zeta] if i % 2 else zeta)
        left = jnp.concatenate(resid + zeta, axis=0)
        right = jnp.concatenate(zeta + resid, axis=0)
        grad = product(weights_ref[n], mixed_ref[n] + product(left, right, 0), 1)

        def write(q, value):
            turn_ref[pl.ds(PITCH * i + q, 8, stride=3), :] = value

        flatten(grad, write)
    for q in range(CUTS):
        grad_ref[8 * q : 8 * q + 8, :] = turn_ref[pl.ds(q, 8, stride=PITCH), :]


def widening(parts, axis, step, most):
    if step is None:
        return parts, None
    size = lax.axis_size(axis)
    if size & (size - 1):
        return [lax.psum(parts[0], axis)], None
    step = step or 1
    while len(parts) > 1:
        parts = [parts[i] + parts[i + 1] for i in range(0, len(parts), 2)]
    width = min(most, size // step)
    total = parts[0]
    parts = [total] + [lax.ppermute(total, axis, [(i, i ^ (d * step)) for i in range(size)]) for d in range(1, width)]
    step *= width
    return parts, step if step < size else None


def all_of(values, axis):
    size = lax.axis_size(axis)
    return [values] + [
        lax.ppermute(values, axis, [(i, (i + d) % size) for i in range(size)]) for d in range(1, size)
    ]


def exchange(up, down):
    size = lax.axis_size("sub")
    rising = [(i, i + 1) for i in range(size - 1)]
    falling = [(j, i) for i, j in rising]
    return lax.ppermute(up, "sub", rising), lax.ppermute(down, "sub", falling)


def plus(first, second):
    if first is None:
        return second
    return first if second is None else first + second


def times(first, second):
    return None if first is None or second is None else first * second


def add(first, second, scale):
    size = max(len(first), len(second))
    first = list(first) + [None] * (size - len(first))
    second = list(second) + [None] * (size - len(second))
    return [plus(a, times(scale, b)) for a, b in zip(first, second)]


def scaled(first, scale):
    return [times(scale, a) for a in first]


def scalars(moments, products, sigma):
    one = jnp.ones_like(sigma)

    def inner(first, second):
        weights = [None] * (len(first) + len(second) - 1)
        for i, a in enumerate(first):
            for j, b in enumerate(second):
                weights[i + j] = plus(weights[i + j], a * b)
        total = None
        for weight, moment in zip(weights, moments):
            total = plus(total, weight * moment)
        return total

    def apply(poly):
        out = [None] * (len(poly) + 1)
        for j, value in enumerate(poly):
            out[j] = plus(out[j], sigma * value)
            out[j + 1] = plus(out[j + 1], value)
        return out

    resid = [[one]]
    direc = [[one]]
    image = []
    step, ratio, norm, curv = [], [None], [moments[0]], []
    for i in range(ITERS):
        image.append(apply(direc[i]))
        curv.append(inner(direc[i], image[i]))
        step.append(norm[i] / curv[i])
        if i + 1 < ITERS:
            resid.append(add(resid[i], image[i], -step[i]))
            norm.append(inner(resid[i + 1], resid[i + 1]))
            ratio.append(norm[i + 1] / norm[i])
            direc.append(add(resid[i + 1], direc[i], ratio[i + 1]))
    cot = []
    for i in range(ITERS):
        total = None
        for j, value in enumerate(resid[i]):
            total = plus(total, value * products[j])
        cot.append(total)
    along = [cot[0]]
    for i in range(1, ITERS):
        along.append(cot[i] + ratio[i] * along[i - 1])

    def row(poly):
        return list(poly) + [None] * (8 - len(poly))

    target = [None] * 6 + [one, None]
    resid_rows = [row(poly) for poly in resid]
    image_rows = [row(poly) for poly in image]
    inverse = [1.0 / value for value in step]

    def resid_prod(i):
        return [norm[l] if l == i else None for l in range(ITERS)]

    def image_prod(i):
        out = [None] * ITERS
        out[i] = norm[i] * inverse[i]
        if i + 1 < ITERS:
            out[i + 1] = -norm[i + 1] * inverse[i]
        return out

    def along_dir(prod, i):
        total = prod[0]
        for l in range(1, i + 1):
            total = plus(prod[l], times(ratio[l], total))
        return total

    def operator_prod(prod):
        out = []
        for l in range(ITERS - 1):
            value = times(add([prod[l]], [prod[l + 1]], -one)[0], inverse[l])
            if l > 0:
                back = times(add([prod[l - 1]], [prod[l]], -one)[0], inverse[l - 1])
                value = add([value], [back], -ratio[l])[0]
            out.append(value)
        return out + [None]

    last = ITERS - 1
    step_bar = along[last]
    curv_bar = -step_bar * step[last] / curv[last]
    dir_row = add(scaled(target, step[last]), image_rows[last], 2 * curv_bar)
    dir_prod = add(scaled(cot, step[last]), image_prod(last), 2 * curv_bar)
    norm_bar = step_bar / curv[last]
    rho_row = [None] * 8
    rho_prod = [None] * ITERS
    zetas = [None] * ITERS
    rho_rows = []
    for i in (2, 1, 0):
        ratio_bar = along_dir(dir_prod, i)
        full = norm_bar + ratio_bar / norm[i]
        zetas[i + 1] = add(dir_row, resid_rows[i + 1], full)
        rho_row = add(add(rho_row, zetas[i + 1], one), resid_rows[i + 1], full)
        rho_prod = add(add(rho_prod, dir_prod, one), resid_prod(i + 1), 2 * full)
        rho_rows.append(rho_row)
        step_bar = along[i] - (rho_prod[i] - rho_prod[i + 1]) * inverse[i]
        curv_bar = -step_bar * step[i] / curv[i]
        oper = [None] * 8
        if i == 2:
            for k in range(5):
                if k < 4:
                    oper[k] = plus(oper[k], times(sigma, rho_row[k]))
                    oper[k + 1] = plus(oper[k + 1], rho_row[k])
                else:
                    oper[5] = plus(oper[5], rho_row[4])
            oper[7] = rho_row[6]
        kept = add(scaled(dir_row, ratio[i + 1]), target, step[i])
        kept = add(kept, image_rows[i], 2 * curv_bar)
        dir_row = add(kept, oper, -step[i])
        dir_prod = add(add(scaled(dir_prod, ratio[i + 1]), cot, step[i]), image_prod(i), 2 * curv_bar)
        dir_prod = add(dir_prod, operator_prod(rho_prod), -step[i])
        norm_bar = step_bar / curv[i] - ratio_bar * norm[i + 1] / (norm[i] * norm[i])
    zetas[0] = add(dir_row, resid_rows[0], norm_bar)
    answer = [None] * 8
    for i in range(ITERS):
        answer = add(answer, row(direc[i]), step[i])
    combos = [resid_rows[1], resid_rows[2], resid_rows[3], zetas[3], zetas[2], rho_rows[1], zetas[1], rho_rows[2], zetas[0], answer]
    return combos, [step[1], ratio[1], step[0]]


def vmem():
    return pl.BlockSpec(memory_space=pltpu.VMEM)


def hbm():
    return pl.BlockSpec(memory_space=pltpu.HBM)


def smem():
    return pl.BlockSpec(memory_space=pltpu.SMEM)


def shards(stiffness, precond, rhs_vec, cotangent, col_index, send_rows, counts):
    count = rhs_vec.shape[0]
    sub = lax.axis_index("sub")
    size = lax.axis_size("sub")
    edge = jnp.stack([sub > 0, sub + 1 < size]).astype(jnp.int32)
    columns = col_index.T
    stiff_cuts = stiffness.reshape(NBLK, K, CUTS, LANES).transpose(0, 2, 1, 3).reshape(NBLK * K * CUTS, LANES)
    weight_cuts = precond.reshape(NBLK // 8, 8, CUTS, LANES).transpose(0, 2, 1, 3).reshape(NBLK * CUTS, LANES)
    base = jnp.concatenate([rhs_vec, cotangent], axis=0).reshape(2 * count, NBLK, BS)
    base = jnp.pad(base, ((0, 0), (OFF, ROWS - HIGH), (0, LANES - BS)))

    def shape(*dims):
        return jax.ShapeDtypeStruct(dims, f32)

    def call(kernel, name, scalars_in, arrays_in, outs, scratch, expected, specs=None, grid=()):
        return pl.pallas_call(
            kernel,
            grid=grid,
            in_specs=[smem()] * len(scalars_in) + [vmem()] * len(arrays_in),
            out_specs=specs or [vmem()] * len(outs),
            out_shape=outs,
            scratch_shapes=scratch,
            compiler_params=pltpu.CompilerParams(vmem_limit_bytes=8 * MIB),
            cost_estimate=pl.CostEstimate(flops=MIB, bytes_accessed=int(expected * 3.2e6), transcendentals=0),
            name=name,
        )(*scalars_in, *arrays_in)

    rows = shape(count, ROWS, LANES)
    message = shape(count, 16, LANES)
    longer = shape(count, 24, LANES)
    ghost_message = shape(IF, CUTS + 8, LANES)
    partial = lambda r: pltpu.VMEM((r, ROWS, 8, LANES), f32)
    turned = [pltpu.VMEM((count, BS, LANES), f32), pltpu.VMEM((LANES, LANES), f32)]
    held = lambda r: pltpu.VMEM((r, ROWS, LANES), f32)
    grams = pltpu.VMEM((2, BS, LANES), f32)
    turn = pltpu.VMEM((8 * PITCH, LANES), f32)

    up, down = call(
        pack_kernel, "pack", [send_rows], [weight_cuts, stiff_cuts, base], [ghost_message] * 2, [], 3
    )
    near, far = exchange(up, down)

    weights, ops = call(
        operator_kernel, "operators", [], [weight_cuts], [shape(NBLK, BS, LANES), shape(NBLK, BS, LANES)],
        [grams, turn], 4,
    )
    stats, partner = up[0, CUTS + 6 :], jnp.where(sub % 2 == 0, far[0, CUTS + 6 :], near[0, CUTS + 6 :])
    if size > 1 and size & (size - 1) == 0:
        stats, waiting = [stats + partner], 2
    else:
        stats, waiting = [stats], 0
    stats, near, far, ops = lax.optimization_barrier((stats, near, far, ops))
    while waiting is not None and waiting < size:
        stats, waiting = widening(stats, "sub", waiting, 4)
    blocks, halo_list = call(
        blocks_kernel, "blocks", [columns], [stiff_cuts],
        [shape(NBLK, K, BS, LANES), jax.ShapeDtypeStruct((1, NBLK * K + 8), jnp.int32)],
        [], 5, [vmem(), smem()],
    )

    zero, a1, a2, up, down = call(
        first_kernel, "first", [columns, halo_list, send_rows, counts], [blocks, ops, base, near, far],
        [shape(2 * count, ROWS, LANES), rows, rows, longer, longer],
        [partial(count), held(count)], 6,
    )
    low, high = exchange(up, down)
    stats = jnp.stack(stats)

    gops, k0, k1 = call(
        ghost_kernel, "ghosts", [], [ops, zero, a1, near, far],
        [shape(2 * IF, BS, LANES), rows, rows], [grams, *turned], 3,
    )

    v1, v2, v3, v4, k3, dots, sigma, up, down = call(
        second_kernel, "second", [columns, halo_list, send_rows, edge],
        [blocks, ops, gops, zero, a1, a2, k0, k1, low, high, stats],
        [rows, rows, rows, rows, rows, shape(count, 12, 8, LANES), shape(8, LANES), message, message],
        [partial(count), *turned, held(count)], 7,
    )
    low, high = exchange(up, down)

    v4, dots = call(
        moment_kernel, "moments", [send_rows, edge], [v4, k3, low, high, dots], [rows, shape(8, LANES)], [], 0.8
    )
    sums, waiting = widening([dots], "sub", 0, 2)
    zero, v4 = lax.optimization_barrier((zero, v4))
    (b1,) = call(
        target_kernel, "target", [columns, halo_list], [blocks, ops, gops, zero], [rows],
        [partial(count), held(count)], 3,
    )
    sums, b1, v4 = lax.optimization_barrier((sums, b1, v4))
    while waiting is not None:
        sums, waiting = widening(sums, "sub", waiting, 4)

    (w5,) = call(
        third_kernel, "third", [columns, halo_list], [blocks, ops, gops, v4], [rows],
        [partial(count), held(count)], 4,
    )

    stored = [zero, v1, v2, v3, v4, w5, b1]
    first, fixed, rho, coefs, scales, up, down = call(
        fourth_kernel, "fourth", [columns, send_rows], [blocks, ops, sigma, *stored, *sums],
        [rows, rows, rows, shape(10, 8, 8, LANES), shape(3, 8, LANES), message, message], [partial(count)], 3,
    )
    (early,) = call(early_kernel, "early", [], [coefs, *stored], [shape(NBLK * EARLY, LANES)], [], 0.5)
    size = lax.axis_size("rhs")
    early = [early]
    if size == 4:
        early.append(lax.ppermute(early[0], "rhs", [(i, i ^ 2) for i in range(size)]))
    low, high = exchange(up, down)

    zeta, answer = call(
        answer_kernel, "answer", [], [ops, coefs, *stored],
        [shape(2, count, ROWS, LANES), rows], [held(count), *turned], 1.5,
    )
    early, low, high, zeta = lax.optimization_barrier((early, low, high, zeta))
    if size == 4:
        early = early + [lax.ppermute(part, "rhs", [(i, i ^ 1) for i in range(size)]) for part in early]
    else:
        early = all_of(early[0], "rhs")

    (late,) = call(
        fifth_kernel, "fifth", [columns, halo_list, send_rows, edge],
        [blocks, ops, gops, rho, fixed, zeta, scales, low, high],
        [shape(NBLK * LATE, LANES)], [partial(count), held(count), held(count)], 4,
    )
    if size == 4:
        late = [late] + [lax.ppermute(late, "rhs", [(i, i ^ d) for i in range(size)]) for d in (2, 1, 3)]
    else:
        late = all_of(late, "rhs")

    (mixed,) = call(mixed_kernel, "mixed", [], early, [shape(NBLK, LANES, LANES)], [], 3)
    (grad,) = call(
        grad_kernel, "grad", [], [*early, *late, mixed, weights], [shape(NBLK * CUTS, LANES)],
        [turn], 10, [pl.BlockSpec((8 * CUTS, LANES), lambda g: (g, 0))], (NBLK // 8,),
    )
    grad = grad.reshape(NBLK // 8, CUTS, 8, LANES).transpose(0, 2, 1, 3).reshape(NBLK, BS * BS)
    return answer[:, OFF:HIGH, :BS].reshape(count, NBLK * BS), grad


def solution(mesh):
    in_specs = (
        P("sub", None, None),
        P("sub", None),
        P("rhs", "sub"),
        P("rhs", "sub"),
        P("sub", None),
        P("sub", None),
        P("sub"),
    )
    out_specs = (P("rhs", "sub"), P("sub", None))
    return jax.shard_map(shards, mesh=mesh, in_specs=in_specs, out_specs=out_specs, check_vma=False)
```

```python
import functools

import jax
import jax.numpy as jnp
from jax import lax
from jax.experimental import pallas as pl
from jax.experimental.pallas import tpu as pltpu
from jax.sharding import PartitionSpec as P

BS = 96
K = 4
NBLK = 48
IF = 6
ITERS = 4
ALL = (0, 1, 2, 3, 4, 5, 6, 7)
USED = ((0, 1), (0, 1, 2), (0, 1, 2, 3), (0, 1, 2, 3, 4, 6), ALL, ALL, ALL, ALL, ALL, (0, 1, 2, 3))
EARLY = 16
LATE = 4
CUTS = BS * BS // 128
GROUPS = 3
LANES = 128
OFF = 8
ROWS = 64
LOW = OFF - IF
HIGH = OFF + NBLK
CHUNK = 8
MIB = 1024 * 1024

highest = lax.Precision.HIGHEST
f32 = jnp.float32


def own(value):
    return value[:, OFF:HIGH]


def lane_ids():
    return lax.broadcasted_iota(jnp.int32, (BS, LANES), 1)


def diagonal():
    pos = lax.broadcasted_iota(jnp.int32, (BS, LANES), 0)
    row = (pos & ~31) + 4 * (pos & 7) + ((pos >> 3) & 3)
    return row == lane_ids()


def fold(prod):
    return jnp.sum(prod.reshape(BS // 8, 8, prod.shape[-1]), axis=0)


def unflatten(read):
    lane = lax.broadcasted_iota(jnp.int32, (8, LANES), 1)
    out = []
    for h in range(BS // 32):
        one, two, three = (read(24 * h + m) for m in range(3))
        out.append(jnp.where(lane < BS, one, 0.0))
        mixed = jnp.where(lane < 32, pltpu.roll(one, 32, 1), pltpu.roll(two, 32, 1))
        out.append(jnp.where(lane < BS, mixed, 0.0))
        mixed = jnp.where(lane < 64, pltpu.roll(two, 64, 1), pltpu.roll(three, 64, 1))
        out.append(jnp.where(lane < BS, mixed, 0.0))
        out.append(jnp.where(lane < BS, pltpu.roll(three, 96, 1), 0.0))
    return jnp.concatenate(out, axis=0)


def flatten(block, write):
    lane = lax.broadcasted_iota(jnp.int32, (8, LANES), 1)
    for h in range(BS // 32):
        one, two, three, four = (block[32 * h + 8 * j : 32 * h + 8 * j + 8] for j in range(4))
        two = pltpu.roll(two, 96, 1)
        three = pltpu.roll(three, 64, 1)
        write(24 * h, jnp.where(lane < BS, one, two))
        write(24 * h + 1, jnp.where(lane < 64, two, three))
        write(24 * h + 2, jnp.where(lane < 32, three, pltpu.roll(four, 32, 1)))


def make_operator(weights, gram_ref):
    gram = lax.dot_general(
        weights, weights, (((0,), (0,)), ((), ())), precision=highest, preferred_element_type=f32
    )
    gram_ref[...] = gram[:BS]
    rows = [gram_ref[pl.ds(32 * h + j, 8, stride=4), :] for h in range(BS // 32) for j in range(4)]
    return jnp.concatenate(rows, axis=0) + jnp.where(diagonal(), 1.0, 0.0)


def scatter_apply(blocks, op_ref, x_ref, y_ref, col_ref, column_ref):
    count = x_ref.shape[0]
    for k in range(1, K):
        for r in range(count):
            y_ref[k][r][...] = jnp.zeros_like(y_ref[k][r])

    def step(group, carry):
        base = pl.multiple_of(group * CHUNK, CHUNK)
        tiles = [x_ref[r, pl.ds(base + OFF, CHUNK), :] for r in range(count)]
        for i in range(CHUNK):
            n = group * CHUNK + i
            oper = op_ref[n]
            images = [jnp.sum(oper * tiles[r][i : i + 1, :], axis=1, keepdims=True) for r in range(count)]
            if column_ref is not None:
                for r in range(count):
                    column_ref[r] = jnp.where(lane_ids() == n + OFF, images[r], column_ref[r])
            for k in range(K):
                block = blocks[n, k]
                slot = n + OFF if k == 0 else col_ref[k, n] + LOW
                for r in range(count):
                    part = fold(block * images[r])
                    y_ref[k][r][slot] = part if k == 0 else y_ref[k][r][slot] + part
        return carry

    lax.fori_loop(0, NBLK // CHUNK, step, 0)


def ghost_images(op_ref, x_ref, g_ref):
    count = x_ref.shape[0]
    mask = diagonal()
    g_ref[...] = jnp.zeros_like(g_ref)
    for first, side in ((LOW, 0), (HIGH, IF)):
        for j in range(IF):
            slot = first + j
            oper = op_ref[side + j]
            for r in range(count):
                image = jnp.sum(oper * x_ref[r, slot : slot + 1, :], axis=1, keepdims=True)
                line = jnp.sum(fold(jnp.where(mask, image, 0.0)), axis=0, keepdims=True)
                g_ref[r, slot : slot + 1, :] = line


def ghost_apply(blocks, g_ref, y_ref, col_ref, list_ref):
    count = g_ref.shape[0]
    mask = diagonal()

    def step(item, carry):
        for u in range(4):
            entry = list_ref[0, 1 + item * 4 + u]
            n = entry >> 2
            k = entry & 3
            slot = col_ref[k, n] + LOW
            block = blocks[n, k]
            for r in range(count):
                image = jnp.sum(block * g_ref[r, pl.ds(slot, 1), :], axis=1, keepdims=True)
                y_ref[0][r][n + OFF] = y_ref[0][r][n + OFF] + fold(jnp.where(mask, image, 0.0))
        return carry

    lax.fori_loop(0, (list_ref[0, 0] + 3) >> 2, step, 0)


def pack(y_ref, r):
    sub = lax.broadcasted_iota(jnp.int32, (8, LANES), 0)
    groups = []
    for g in range(ROWS // 8):
        total = jnp.zeros((8, LANES), f32)
        for i in range(8):
            slot = g * 8 + i
            line = y_ref[1][r][slot]
            for k in range(2, K):
                line = line + y_ref[k][r][slot]
            if OFF <= slot < HIGH:
                line = line + y_ref[0][r][slot]
            line = jnp.sum(line, axis=0, keepdims=True)
            total = jnp.where(sub == i, line, total)
        groups.append(total)
    return jnp.concatenate(groups, axis=0)


def unpack_columns(column_ref, square_ref, r):
    for h in range(BS // 32):
        for j in range(4):
            start = 32 * h + 8 * j
            square_ref[pl.ds(32 * h + j, 8, stride=4), :] = column_ref[r, start : start + 8, :]
    square_ref[BS:, :] = jnp.zeros((LANES - BS, LANES), f32)
    return square_ref[...].T[:ROWS]


def messages(up_ref, down_ref, v_ref, send_ref, extra_ref=None):
    for r in range(v_ref.shape[0]):
        for j in range(IF):
            low = pl.ds(send_ref[0, j] + OFF, 1)
            high = pl.ds(send_ref[0, IF + j] + OFF, 1)
            down_ref[r, j : j + 1, :] = v_ref[r, low, :]
            up_ref[r, j : j + 1, :] = v_ref[r, high, :]
            down_ref[r, 8 + j : 9 + j, :] = v_ref[r, LOW + j : LOW + j + 1, :]
            up_ref[r, 8 + j : 9 + j, :] = v_ref[r, HIGH + j : HIGH + j + 1, :]
            if extra_ref is not None:
                down_ref[r, 16 + j : 17 + j, :] = extra_ref[r, low, :]
                up_ref[r, 16 + j : 17 + j, :] = extra_ref[r, high, :]


def complete(v_ref, low_ref, high_ref, send_ref, edge_ref):
    for r in range(v_ref.shape[0]):
        for j in range(IF):
            for part, base, ghost, flag in ((low_ref, 0, LOW, 0), (high_ref, IF, HIGH, 1)):
                at = pl.ds(send_ref[0, base + j] + OFF, 1)
                v_ref[r, at, :] = v_ref[r, at, :] + part[r, 8 + j : 9 + j, :]
                slot = ghost + j
                summed = v_ref[r, slot : slot + 1, :] + part[r, j : j + 1, :]
                v_ref[r, slot : slot + 1, :] = jnp.where(edge_ref[flag] > 0, summed, 0.0)


def tile_sum(first, second):
    prod = first * second
    return jnp.sum(prod.reshape(prod.shape[0] // 8, 8, LANES), axis=0)


def whole_sum(tile):
    return jnp.sum(jnp.sum(tile, axis=0, keepdims=True), axis=1, keepdims=True)


def inner_rows():
    row = lax.broadcasted_iota(jnp.int32, (ROWS, LANES), 0)
    return (row >= OFF) & (row < HIGH)


def pack_kernel(send_ref, raw_ref, stiff_ref, base_ref, up_ref, down_ref):
    vectors = base_ref.shape[0]
    flat = lax.broadcasted_iota(jnp.int32, (CUTS, LANES), 0) * LANES
    flat = (flat + lax.broadcasted_iota(jnp.int32, (CUTS, LANES), 1)).astype(f32)
    step = float(BS + 1)
    mask = jnp.where(flat - step * jnp.floor((flat + 0.5) * (1.0 / step)) == 0.0, 1.0, 0.0)

    def gather(group, carry):
        squares, traces = carry
        for i in range(CUTS):
            tile = raw_ref[pl.ds(pl.multiple_of(group * (8 * CUTS) + 8 * i, 8), 8), :]
            squares = squares + tile * tile
        return squares, traces

    blank = jnp.zeros((8, LANES), f32)
    squares, traces = lax.fori_loop(0, NBLK // CHUNK, gather, (blank, blank))
    for i in range(CHUNK):
        for q in range(0, CUTS, 8):
            start = i * (CUTS * K) + K * q
            traces = traces + mask[q : q + 8] * stiff_ref[pl.ds(start, 8, stride=K), :]
    squares = jnp.sum(squares, axis=0, keepdims=True)
    traces = (NBLK // CHUNK) * jnp.sum(traces, axis=0, keepdims=True)
    for part, ref in ((0, down_ref), (IF, up_ref)):
        for j in range(IF):
            n = send_ref[0, part + j]
            start = (n >> 3) * (8 * CUTS) + (n & 7)
            for i in range(CUTS // 8):
                ref[j, 8 * i : 8 * i + 8, :] = raw_ref[pl.ds(start + 64 * i, 8, stride=8), :]
            ref[j, CUTS:, :] = jnp.zeros((8, LANES), f32)
            weights = unflatten(lambda q: raw_ref[pl.ds(start + 8 * q, 8, stride=24), :])
            for r in range(vectors):
                line = base_ref[r, pl.ds(n + OFF, 1), :]
                ref[j, CUTS + r : CUTS + r + 1, :] = line
                if r < vectors // 2:
                    inside = jnp.sum(weights * line, axis=1, keepdims=True)
                    image = line + jnp.sum(fold(weights * inside), axis=0, keepdims=True)
                    at = CUTS + vectors + r
                    ref[j, at : at + 1, :] = image
        ref[0, CUTS + 6 : CUTS + 7, :] = squares
        ref[0, CUTS + 7 : CUTS + 8, :] = traces


def operator_kernel(raw_ref, weights_ref, ops_ref, gram_ref):
    base = pl.program_id(0) * CHUNK
    for i in range(CHUNK):
        weights = unflatten(lambda q: raw_ref[pl.ds(8 * q + i, 8, stride=24), :])
        weights_ref[i] = weights
        ops_ref[base + i] = make_operator(weights, gram_ref.at[i & 1])


def blocks_kernel(col_ref, stiff_ref, blocks_ref, list_ref, count_ref):
    base = pl.program_id(0) * CHUNK

    @pl.when(base == 0)
    def _():
        count_ref[0] = 0

    count = count_ref[0]
    for i in range(CHUNK):
        for k in range(K):
            blocks_ref[base + i, k] = unflatten(lambda q: stiff_ref[pl.ds(i * (CUTS * K) + 4 * q + k, 8, stride=12), :])
            col = col_ref[k, base + i]
            list_ref[0, 1 + count] = (base + i) * K + k
            count = count + jnp.where((col < IF) | (col >= IF + NBLK), 1, 0)
    count_ref[0] = count
    list_ref[0, 0] = count
    for u in range(4):
        list_ref[0, 1 + count + u] = 0


def first_kernel(
    col_ref, list_ref, send_ref, count_ref,
    blocks, op_ref, base_ref, low_ref, high_ref,
    zero_ref, a1_ref, a2_ref, up_ref, down_ref,
    y_ref, g_ref,
):
    count = a1_ref.shape[0]
    zero_ref[...] = base_ref[...]
    g_ref[...] = jnp.zeros_like(g_ref)
    row = lax.broadcasted_iota(jnp.int32, (ROWS, LANES), 0)
    dead = (row >= count_ref[0] + OFF) & (row < HIGH)
    for r in range(count):
        zero_ref[r] = jnp.where(dead, 0.0, zero_ref[r])
        for part, first in ((low_ref, LOW), (high_ref, HIGH)):
            for j in range(IF):
                at = slice(first + j, first + j + 1)
                for s in (r, count + r):
                    zero_ref[s, at, :] = part[j, CUTS + s : CUTS + s + 1, :]
                g_ref[r, at, :] = part[j, CUTS + 2 * count + r : CUTS + 2 * count + r + 1, :]
    scatter_apply(blocks, op_ref, zero_ref.at[pl.ds(0, count)], y_ref, col_ref, None)
    ghost_apply(blocks, g_ref, y_ref, col_ref, list_ref)
    inner = inner_rows()
    for r in range(count):
        a1_ref[r] = jnp.where(inner, pack(y_ref, r), 0.0)
    scatter_apply(blocks, op_ref, a1_ref, y_ref, col_ref, None)
    for r in range(count):
        a2_ref[r] = pack(y_ref, r)
    messages(up_ref, down_ref, a2_ref, send_ref, a1_ref)


def operator_rows(op_ref, x_ref, out_ref, column_ref, square_ref):
    column_ref[...] = jnp.zeros_like(column_ref)
    lanes = lane_ids()
    for r in range(column_ref.shape[0]):
        for n in range(NBLK):
            image = jnp.sum(op_ref[n] * x_ref[r, n + OFF : n + OFF + 1, :], axis=1, keepdims=True)
            column_ref[r] = jnp.where(lanes == n + OFF, image, column_ref[r])
        out_ref[r] = unpack_columns(column_ref, square_ref, r)


def ghost_kernel(op_ref, zero_ref, a1_ref, low_ref, high_ref, gop_ref, k0_ref, k1_ref, gram_ref, column_ref, square_ref):
    for part, first in ((low_ref, 0), (high_ref, IF)):
        for j in range(IF):
            weights = unflatten(lambda q: part[j, pl.ds(q, 8, stride=3), :])
            gop_ref[first + j] = make_operator(weights, gram_ref.at[j & 1])
    operator_rows(op_ref, zero_ref, k0_ref, column_ref, square_ref)
    operator_rows(op_ref, a1_ref, k1_ref, column_ref, square_ref)


def target_kernel(col_ref, list_ref, blocks, op_ref, gop_ref, zero_ref, b1_ref, y_ref, g_ref):
    count = b1_ref.shape[0]
    target = zero_ref.at[pl.ds(count, count)]
    scatter_apply(blocks, op_ref, target, y_ref, col_ref, None)
    ghost_images(gop_ref, target, g_ref)
    ghost_apply(blocks, g_ref, y_ref, col_ref, list_ref)
    inner = inner_rows()
    for r in range(count):
        b1_ref[r] = jnp.where(inner, pack(y_ref, r), 0.0)


def second_kernel(
    col_ref, list_ref, send_ref, edge_ref,
    blocks, ops_ref, gop_ref, zero_ref, a1_ref, a2_in, k0_ref, k1_ref, low_ref, high_ref, stats_ref,
    v1_ref, v2_ref, v3_ref, v4_ref, k3_ref, dots_ref, sigma_ref, up_ref, down_ref,
    y_ref, column_ref, square_ref, g_ref,
):
    count = a1_ref.shape[0]
    inner = inner_rows()
    squares, traces = stats_ref[0, :1], stats_ref[0, 1:]
    for s in range(1, stats_ref.shape[0]):
        squares = squares + stats_ref[s, :1]
        traces = traces + stats_ref[s, 1:]
    scale = 1.0 / (lax.axis_size("sub") * NBLK * BS)
    sigma = (1.0 + scale * whole_sum(squares)) * (scale * whole_sum(traces))
    sigma_ref[...] = jnp.broadcast_to(sigma, sigma_ref.shape)
    column_ref[...] = jnp.zeros_like(column_ref)
    v2_ref[...] = a2_in[...]
    complete(v2_ref, low_ref, high_ref, send_ref, edge_ref)
    for r in range(count):
        v1_ref[r] = a1_ref[r]
        for part, ghost, flag in ((low_ref, LOW, 0), (high_ref, HIGH, 1)):
            for j in range(IF):
                v1_ref[r, ghost + j : ghost + j + 1, :] = part[r, 16 + j : 17 + j, :]
        v1 = v1_ref[r] - sigma * zero_ref[r]
        v2_ref[r] = v2_ref[r] - sigma * v1_ref[r] - sigma * v1
        v1 = jnp.where(inner, v1, 0.0)
        v1_ref[r] = v1
        v0 = jnp.where(inner, zero_ref[r], 0.0)
        target = jnp.where(inner, zero_ref[count + r], 0.0)
        second = k1_ref[r] - sigma * k0_ref[r]
        dots_ref[r, 0] = tile_sum(v0, k0_ref[r])
        dots_ref[r, 1] = tile_sum(v1, k0_ref[r])
        dots_ref[r, 2] = tile_sum(v1, second)
        dots_ref[r, 8] = tile_sum(target, k0_ref[r])
        dots_ref[r, 9] = tile_sum(target, second)
    scatter_apply(blocks, ops_ref, v2_ref, y_ref, col_ref, column_ref)
    ghost_images(gop_ref, v2_ref, g_ref)
    ghost_apply(blocks, g_ref, y_ref, col_ref, list_ref)
    for r in range(count):
        image = unpack_columns(column_ref, square_ref, r)
        v3 = jnp.where(inner, pack(y_ref, r) - sigma * v2_ref[r], 0.0)
        v3_ref[r] = v3
        dots_ref[r, 3] = tile_sum(v1_ref[r], image)
        dots_ref[r, 4] = tile_sum(jnp.where(inner, v2_ref[r], 0.0), image)
        dots_ref[r, 5] = tile_sum(v3, image)
        dots_ref[r, 10] = tile_sum(jnp.where(inner, zero_ref[count + r], 0.0), image)
    scatter_apply(blocks, ops_ref, v3_ref, y_ref, col_ref, column_ref)
    for r in range(count):
        image = unpack_columns(column_ref, square_ref, r)
        dots_ref[r, 6] = tile_sum(v3_ref[r], image)
        dots_ref[r, 7] = jnp.zeros((8, LANES), f32)
        dots_ref[r, 11] = tile_sum(jnp.where(inner, zero_ref[count + r], 0.0), image)
        k3_ref[r] = image
        v4_ref[r] = pack(y_ref, r) - sigma * v3_ref[r]
    messages(up_ref, down_ref, v4_ref, send_ref)


def moment_kernel(send_ref, edge_ref, v4_in, k3_ref, low_ref, high_ref, dots_in, v4_ref, dots_ref):
    v4_ref[...] = v4_in[...]
    complete(v4_ref, low_ref, high_ref, send_ref, edge_ref)
    lane = lax.broadcasted_iota(jnp.int32, (8, LANES), 1)
    sub = lax.broadcasted_iota(jnp.int32, (8, LANES), 0)
    total = jnp.zeros((8, LANES), f32)
    for r in range(v4_ref.shape[0]):
        for d in range(12):
            part = tile_sum(v4_ref[r], k3_ref[r]) if d == 7 else dots_in[r, d]
            total = jnp.where((lane == d) & (sub == r), whole_sum(part), total)
    dots_ref[...] = total


def third_kernel(col_ref, list_ref, blocks, ops_ref, gop_ref, v4_ref, w5_ref, y_ref, g_ref):
    scatter_apply(blocks, ops_ref, v4_ref, y_ref, col_ref, None)
    ghost_images(gop_ref, v4_ref, g_ref)
    ghost_apply(blocks, g_ref, y_ref, col_ref, list_ref)
    for r in range(v4_ref.shape[0]):
        w5_ref[r] = pack(y_ref, r)


def combine(coef_ref, parts, g, r):
    total = None
    for s in USED[g]:
        term = coef_ref[g, s, r : r + 1, :] * parts[s]
        total = term if total is None else total + term
    return total


def sources(zero_ref, stored, r, count):
    v1_ref, v2_ref, v3_ref, v4_ref, w5_ref, b1_ref = stored
    parts = [zero_ref[r], v1_ref[r], v2_ref[r], v3_ref[r], v4_ref[r], w5_ref[r], zero_ref[count + r], b1_ref[r]]
    inner = inner_rows()
    return [jnp.where(inner, part, 0.0) for part in parts]


def fourth_kernel(col_ref, send_ref, blocks, ops_ref, sigma_ref, zero_ref, *refs):
    stored, sums = refs[:6], [part[...] for part in refs[6:-8]]
    first_ref, base_ref, rho_ref, coef_ref, scale_ref, up_ref, down_ref, y_ref = refs[-8:]
    while len(sums) > 1:
        sums = [sums[i] + sums[i + 1] for i in range(0, len(sums), 2)]
    sums = sums[0]
    column = lambda d: jnp.broadcast_to(sums[:, d : d + 1], (8, LANES))
    combos, scales = scalars([column(d) for d in range(8)], [column(8 + d) for d in range(4)], sigma_ref[...])
    for g, value in enumerate(scales):
        scale_ref[g] = value
    for g, combo in enumerate(combos):
        for s, value in enumerate(combo):
            if s in USED[g]:
                coef_ref[g, s] = value
    count = rho_ref.shape[0]
    for r in range(count):
        parts = sources(zero_ref, stored, r, count)
        first_ref[r] = combine(coef_ref, parts, 5, r)
        base_ref[r] = combine(coef_ref, parts, 7, r)
    scatter_apply(blocks, ops_ref, first_ref, y_ref, col_ref, None)
    for r in range(count):
        rho_ref[r] = base_ref[r] - scale_ref[0, r : r + 1, :] * pack(y_ref, r)
    messages(up_ref, down_ref, rho_ref, send_ref)


def early_kernel(coef_ref, zero_ref, *refs):
    stored, early_ref = refs[:6], refs[6]
    count = zero_ref.shape[0] // 2
    for r in range(count):
        parts = sources(zero_ref, stored, r, count)
        early_ref[pl.ds(r, NBLK, stride=EARLY), :] = parts[0][OFF:HIGH]
        for g, slot in ((0, 2), (1, 4), (2, 6), (4, 12), (3, 14)):
            early_ref[pl.ds(slot + r, NBLK, stride=EARLY), :] = combine(coef_ref, parts, g, r)[OFF:HIGH]
        for slot in (8, 10):
            early_ref[pl.ds(slot + r, NBLK, stride=EARLY), :] = jnp.zeros((NBLK, LANES), f32)


def answer_kernel(ops_ref, coef_ref, zero_ref, *refs):
    stored, (zeta_ref, sol_ref, x_ref, column_ref, square_ref) = refs[:6], refs[6:]
    count = zeta_ref.shape[1]
    for r in range(count):
        parts = sources(zero_ref, stored, r, count)
        zeta_ref[0, r] = combine(coef_ref, parts, 8, r)
        zeta_ref[1, r] = combine(coef_ref, parts, 6, r)
        x_ref[r] = combine(coef_ref, parts, 9, r)
    operator_rows(ops_ref, x_ref, sol_ref, column_ref, square_ref)


def fifth_kernel(
    col_ref, list_ref, send_ref, edge_ref,
    blocks, ops_ref, gop_ref, rho_in, base_ref, zeta_ref, scale_ref, low_ref, high_ref,
    late_ref, y_ref, rho_ref, g_ref,
):
    count = rho_in.shape[0]
    rho_ref[...] = rho_in[...]
    complete(rho_ref, low_ref, high_ref, send_ref, edge_ref)
    scatter_apply(blocks, ops_ref, rho_ref, y_ref, col_ref, None)
    ghost_images(gop_ref, rho_ref, g_ref)
    ghost_apply(blocks, g_ref, y_ref, col_ref, list_ref)
    for r in range(count):
        change = rho_ref[r] - base_ref[r]
        first = zeta_ref[0, r] + scale_ref[1, r : r + 1, :] * change - scale_ref[2, r : r + 1, :] * pack(y_ref, r)
        second = zeta_ref[1, r] + change
        late_ref[pl.ds(r, NBLK, stride=LATE), :] = first[OFF:HIGH]
        late_ref[pl.ds(2 + r, NBLK, stride=LATE), :] = second[OFF:HIGH]


def split(value):
    high = value.astype(jnp.bfloat16)
    return high, (value - high.astype(f32)).astype(jnp.bfloat16)


def product(first, second, dim):
    (fh, fl), (sh, sl) = split(first), split(second)
    left = jnp.concatenate([fh, fl, fh], axis=dim)
    right = jnp.concatenate([sh, sh, sl], axis=0)
    return lax.dot_general(left, right, (((dim,), (0,)), ((), ())), preferred_element_type=f32)


def mixed_kernel(*refs):
    early, mixed_ref = refs[:-1], refs[-1]

    def step(group, carry):
        for i in range(CHUNK):
            at = pl.multiple_of((group * CHUNK + i) * EARLY, EARLY)
            resid = [ref[pl.ds(at, 8), :] for ref in early]
            zeta = [ref[pl.ds(at + 8, 8), :] for ref in early]
            left = jnp.concatenate(resid + zeta, axis=0)
            right = jnp.concatenate(zeta + resid, axis=0)
            mixed_ref[group * CHUNK + i] = product(left, right, 0)
        return carry

    lax.fori_loop(0, NBLK // CHUNK, step, 0)


def grad_kernel(*refs):
    peers = (len(refs) - 3) // 2
    early, late, mixed_ref, weights_ref, grad_ref = refs[:peers], refs[peers : 2 * peers], *refs[-3:]
    first = pl.program_id(0) * GROUPS
    upper = lax.broadcasted_iota(jnp.int32, (8, LANES), 0) < LATE

    def join(tiles):
        out = []
        for q in range(0, len(tiles), 2):
            other = pltpu.roll(tiles[q + 1], LATE, 0) if q + 1 < len(tiles) else jnp.zeros((8, LANES), f32)
            out.append(jnp.where(upper, tiles[q], other))
        return out

    def step(part, carry):
        group = first + part
        for i in range(CHUNK):
            n = group * CHUNK + i
            at = pl.multiple_of(n * EARLY, EARLY)
            pair = pl.ds(pl.multiple_of(group * (CHUNK * LATE) + 8 * (i // 2), 8), 8)
            resid = join([ref[pl.ds(at, 8), :] for ref in early])
            zeta = [ref[pair, :] for ref in late]
            zeta = join([pltpu.roll(tile, LATE, 0) for tile in zeta] if i % 2 else zeta)
            left = jnp.concatenate(resid + zeta, axis=0)
            right = jnp.concatenate(zeta + resid, axis=0)
            grad = product(weights_ref[part * CHUNK + i], mixed_ref[n] + product(left, right, 0), 1)

            def write(q, value):
                grad_ref[pl.ds(part * (8 * CUTS) + 8 * q + i, 8, stride=24), :] = value

            flatten(grad, write)
        return carry

    lax.fori_loop(0, GROUPS, step, 0)


def widening(parts, axis, step, most):
    if step is None:
        return parts, None
    size = lax.axis_size(axis)
    if size & (size - 1):
        return [lax.psum(parts[0], axis)], None
    step = step or 1
    while len(parts) > 1:
        parts = [parts[i] + parts[i + 1] for i in range(0, len(parts), 2)]
    width = min(most, size // step)
    total = parts[0]
    parts = [total] + [lax.ppermute(total, axis, [(i, i ^ (d * step)) for i in range(size)]) for d in range(1, width)]
    step *= width
    return parts, step if step < size else None


def all_of(values, axis):
    size = lax.axis_size(axis)
    return [values] + [
        lax.ppermute(values, axis, [(i, (i + d) % size) for i in range(size)]) for d in range(1, size)
    ]


def exchange(up, down):
    size = lax.axis_size("sub")
    rising = [(i, i + 1) for i in range(size - 1)]
    falling = [(j, i) for i, j in rising]
    return lax.ppermute(up, "sub", rising), lax.ppermute(down, "sub", falling)


def plus(first, second):
    if first is None:
        return second
    return first if second is None else first + second


def times(first, second):
    return None if first is None or second is None else first * second


def add(first, second, scale):
    size = max(len(first), len(second))
    first = list(first) + [None] * (size - len(first))
    second = list(second) + [None] * (size - len(second))
    return [plus(a, times(scale, b)) for a, b in zip(first, second)]


def scaled(first, scale):
    return [times(scale, a) for a in first]


def scalars(moments, products, sigma):
    one = jnp.ones_like(sigma)

    def inner(first, second):
        weights = [None] * (len(first) + len(second) - 1)
        for i, a in enumerate(first):
            for j, b in enumerate(second):
                weights[i + j] = plus(weights[i + j], a * b)
        total = None
        for weight, moment in zip(weights, moments):
            total = plus(total, weight * moment)
        return total

    def apply(poly):
        out = [None] * (len(poly) + 1)
        for j, value in enumerate(poly):
            out[j] = plus(out[j], sigma * value)
            out[j + 1] = plus(out[j + 1], value)
        return out

    resid = [[one]]
    direc = [[one]]
    image = []
    step, ratio, norm, curv = [], [None], [moments[0]], []
    for i in range(ITERS):
        image.append(apply(direc[i]))
        curv.append(inner(direc[i], image[i]))
        step.append(norm[i] / curv[i])
        if i + 1 < ITERS:
            resid.append(add(resid[i], image[i], -step[i]))
            norm.append(inner(resid[i + 1], resid[i + 1]))
            ratio.append(norm[i + 1] / norm[i])
            direc.append(add(resid[i + 1], direc[i], ratio[i + 1]))
    cot = []
    for i in range(ITERS):
        total = None
        for j, value in enumerate(resid[i]):
            total = plus(total, value * products[j])
        cot.append(total)
    along = [cot[0]]
    for i in range(1, ITERS):
        along.append(cot[i] + ratio[i] * along[i - 1])

    def row(poly):
        return list(poly) + [None] * (8 - len(poly))

    target = [None] * 6 + [one, None]
    resid_rows = [row(poly) for poly in resid]
    image_rows = [row(poly) for poly in image]
    inverse = [1.0 / value for value in step]

    def resid_prod(i):
        return [norm[l] if l == i else None for l in range(ITERS)]

    def image_prod(i):
        out = [None] * ITERS
        out[i] = norm[i] * inverse[i]
        if i + 1 < ITERS:
            out[i + 1] = -norm[i + 1] * inverse[i]
        return out

    def along_dir(prod, i):
        total = prod[0]
        for l in range(1, i + 1):
            total = plus(prod[l], times(ratio[l], total))
        return total

    def operator_prod(prod):
        out = []
        for l in range(ITERS - 1):
            value = times(add([prod[l]], [prod[l + 1]], -one)[0], inverse[l])
            if l > 0:
                back = times(add([prod[l - 1]], [prod[l]], -one)[0], inverse[l - 1])
                value = add([value], [back], -ratio[l])[0]
            out.append(value)
        return out + [None]

    last = ITERS - 1
    step_bar = along[last]
    curv_bar = -step_bar * step[last] / curv[last]
    dir_row = add(scaled(target, step[last]), image_rows[last], 2 * curv_bar)
    dir_prod = add(scaled(cot, step[last]), image_prod(last), 2 * curv_bar)
    norm_bar = step_bar / curv[last]
    rho_row = [None] * 8
    rho_prod = [None] * ITERS
    zetas = [None] * ITERS
    rho_rows = []
    for i in (2, 1, 0):
        ratio_bar = along_dir(dir_prod, i)
        full = norm_bar + ratio_bar / norm[i]
        zetas[i + 1] = add(dir_row, resid_rows[i + 1], full)
        rho_row = add(add(rho_row, zetas[i + 1], one), resid_rows[i + 1], full)
        rho_prod = add(add(rho_prod, dir_prod, one), resid_prod(i + 1), 2 * full)
        rho_rows.append(rho_row)
        step_bar = along[i] - (rho_prod[i] - rho_prod[i + 1]) * inverse[i]
        curv_bar = -step_bar * step[i] / curv[i]
        oper = [None] * 8
        if i == 2:
            for k in range(5):
                if k < 4:
                    oper[k] = plus(oper[k], times(sigma, rho_row[k]))
                    oper[k + 1] = plus(oper[k + 1], rho_row[k])
                else:
                    oper[5] = plus(oper[5], rho_row[4])
            oper[7] = rho_row[6]
        kept = add(scaled(dir_row, ratio[i + 1]), target, step[i])
        kept = add(kept, image_rows[i], 2 * curv_bar)
        dir_row = add(kept, oper, -step[i])
        dir_prod = add(add(scaled(dir_prod, ratio[i + 1]), cot, step[i]), image_prod(i), 2 * curv_bar)
        dir_prod = add(dir_prod, operator_prod(rho_prod), -step[i])
        norm_bar = step_bar / curv[i] - ratio_bar * norm[i + 1] / (norm[i] * norm[i])
    zetas[0] = add(dir_row, resid_rows[0], norm_bar)
    answer = [None] * 8
    for i in range(ITERS):
        answer = add(answer, row(direc[i]), step[i])
    combos = [resid_rows[1], resid_rows[2], resid_rows[3], zetas[3], zetas[2], rho_rows[1], zetas[1], rho_rows[2], zetas[0], answer]
    return combos, [step[1], ratio[1], step[0]]


def vmem():
    return pl.BlockSpec(memory_space=pltpu.VMEM)


def hbm():
    return pl.BlockSpec(memory_space=pltpu.HBM)


def smem():
    return pl.BlockSpec(memory_space=pltpu.SMEM)


def shards(stiffness, precond, rhs_vec, cotangent, col_index, send_rows, counts):
    count = rhs_vec.shape[0]
    sub = lax.axis_index("sub")
    size = lax.axis_size("sub")
    edge = jnp.stack([sub > 0, sub + 1 < size]).astype(jnp.int32)
    columns = col_index.T
    stiff_cuts = stiffness.reshape(NBLK, K, CUTS, LANES).transpose(0, 2, 1, 3).reshape(NBLK * K * CUTS, LANES)
    weight_cuts = precond.reshape(NBLK // 8, 8, CUTS, LANES).transpose(0, 2, 1, 3).reshape(NBLK * CUTS, LANES)
    base = jnp.concatenate([rhs_vec, cotangent], axis=0).reshape(2 * count, NBLK, BS)
    base = jnp.pad(base, ((0, 0), (OFF, ROWS - HIGH), (0, LANES - BS)))

    def shape(*dims):
        return jax.ShapeDtypeStruct(dims, f32)

    def call(kernel, name, scalars_in, arrays_in, outs, scratch, expected, specs=None, grid=(), in_specs=None):
        return pl.pallas_call(
            kernel,
            grid=grid,
            in_specs=in_specs or [smem()] * len(scalars_in) + [vmem()] * len(arrays_in),
            out_specs=specs or [vmem()] * len(outs),
            out_shape=outs,
            scratch_shapes=scratch,
            compiler_params=pltpu.CompilerParams(vmem_limit_bytes=8 * MIB),
            cost_estimate=pl.CostEstimate(flops=MIB, bytes_accessed=int(expected * 3.2e6), transcendentals=0),
            name=name,
        )(*scalars_in, *arrays_in)

    rows = shape(count, ROWS, LANES)
    message = shape(count, 16, LANES)
    longer = shape(count, 24, LANES)
    ghost_message = shape(IF, CUTS + 8, LANES)
    partial = lambda r: [[pltpu.VMEM((ROWS, 8, LANES), f32)] * r] * K
    turned = [pltpu.VMEM((count, BS, LANES), f32), pltpu.VMEM((LANES, LANES), f32)]
    held = lambda r: pltpu.VMEM((r, ROWS, LANES), f32)
    grams = pltpu.VMEM((2, BS, LANES), f32)

    up, down = call(
        pack_kernel, "pack", [send_rows], [weight_cuts, lax.slice_in_dim(stiff_cuts, 0, CHUNK * CUTS * K), base], [ghost_message] * 2, [], 3
    )
    near, far = exchange(up, down)

    weights, ops = call(
        operator_kernel, "operators", [], [weight_cuts], [shape(NBLK, BS, LANES), shape(NBLK, BS, LANES)],
        [grams], 4, [pl.BlockSpec((CHUNK, BS, LANES), lambda g: (g, 0, 0)), vmem()], (NBLK // CHUNK,),
        [pl.BlockSpec((CHUNK * CUTS, LANES), lambda g: (g, 0))],
    )
    stats, partner = up[0, CUTS + 6 :], jnp.where(sub % 2 == 0, far[0, CUTS + 6 :], near[0, CUTS + 6 :])
    if size > 1 and size & (size - 1) == 0:
        stats, waiting = [stats + partner], 2
    else:
        stats, waiting = [stats], 0
    stats, near, far, ops = lax.optimization_barrier((stats, near, far, ops))
    while waiting is not None and waiting < size:
        stats, waiting = widening(stats, "sub", waiting, 4)
    blocks, halo_list = call(
        blocks_kernel, "blocks", [columns], [stiff_cuts],
        [shape(NBLK, K, BS, LANES), jax.ShapeDtypeStruct((1, NBLK * K + 8), jnp.int32)],
        [pltpu.SMEM((1,), jnp.int32)], 5, [vmem(), smem()], (NBLK // CHUNK,),
        [smem(), pl.BlockSpec((CHUNK * CUTS * K, LANES), lambda g: (g, 0))],
    )

    zero, a1, a2, up, down = call(
        first_kernel, "first", [columns, halo_list, send_rows, counts], [blocks, ops, base, near, far],
        [shape(2 * count, ROWS, LANES), rows, rows, longer, longer],
        [partial(count), held(count)], 6,
    )
    low, high = exchange(up, down)
    stats = jnp.stack(stats)

    gops, k0, k1 = call(
        ghost_kernel, "ghosts", [], [ops, zero, a1, near, far],
        [shape(2 * IF, BS, LANES), rows, rows], [grams, *turned], 3,
    )

    v1, v2, v3, v4, k3, dots, sigma, up, down = call(
        second_kernel, "second", [columns, halo_list, send_rows, edge],
        [blocks, ops, gops, zero, a1, a2, k0, k1, low, high, stats],
        [rows, rows, rows, rows, rows, shape(count, 12, 8, LANES), shape(8, LANES), message, message],
        [partial(count), *turned, held(count)], 7,
    )
    low, high = exchange(up, down)

    v4, dots = call(
        moment_kernel, "moments", [send_rows, edge], [v4, k3, low, high, dots], [rows, shape(8, LANES)], [], 0.8
    )
    sums, waiting = widening([dots], "sub", 0, 2)
    zero, v4 = lax.optimization_barrier((zero, v4))
    (b1,) = call(
        target_kernel, "target", [columns, halo_list], [blocks, ops, gops, zero], [rows],
        [partial(count), held(count)], 3,
    )
    sums, b1, v4 = lax.optimization_barrier((sums, b1, v4))
    while waiting is not None:
        sums, waiting = widening(sums, "sub", waiting, 4)

    (w5,) = call(
        third_kernel, "third", [columns, halo_list], [blocks, ops, gops, v4], [rows],
        [partial(count), held(count)], 4,
    )

    stored = [zero, v1, v2, v3, v4, w5, b1]
    first, fixed, rho, coefs, scales, up, down = call(
        fourth_kernel, "fourth", [columns, send_rows], [blocks, ops, sigma, *stored, *sums],
        [rows, rows, rows, shape(10, 8, 8, LANES), shape(3, 8, LANES), message, message], [partial(count)], 3,
    )
    (early,) = call(early_kernel, "early", [], [coefs, *stored], [shape(NBLK * EARLY, LANES)], [], 0.5)
    size = lax.axis_size("rhs")
    early = [early]
    if size == 4:
        early.append(lax.ppermute(early[0], "rhs", [(i, i ^ 2) for i in range(size)]))
    low, high = exchange(up, down)

    zeta, answer = call(
        answer_kernel, "answer", [], [ops, coefs, *stored],
        [shape(2, count, ROWS, LANES), rows], [held(count), *turned], 1.5,
    )
    early, low, high, zeta = lax.optimization_barrier((early, low, high, zeta))
    if size == 4:
        early = early + [lax.ppermute(part, "rhs", [(i, i ^ 1) for i in range(size)]) for part in early]
    else:
        early = all_of(early[0], "rhs")

    (late,) = call(
        fifth_kernel, "fifth", [columns, halo_list, send_rows, edge],
        [blocks, ops, gops, rho, fixed, zeta, scales, low, high],
        [shape(NBLK * LATE, LANES)], [partial(count), held(count), held(count)], 4,
    )
    if size == 4:
        late = [late] + [lax.ppermute(late, "rhs", [(i, i ^ d) for i in range(size)]) for d in (2, 1, 3)]
    else:
        late = all_of(late, "rhs")

    (mixed,) = call(mixed_kernel, "mixed", [], early, [shape(NBLK, LANES, LANES)], [], 3)
    (grad,) = call(
        grad_kernel, "grad", [], [*early, *late, mixed, weights], [shape(NBLK * CUTS, LANES)], [], 10,
        [pl.BlockSpec((GROUPS * 8 * CUTS, LANES), lambda g: (g, 0))], (NBLK // (GROUPS * CHUNK),),
        [vmem()] * (len(early) + len(late) + 1) + [pl.BlockSpec((GROUPS * CHUNK, BS, LANES), lambda g: (g, 0, 0))],
    )
    grad = grad.reshape(NBLK // 8, CUTS, 8, LANES).transpose(0, 2, 1, 3).reshape(NBLK, BS * BS)
    return answer[:, OFF:HIGH, :BS].reshape(count, NBLK * BS), grad


def solution(mesh):
    in_specs = (
        P("sub", None, None),
        P("sub", None),
        P("rhs", "sub"),
        P("rhs", "sub"),
        P("sub", None),
        P("sub", None),
        P("sub"),
    )
    out_specs = (P("rhs", "sub"), P("sub", None))
    return jax.shard_map(shards, mesh=mesh, in_specs=in_specs, out_specs=out_specs, check_vma=False)
```

```python
import functools

import jax
import jax.numpy as jnp
from jax import lax
from jax.experimental import pallas as pl
from jax.experimental.pallas import tpu as pltpu
from jax.sharding import PartitionSpec as P

BS = 96
K = 4
NBLK = 48
IF = 6
ITERS = 4
ALL = (0, 1, 2, 3, 4, 5, 6, 7)
USED = ((0, 1), (0, 1, 2), (0, 1, 2, 3), (0, 1, 2, 3, 4, 6), ALL, ALL, ALL, ALL, ALL, (0, 1, 2, 3))
EARLY = 16
LATE = 4
CUTS = BS * BS // 128
SPAN = 24
WIDE = 16
LANES = 128
OFF = 8
ROWS = 64
LOW = OFF - IF
HIGH = OFF + NBLK
CHUNK = 8
MIB = 1024 * 1024

highest = lax.Precision.HIGHEST
f32 = jnp.float32


def own(value):
    return value[:, OFF:HIGH]


def lane_ids():
    return lax.broadcasted_iota(jnp.int32, (BS, LANES), 1)


def diagonal():
    pos = lax.broadcasted_iota(jnp.int32, (BS, LANES), 0)
    row = (pos & ~31) + 4 * (pos & 7) + ((pos >> 3) & 3)
    return row == lane_ids()


def fold(prod):
    return jnp.sum(prod.reshape(BS // 8, 8, prod.shape[-1]), axis=0)


def unflatten(read):
    lane = lax.broadcasted_iota(jnp.int32, (8, LANES), 1)
    out = []
    for h in range(BS // 32):
        one, two, three = (read(24 * h + m) for m in range(3))
        out.append(jnp.where(lane < BS, one, 0.0))
        mixed = jnp.where(lane < 32, pltpu.roll(one, 32, 1), pltpu.roll(two, 32, 1))
        out.append(jnp.where(lane < BS, mixed, 0.0))
        mixed = jnp.where(lane < 64, pltpu.roll(two, 64, 1), pltpu.roll(three, 64, 1))
        out.append(jnp.where(lane < BS, mixed, 0.0))
        out.append(jnp.where(lane < BS, pltpu.roll(three, 96, 1), 0.0))
    return jnp.concatenate(out, axis=0)


def flatten(block, write):
    lane = lax.broadcasted_iota(jnp.int32, (8, LANES), 1)
    for h in range(BS // 32):
        one, two, three, four = (block[32 * h + 8 * j : 32 * h + 8 * j + 8] for j in range(4))
        two = pltpu.roll(two, 96, 1)
        three = pltpu.roll(three, 64, 1)
        write(24 * h, jnp.where(lane < BS, one, two))
        write(24 * h + 1, jnp.where(lane < 64, two, three))
        write(24 * h + 2, jnp.where(lane < 32, three, pltpu.roll(four, 32, 1)))


def make_operator(weights, gram_ref):
    gram = lax.dot_general(
        weights, weights, (((0,), (0,)), ((), ())), precision=highest, preferred_element_type=f32
    )
    gram_ref[...] = gram[:BS]
    rows = [gram_ref[pl.ds(32 * h + j, 8, stride=4), :] for h in range(BS // 32) for j in range(4)]
    return jnp.concatenate(rows, axis=0) + jnp.where(diagonal(), 1.0, 0.0)


def scatter_apply(blocks, op_ref, x_ref, y_ref, col_ref, column_ref):
    count = x_ref.shape[0]
    for k in range(1, K):
        for r in range(count):
            y_ref[k][r][...] = jnp.zeros_like(y_ref[k][r])

    def step(group, carry):
        base = pl.multiple_of(group * SPAN, CHUNK)
        tiles = [x_ref[r, pl.ds(base + OFF, SPAN), :] for r in range(count)]
        for i in range(SPAN):
            n = group * SPAN + i
            oper = op_ref[n]
            images = [jnp.sum(oper * tiles[r][i : i + 1, :], axis=1, keepdims=True) for r in range(count)]
            if column_ref is not None:
                for r in range(count):
                    column_ref[r] = jnp.where(lane_ids() == n + OFF, images[r], column_ref[r])
            for k in range(K):
                block = blocks[n, k]
                slot = n + OFF if k == 0 else col_ref[k, n] + LOW
                for r in range(count):
                    part = fold(block * images[r])
                    y_ref[k][r][slot] = part if k == 0 else y_ref[k][r][slot] + part
        return carry

    lax.fori_loop(0, NBLK // SPAN, step, 0)


def ghost_images(op_ref, x_ref, g_ref):
    count = x_ref.shape[0]
    mask = diagonal()
    g_ref[...] = jnp.zeros_like(g_ref)
    for first, side in ((LOW, 0), (HIGH, IF)):
        for j in range(IF):
            slot = first + j
            oper = op_ref[side + j]
            for r in range(count):
                image = jnp.sum(oper * x_ref[r, slot : slot + 1, :], axis=1, keepdims=True)
                line = jnp.sum(fold(jnp.where(mask, image, 0.0)), axis=0, keepdims=True)
                g_ref[r, slot : slot + 1, :] = line


def ghost_apply(blocks, g_ref, y_ref, col_ref, list_ref):
    count = g_ref.shape[0]
    mask = diagonal()

    def step(item, carry):
        for u in range(4):
            entry = list_ref[0, 1 + item * 4 + u]
            n = entry >> 2
            k = entry & 3
            slot = col_ref[k, n] + LOW
            block = blocks[n, k]
            for r in range(count):
                image = jnp.sum(block * g_ref[r, pl.ds(slot, 1), :], axis=1, keepdims=True)
                y_ref[0][r][n + OFF] = y_ref[0][r][n + OFF] + fold(jnp.where(mask, image, 0.0))
        return carry

    lax.fori_loop(0, (list_ref[0, 0] + 3) >> 2, step, 0)


def pack(y_ref, r):
    sub = lax.broadcasted_iota(jnp.int32, (8, LANES), 0)
    groups = []
    for g in range(ROWS // 8):
        total = jnp.zeros((8, LANES), f32)
        for i in range(8):
            slot = g * 8 + i
            line = y_ref[1][r][slot]
            for k in range(2, K):
                line = line + y_ref[k][r][slot]
            if OFF <= slot < HIGH:
                line = line + y_ref[0][r][slot]
            line = jnp.sum(line, axis=0, keepdims=True)
            total = jnp.where(sub == i, line, total)
        groups.append(total)
    return jnp.concatenate(groups, axis=0)


def unpack_columns(column_ref, square_ref, r):
    for h in range(BS // 32):
        for j in range(4):
            start = 32 * h + 8 * j
            square_ref[pl.ds(32 * h + j, 8, stride=4), :] = column_ref[r, start : start + 8, :]
    square_ref[BS:, :] = jnp.zeros((LANES - BS, LANES), f32)
    return square_ref[...].T[:ROWS]


def messages(up_ref, down_ref, v_ref, send_ref, extra_ref=None):
    for r in range(v_ref.shape[0]):
        for j in range(IF):
            low = pl.ds(send_ref[0, j] + OFF, 1)
            high = pl.ds(send_ref[0, IF + j] + OFF, 1)
            down_ref[r, j : j + 1, :] = v_ref[r, low, :]
            up_ref[r, j : j + 1, :] = v_ref[r, high, :]
            down_ref[r, 8 + j : 9 + j, :] = v_ref[r, LOW + j : LOW + j + 1, :]
            up_ref[r, 8 + j : 9 + j, :] = v_ref[r, HIGH + j : HIGH + j + 1, :]
            if extra_ref is not None:
                down_ref[r, 16 + j : 17 + j, :] = extra_ref[r, low, :]
                up_ref[r, 16 + j : 17 + j, :] = extra_ref[r, high, :]


def complete(v_ref, low_ref, high_ref, send_ref, edge_ref):
    for r in range(v_ref.shape[0]):
        for j in range(IF):
            for part, base, ghost, flag in ((low_ref, 0, LOW, 0), (high_ref, IF, HIGH, 1)):
                at = pl.ds(send_ref[0, base + j] + OFF, 1)
                v_ref[r, at, :] = v_ref[r, at, :] + part[r, 8 + j : 9 + j, :]
                slot = ghost + j
                summed = v_ref[r, slot : slot + 1, :] + part[r, j : j + 1, :]
                v_ref[r, slot : slot + 1, :] = jnp.where(edge_ref[flag] > 0, summed, 0.0)


def tile_sum(first, second):
    prod = first * second
    return jnp.sum(prod.reshape(prod.shape[0] // 8, 8, LANES), axis=0)


def whole_sum(tile):
    return jnp.sum(jnp.sum(tile, axis=0, keepdims=True), axis=1, keepdims=True)


def inner_rows():
    row = lax.broadcasted_iota(jnp.int32, (ROWS, LANES), 0)
    return (row >= OFF) & (row < HIGH)


def pack_kernel(send_ref, raw_ref, stiff_ref, base_ref, up_ref, down_ref):
    vectors = base_ref.shape[0]
    flat = lax.broadcasted_iota(jnp.int32, (CUTS, LANES), 0) * LANES
    flat = (flat + lax.broadcasted_iota(jnp.int32, (CUTS, LANES), 1)).astype(f32)
    step = float(BS + 1)
    mask = jnp.where(flat - step * jnp.floor((flat + 0.5) * (1.0 / step)) == 0.0, 1.0, 0.0)

    def gather(group, carry):
        squares, traces = carry
        for i in range(CUTS):
            tile = raw_ref[pl.ds(pl.multiple_of(group * (8 * CUTS) + 8 * i, 8), 8), :]
            squares = squares + tile * tile
        return squares, traces

    blank = jnp.zeros((8, LANES), f32)
    squares, traces = lax.fori_loop(0, NBLK // CHUNK, gather, (blank, blank))
    for i in range(CHUNK):
        for q in range(0, CUTS, 8):
            start = i * (CUTS * K) + K * q
            traces = traces + mask[q : q + 8] * stiff_ref[pl.ds(start, 8, stride=K), :]
    squares = jnp.sum(squares, axis=0, keepdims=True)
    traces = (NBLK // CHUNK) * jnp.sum(traces, axis=0, keepdims=True)
    for part, ref in ((0, down_ref), (IF, up_ref)):
        for j in range(IF):
            n = send_ref[0, part + j]
            start = (n >> 3) * (8 * CUTS) + (n & 7)
            for i in range(CUTS // 8):
                ref[j, 8 * i : 8 * i + 8, :] = raw_ref[pl.ds(start + 64 * i, 8, stride=8), :]
            ref[j, CUTS:, :] = jnp.zeros((8, LANES), f32)
            weights = unflatten(lambda q: raw_ref[pl.ds(start + 8 * q, 8, stride=24), :])
            for r in range(vectors):
                line = base_ref[r, pl.ds(n + OFF, 1), :]
                ref[j, CUTS + r : CUTS + r + 1, :] = line
                if r < vectors // 2:
                    inside = jnp.sum(weights * line, axis=1, keepdims=True)
                    image = line + jnp.sum(fold(weights * inside), axis=0, keepdims=True)
                    at = CUTS + vectors + r
                    ref[j, at : at + 1, :] = image
        ref[0, CUTS + 6 : CUTS + 7, :] = squares
        ref[0, CUTS + 7 : CUTS + 8, :] = traces


def operator_kernel(raw_ref, ops_ref, gram_ref):
    base = pl.program_id(0) * WIDE
    for i in range(WIDE):
        start = i // 8 * (8 * CUTS) + i % 8
        weights = unflatten(lambda q: raw_ref[pl.ds(start + 8 * q, 8, stride=24), :])
        ops_ref[base + i] = make_operator(weights, gram_ref.at[i & 3])


def blocks_kernel(col_ref, stiff_ref, blocks_ref, list_ref, count_ref):
    base = pl.program_id(0) * CHUNK

    @pl.when(base == 0)
    def _():
        count_ref[0] = 0

    count = count_ref[0]
    for i in range(CHUNK):
        for k in range(K):
            blocks_ref[base + i, k] = unflatten(lambda q: stiff_ref[pl.ds(i * (CUTS * K) + 4 * q + k, 8, stride=12), :])
            col = col_ref[k, base + i]
            list_ref[0, 1 + count] = (base + i) * K + k
            count = count + jnp.where((col < IF) | (col >= IF + NBLK), 1, 0)
    count_ref[0] = count
    list_ref[0, 0] = count
    for u in range(4):
        list_ref[0, 1 + count + u] = 0


def first_kernel(
    col_ref, list_ref, send_ref, count_ref,
    blocks, op_ref, base_ref, low_ref, high_ref,
    zero_ref, a1_ref, a2_ref, up_ref, down_ref,
    y_ref, g_ref,
):
    count = a1_ref.shape[0]
    zero_ref[...] = base_ref[...]
    g_ref[...] = jnp.zeros_like(g_ref)
    row = lax.broadcasted_iota(jnp.int32, (ROWS, LANES), 0)
    dead = (row >= count_ref[0] + OFF) & (row < HIGH)
    for r in range(count):
        zero_ref[r] = jnp.where(dead, 0.0, zero_ref[r])
        for part, first in ((low_ref, LOW), (high_ref, HIGH)):
            for j in range(IF):
                at = slice(first + j, first + j + 1)
                for s in (r, count + r):
                    zero_ref[s, at, :] = part[j, CUTS + s : CUTS + s + 1, :]
                g_ref[r, at, :] = part[j, CUTS + 2 * count + r : CUTS + 2 * count + r + 1, :]
    scatter_apply(blocks, op_ref, zero_ref.at[pl.ds(0, count)], y_ref, col_ref, None)
    ghost_apply(blocks, g_ref, y_ref, col_ref, list_ref)
    inner = inner_rows()
    for r in range(count):
        a1_ref[r] = jnp.where(inner, pack(y_ref, r), 0.0)
    scatter_apply(blocks, op_ref, a1_ref, y_ref, col_ref, None)
    for r in range(count):
        a2_ref[r] = pack(y_ref, r)
    messages(up_ref, down_ref, a2_ref, send_ref, a1_ref)


def operator_rows(op_ref, x_ref, out_ref, column_ref, square_ref):
    column_ref[...] = jnp.zeros_like(column_ref)
    lanes = lane_ids()
    for r in range(column_ref.shape[0]):
        for n in range(NBLK):
            image = jnp.sum(op_ref[n] * x_ref[r, n + OFF : n + OFF + 1, :], axis=1, keepdims=True)
            column_ref[r] = jnp.where(lanes == n + OFF, image, column_ref[r])
        out_ref[r] = unpack_columns(column_ref, square_ref, r)


def ghost_kernel(op_ref, zero_ref, a1_ref, low_ref, high_ref, gop_ref, k0_ref, k1_ref, gram_ref, column_ref, square_ref):
    for part, first in ((low_ref, 0), (high_ref, IF)):
        for j in range(IF):
            weights = unflatten(lambda q: part[j, pl.ds(q, 8, stride=3), :])
            gop_ref[first + j] = make_operator(weights, gram_ref.at[j & 1])
    operator_rows(op_ref, zero_ref, k0_ref, column_ref, square_ref)
    operator_rows(op_ref, a1_ref, k1_ref, column_ref, square_ref)


def target_kernel(col_ref, list_ref, blocks, op_ref, gop_ref, zero_ref, b1_ref, y_ref, g_ref):
    count = b1_ref.shape[0]
    target = zero_ref.at[pl.ds(count, count)]
    scatter_apply(blocks, op_ref, target, y_ref, col_ref, None)
    ghost_images(gop_ref, target, g_ref)
    ghost_apply(blocks, g_ref, y_ref, col_ref, list_ref)
    inner = inner_rows()
    for r in range(count):
        b1_ref[r] = jnp.where(inner, pack(y_ref, r), 0.0)


def second_kernel(
    col_ref, list_ref, send_ref, edge_ref,
    blocks, ops_ref, gop_ref, zero_ref, a1_ref, a2_in, k0_ref, k1_ref, low_ref, high_ref, stats_ref,
    v1_ref, v2_ref, v3_ref, v4_ref, k3_ref, dots_ref, sigma_ref, up_ref, down_ref,
    y_ref, column_ref, square_ref, g_ref,
):
    count = a1_ref.shape[0]
    inner = inner_rows()
    squares, traces = stats_ref[0, :1], stats_ref[0, 1:]
    for s in range(1, stats_ref.shape[0]):
        squares = squares + stats_ref[s, :1]
        traces = traces + stats_ref[s, 1:]
    scale = 1.0 / (lax.axis_size("sub") * NBLK * BS)
    sigma = (1.0 + scale * whole_sum(squares)) * (scale * whole_sum(traces))
    sigma_ref[...] = jnp.broadcast_to(sigma, sigma_ref.shape)
    column_ref[...] = jnp.zeros_like(column_ref)
    v2_ref[...] = a2_in[...]
    complete(v2_ref, low_ref, high_ref, send_ref, edge_ref)
    for r in range(count):
        v1_ref[r] = a1_ref[r]
        for part, ghost, flag in ((low_ref, LOW, 0), (high_ref, HIGH, 1)):
            for j in range(IF):
                v1_ref[r, ghost + j : ghost + j + 1, :] = part[r, 16 + j : 17 + j, :]
        v1 = v1_ref[r] - sigma * zero_ref[r]
        v2_ref[r] = v2_ref[r] - sigma * v1_ref[r] - sigma * v1
        v1 = jnp.where(inner, v1, 0.0)
        v1_ref[r] = v1
        v0 = jnp.where(inner, zero_ref[r], 0.0)
        target = jnp.where(inner, zero_ref[count + r], 0.0)
        second = k1_ref[r] - sigma * k0_ref[r]
        dots_ref[r, 0] = tile_sum(v0, k0_ref[r])
        dots_ref[r, 1] = tile_sum(v1, k0_ref[r])
        dots_ref[r, 2] = tile_sum(v1, second)
        dots_ref[r, 8] = tile_sum(target, k0_ref[r])
        dots_ref[r, 9] = tile_sum(target, second)
    scatter_apply(blocks, ops_ref, v2_ref, y_ref, col_ref, column_ref)
    ghost_images(gop_ref, v2_ref, g_ref)
    ghost_apply(blocks, g_ref, y_ref, col_ref, list_ref)
    for r in range(count):
        image = unpack_columns(column_ref, square_ref, r)
        v3 = jnp.where(inner, pack(y_ref, r) - sigma * v2_ref[r], 0.0)
        v3_ref[r] = v3
        dots_ref[r, 3] = tile_sum(v1_ref[r], image)
        dots_ref[r, 4] = tile_sum(jnp.where(inner, v2_ref[r], 0.0), image)
        dots_ref[r, 5] = tile_sum(v3, image)
        dots_ref[r, 10] = tile_sum(jnp.where(inner, zero_ref[count + r], 0.0), image)
    scatter_apply(blocks, ops_ref, v3_ref, y_ref, col_ref, column_ref)
    for r in range(count):
        image = unpack_columns(column_ref, square_ref, r)
        dots_ref[r, 6] = tile_sum(v3_ref[r], image)
        dots_ref[r, 7] = jnp.zeros((8, LANES), f32)
        dots_ref[r, 11] = tile_sum(jnp.where(inner, zero_ref[count + r], 0.0), image)
        k3_ref[r] = image
        v4_ref[r] = pack(y_ref, r) - sigma * v3_ref[r]
    messages(up_ref, down_ref, v4_ref, send_ref)


def moment_kernel(send_ref, edge_ref, v4_in, k3_ref, low_ref, high_ref, dots_in, v4_ref, dots_ref):
    v4_ref[...] = v4_in[...]
    complete(v4_ref, low_ref, high_ref, send_ref, edge_ref)
    lane = lax.broadcasted_iota(jnp.int32, (8, LANES), 1)
    sub = lax.broadcasted_iota(jnp.int32, (8, LANES), 0)
    total = jnp.zeros((8, LANES), f32)
    for r in range(v4_ref.shape[0]):
        for d in range(12):
            part = tile_sum(v4_ref[r], k3_ref[r]) if d == 7 else dots_in[r, d]
            total = jnp.where((lane == d) & (sub == r), whole_sum(part), total)
    dots_ref[...] = total


def third_kernel(col_ref, list_ref, blocks, ops_ref, gop_ref, v4_ref, w5_ref, y_ref, g_ref):
    scatter_apply(blocks, ops_ref, v4_ref, y_ref, col_ref, None)
    ghost_images(gop_ref, v4_ref, g_ref)
    ghost_apply(blocks, g_ref, y_ref, col_ref, list_ref)
    for r in range(v4_ref.shape[0]):
        w5_ref[r] = pack(y_ref, r)


def combine(coef_ref, parts, g, r):
    total = None
    for s in USED[g]:
        term = coef_ref[g, s, r : r + 1, :] * parts[s]
        total = term if total is None else total + term
    return total


def sources(zero_ref, stored, r, count):
    v1_ref, v2_ref, v3_ref, v4_ref, w5_ref, b1_ref = stored
    parts = [zero_ref[r], v1_ref[r], v2_ref[r], v3_ref[r], v4_ref[r], w5_ref[r], zero_ref[count + r], b1_ref[r]]
    inner = inner_rows()
    return [jnp.where(inner, part, 0.0) for part in parts]


def fourth_kernel(col_ref, send_ref, blocks, ops_ref, sigma_ref, zero_ref, *refs):
    stored, sums = refs[:6], [part[...] for part in refs[6:-8]]
    first_ref, base_ref, rho_ref, coef_ref, scale_ref, up_ref, down_ref, y_ref = refs[-8:]
    while len(sums) > 1:
        sums = [sums[i] + sums[i + 1] for i in range(0, len(sums), 2)]
    sums = sums[0]
    column = lambda d: jnp.broadcast_to(sums[:, d : d + 1], (8, LANES))
    combos, scales = scalars([column(d) for d in range(8)], [column(8 + d) for d in range(4)], sigma_ref[...])
    for g, value in enumerate(scales):
        scale_ref[g] = value
    for g, combo in enumerate(combos):
        for s, value in enumerate(combo):
            if s in USED[g]:
                coef_ref[g, s] = value
    count = rho_ref.shape[0]
    for r in range(count):
        parts = sources(zero_ref, stored, r, count)
        first_ref[r] = combine(coef_ref, parts, 5, r)
        base_ref[r] = combine(coef_ref, parts, 7, r)
    scatter_apply(blocks, ops_ref, first_ref, y_ref, col_ref, None)
    for r in range(count):
        rho_ref[r] = base_ref[r] - scale_ref[0, r : r + 1, :] * pack(y_ref, r)
    messages(up_ref, down_ref, rho_ref, send_ref)


def early_kernel(coef_ref, zero_ref, *refs):
    stored, early_ref = refs[:6], refs[6]
    count = zero_ref.shape[0] // 2
    for r in range(count):
        parts = sources(zero_ref, stored, r, count)
        early_ref[pl.ds(r, NBLK, stride=EARLY), :] = parts[0][OFF:HIGH]
        for g, slot in ((0, 2), (1, 4), (2, 6), (4, 12), (3, 14)):
            early_ref[pl.ds(slot + r, NBLK, stride=EARLY), :] = combine(coef_ref, parts, g, r)[OFF:HIGH]
        for slot in (8, 10):
            early_ref[pl.ds(slot + r, NBLK, stride=EARLY), :] = jnp.zeros((NBLK, LANES), f32)


def answer_kernel(ops_ref, coef_ref, zero_ref, *refs):
    stored, (zeta_ref, sol_ref, x_ref, column_ref, square_ref) = refs[:6], refs[6:]
    count = zeta_ref.shape[1]
    for r in range(count):
        parts = sources(zero_ref, stored, r, count)
        zeta_ref[0, r] = combine(coef_ref, parts, 8, r)
        zeta_ref[1, r] = combine(coef_ref, parts, 6, r)
        x_ref[r] = combine(coef_ref, parts, 9, r)
    operator_rows(ops_ref, x_ref, sol_ref, column_ref, square_ref)


def fifth_kernel(
    col_ref, list_ref, send_ref, edge_ref,
    blocks, ops_ref, gop_ref, rho_in, base_ref, zeta_ref, scale_ref, low_ref, high_ref,
    late_ref, y_ref, rho_ref, g_ref,
):
    count = rho_in.shape[0]
    rho_ref[...] = rho_in[...]
    complete(rho_ref, low_ref, high_ref, send_ref, edge_ref)
    scatter_apply(blocks, ops_ref, rho_ref, y_ref, col_ref, None)
    ghost_images(gop_ref, rho_ref, g_ref)
    ghost_apply(blocks, g_ref, y_ref, col_ref, list_ref)
    for r in range(count):
        change = rho_ref[r] - base_ref[r]
        first = zeta_ref[0, r] + scale_ref[1, r : r + 1, :] * change - scale_ref[2, r : r + 1, :] * pack(y_ref, r)
        second = zeta_ref[1, r] + change
        late_ref[pl.ds(r, NBLK, stride=LATE), :] = first[OFF:HIGH]
        late_ref[pl.ds(2 + r, NBLK, stride=LATE), :] = second[OFF:HIGH]


def split(value):
    high = value.astype(jnp.bfloat16)
    return high, (value - high.astype(f32)).astype(jnp.bfloat16)


def product(first, second, dim):
    (fh, fl), (sh, sl) = split(first), split(second)
    left = jnp.concatenate([fh, fl, fh], axis=dim)
    right = jnp.concatenate([sh, sh, sl], axis=0)
    return lax.dot_general(left, right, (((dim,), (0,)), ((), ())), preferred_element_type=f32)


def mixed_kernel(*refs):
    early, (raw_ref, mixed_ref, weights_ref) = refs[:-3], refs[-3:]

    def step(group, carry):
        for i in range(CHUNK):
            at = pl.multiple_of((group * CHUNK + i) * EARLY, EARLY)
            resid = [ref[pl.ds(at, 8), :] for ref in early]
            zeta = [ref[pl.ds(at + 8, 8), :] for ref in early]
            left = jnp.concatenate(resid + zeta, axis=0)
            right = jnp.concatenate(zeta + resid, axis=0)
            mixed_ref[group * CHUNK + i] = product(left, right, 0)
            start = group * (8 * CUTS) + i
            weights_ref[group * CHUNK + i] = unflatten(lambda q: raw_ref[pl.ds(start + 8 * q, 8, stride=24), :])
        return carry

    lax.fori_loop(0, NBLK // CHUNK, step, 0)


def grad_kernel(*refs):
    peers = (len(refs) - 3) // 2
    early, late, mixed_ref, weights_ref, grad_ref = refs[:peers], refs[peers : 2 * peers], *refs[-3:]
    first = pl.program_id(0) * WIDE
    upper = lax.broadcasted_iota(jnp.int32, (8, LANES), 0) < LATE

    def join(tiles):
        out = []
        for q in range(0, len(tiles), 2):
            other = pltpu.roll(tiles[q + 1], LATE, 0) if q + 1 < len(tiles) else jnp.zeros((8, LANES), f32)
            out.append(jnp.where(upper, tiles[q], other))
        return out

    for i in range(WIDE):
        n = first + i
        at = pl.multiple_of(n * EARLY, EARLY)
        pair = pl.ds(pl.multiple_of(first * LATE + 8 * (i // 2), 8), 8)
        resid = join([ref[pl.ds(at, 8), :] for ref in early])
        zeta = [ref[pair, :] for ref in late]
        zeta = join([pltpu.roll(tile, LATE, 0) for tile in zeta] if i % 2 else zeta)
        left = jnp.concatenate(resid + zeta, axis=0)
        right = jnp.concatenate(zeta + resid, axis=0)
        grad = product(weights_ref[i], mixed_ref[n] + product(left, right, 0), 1)

        def write(q, value):
            grad_ref[pl.ds(i // 8 * (8 * CUTS) + 8 * q + i % 8, 8, stride=24), :] = value

        flatten(grad, write)


def widening(parts, axis, step, most):
    if step is None:
        return parts, None
    size = lax.axis_size(axis)
    if size & (size - 1):
        return [lax.psum(parts[0], axis)], None
    step = step or 1
    while len(parts) > 1:
        parts = [parts[i] + parts[i + 1] for i in range(0, len(parts), 2)]
    width = min(most, size // step)
    total = parts[0]
    parts = [total] + [lax.ppermute(total, axis, [(i, i ^ (d * step)) for i in range(size)]) for d in range(1, width)]
    step *= width
    return parts, step if step < size else None


def all_of(values, axis):
    size = lax.axis_size(axis)
    return [values] + [
        lax.ppermute(values, axis, [(i, (i + d) % size) for i in range(size)]) for d in range(1, size)
    ]


def exchange(up, down):
    size = lax.axis_size("sub")
    rising = [(i, i + 1) for i in range(size - 1)]
    falling = [(j, i) for i, j in rising]
    return lax.ppermute(up, "sub", rising), lax.ppermute(down, "sub", falling)


def plus(first, second):
    if first is None:
        return second
    return first if second is None else first + second


def times(first, second):
    return None if first is None or second is None else first * second


def add(first, second, scale):
    size = max(len(first), len(second))
    first = list(first) + [None] * (size - len(first))
    second = list(second) + [None] * (size - len(second))
    return [plus(a, times(scale, b)) for a, b in zip(first, second)]


def scaled(first, scale):
    return [times(scale, a) for a in first]


def scalars(moments, products, sigma):
    one = jnp.ones_like(sigma)

    def inner(first, second):
        weights = [None] * (len(first) + len(second) - 1)
        for i, a in enumerate(first):
            for j, b in enumerate(second):
                weights[i + j] = plus(weights[i + j], a * b)
        total = None
        for weight, moment in zip(weights, moments):
            total = plus(total, weight * moment)
        return total

    def apply(poly):
        out = [None] * (len(poly) + 1)
        for j, value in enumerate(poly):
            out[j] = plus(out[j], sigma * value)
            out[j + 1] = plus(out[j + 1], value)
        return out

    resid = [[one]]
    direc = [[one]]
    image = []
    step, ratio, norm, curv = [], [None], [moments[0]], []
    for i in range(ITERS):
        image.append(apply(direc[i]))
        curv.append(inner(direc[i], image[i]))
        step.append(norm[i] / curv[i])
        if i + 1 < ITERS:
            resid.append(add(resid[i], image[i], -step[i]))
            norm.append(inner(resid[i + 1], resid[i + 1]))
            ratio.append(norm[i + 1] / norm[i])
            direc.append(add(resid[i + 1], direc[i], ratio[i + 1]))
    cot = []
    for i in range(ITERS):
        total = None
        for j, value in enumerate(resid[i]):
            total = plus(total, value * products[j])
        cot.append(total)
    along = [cot[0]]
    for i in range(1, ITERS):
        along.append(cot[i] + ratio[i] * along[i - 1])

    def row(poly):
        return list(poly) + [None] * (8 - len(poly))

    target = [None] * 6 + [one, None]
    resid_rows = [row(poly) for poly in resid]
    image_rows = [row(poly) for poly in image]
    inverse = [1.0 / value for value in step]

    def resid_prod(i):
        return [norm[l] if l == i else None for l in range(ITERS)]

    def image_prod(i):
        out = [None] * ITERS
        out[i] = norm[i] * inverse[i]
        if i + 1 < ITERS:
            out[i + 1] = -norm[i + 1] * inverse[i]
        return out

    def along_dir(prod, i):
        total = prod[0]
        for l in range(1, i + 1):
            total = plus(prod[l], times(ratio[l], total))
        return total

    def operator_prod(prod):
        out = []
        for l in range(ITERS - 1):
            value = times(add([prod[l]], [prod[l + 1]], -one)[0], inverse[l])
            if l > 0:
                back = times(add([prod[l - 1]], [prod[l]], -one)[0], inverse[l - 1])
                value = add([value], [back], -ratio[l])[0]
            out.append(value)
        return out + [None]

    last = ITERS - 1
    step_bar = along[last]
    curv_bar = -step_bar * step[last] / curv[last]
    dir_row = add(scaled(target, step[last]), image_rows[last], 2 * curv_bar)
    dir_prod = add(scaled(cot, step[last]), image_prod(last), 2 * curv_bar)
    norm_bar = step_bar / curv[last]
    rho_row = [None] * 8
    rho_prod = [None] * ITERS
    zetas = [None] * ITERS
    rho_rows = []
    for i in (2, 1, 0):
        ratio_bar = along_dir(dir_prod, i)
        full = norm_bar + ratio_bar / norm[i]
        zetas[i + 1] = add(dir_row, resid_rows[i + 1], full)
        rho_row = add(add(rho_row, zetas[i + 1], one), resid_rows[i + 1], full)
        rho_prod = add(add(rho_prod, dir_prod, one), resid_prod(i + 1), 2 * full)
        rho_rows.append(rho_row)
        step_bar = along[i] - (rho_prod[i] - rho_prod[i + 1]) * inverse[i]
        curv_bar = -step_bar * step[i] / curv[i]
        oper = [None] * 8
        if i == 2:
            for k in range(5):
                if k < 4:
                    oper[k] = plus(oper[k], times(sigma, rho_row[k]))
                    oper[k + 1] = plus(oper[k + 1], rho_row[k])
                else:
                    oper[5] = plus(oper[5], rho_row[4])
            oper[7] = rho_row[6]
        kept = add(scaled(dir_row, ratio[i + 1]), target, step[i])
        kept = add(kept, image_rows[i], 2 * curv_bar)
        dir_row = add(kept, oper, -step[i])
        dir_prod = add(add(scaled(dir_prod, ratio[i + 1]), cot, step[i]), image_prod(i), 2 * curv_bar)
        dir_prod = add(dir_prod, operator_prod(rho_prod), -step[i])
        norm_bar = step_bar / curv[i] - ratio_bar * norm[i + 1] / (norm[i] * norm[i])
    zetas[0] = add(dir_row, resid_rows[0], norm_bar)
    answer = [None] * 8
    for i in range(ITERS):
        answer = add(answer, row(direc[i]), step[i])
    combos = [resid_rows[1], resid_rows[2], resid_rows[3], zetas[3], zetas[2], rho_rows[1], zetas[1], rho_rows[2], zetas[0], answer]
    return combos, [step[1], ratio[1], step[0]]


def vmem():
    return pl.BlockSpec(memory_space=pltpu.VMEM)


def hbm():
    return pl.BlockSpec(memory_space=pltpu.HBM)


def smem():
    return pl.BlockSpec(memory_space=pltpu.SMEM)


def shards(stiffness, precond, rhs_vec, cotangent, col_index, send_rows, counts):
    count = rhs_vec.shape[0]
    sub = lax.axis_index("sub")
    size = lax.axis_size("sub")
    edge = jnp.stack([sub > 0, sub + 1 < size]).astype(jnp.int32)
    columns = col_index.T
    stiff_cuts = stiffness.reshape(NBLK, K, CUTS, LANES).transpose(0, 2, 1, 3).reshape(NBLK * K * CUTS, LANES)
    weight_cuts = precond.reshape(NBLK // 8, 8, CUTS, LANES).transpose(0, 2, 1, 3).reshape(NBLK * CUTS, LANES)
    base = jnp.concatenate([rhs_vec, cotangent], axis=0).reshape(2 * count, NBLK, BS)
    base = jnp.pad(base, ((0, 0), (OFF, ROWS - HIGH), (0, LANES - BS)))

    def shape(*dims):
        return jax.ShapeDtypeStruct(dims, f32)

    def call(kernel, name, scalars_in, arrays_in, outs, scratch, expected, specs=None, grid=(), in_specs=None):
        return pl.pallas_call(
            kernel,
            grid=grid,
            in_specs=in_specs or [smem()] * len(scalars_in) + [vmem()] * len(arrays_in),
            out_specs=specs or [vmem()] * len(outs),
            out_shape=outs,
            scratch_shapes=scratch,
            compiler_params=pltpu.CompilerParams(vmem_limit_bytes=8 * MIB),
            cost_estimate=pl.CostEstimate(flops=MIB, bytes_accessed=int(expected * 3.2e6), transcendentals=0),
            name=name,
        )(*scalars_in, *arrays_in)

    rows = shape(count, ROWS, LANES)
    message = shape(count, 16, LANES)
    longer = shape(count, 24, LANES)
    ghost_message = shape(IF, CUTS + 8, LANES)
    partial = lambda r: [[pltpu.VMEM((ROWS, 8, LANES), f32)] * r] * K
    turned = [pltpu.VMEM((count, BS, LANES), f32), pltpu.VMEM((LANES, LANES), f32)]
    held = lambda r: pltpu.VMEM((r, ROWS, LANES), f32)
    grams = pltpu.VMEM((4, BS, LANES), f32)

    up, down = call(
        pack_kernel, "pack", [send_rows], [weight_cuts, lax.slice_in_dim(stiff_cuts, 0, CHUNK * CUTS * K), base], [ghost_message] * 2, [], 3
    )
    near, far = exchange(up, down)

    (ops,) = call(
        operator_kernel, "operators", [], [weight_cuts], [shape(NBLK, BS, LANES)],
        [grams], 4, [vmem()], (NBLK // WIDE,),
        [pl.BlockSpec((WIDE * CUTS, LANES), lambda g: (g, 0))],
    )
    stats, partner = up[0, CUTS + 6 :], jnp.where(sub % 2 == 0, far[0, CUTS + 6 :], near[0, CUTS + 6 :])
    if size > 1 and size & (size - 1) == 0:
        stats, waiting = [stats + partner], 2
    else:
        stats, waiting = [stats], 0
    stats, near, far, ops = lax.optimization_barrier((stats, near, far, ops))
    while waiting is not None and waiting < size:
        stats, waiting = widening(stats, "sub", waiting, 4)
    blocks, halo_list = call(
        blocks_kernel, "blocks", [columns], [stiff_cuts],
        [shape(NBLK, K, BS, LANES), jax.ShapeDtypeStruct((1, NBLK * K + 8), jnp.int32)],
        [pltpu.SMEM((1,), jnp.int32)], 5, [vmem(), smem()], (NBLK // CHUNK,),
        [smem(), pl.BlockSpec((CHUNK * CUTS * K, LANES), lambda g: (g, 0))],
    )

    zero, a1, a2, up, down = call(
        first_kernel, "first", [columns, halo_list, send_rows, counts], [blocks, ops, base, near, far],
        [shape(2 * count, ROWS, LANES), rows, rows, longer, longer],
        [partial(count), held(count)], 6,
    )
    low, high = exchange(up, down)
    stats = jnp.stack(stats)

    gops, k0, k1 = call(
        ghost_kernel, "ghosts", [], [ops, zero, a1, near, far],
        [shape(2 * IF, BS, LANES), rows, rows], [grams, *turned], 3,
    )

    v1, v2, v3, v4, k3, dots, sigma, up, down = call(
        second_kernel, "second", [columns, halo_list, send_rows, edge],
        [blocks, ops, gops, zero, a1, a2, k0, k1, low, high, stats],
        [rows, rows, rows, rows, rows, shape(count, 12, 8, LANES), shape(8, LANES), message, message],
        [partial(count), *turned, held(count)], 7,
    )
    low, high = exchange(up, down)

    v4, dots = call(
        moment_kernel, "moments", [send_rows, edge], [v4, k3, low, high, dots], [rows, shape(8, LANES)], [], 0.8
    )
    sums, waiting = widening([dots], "sub", 0, 2)
    zero, v4 = lax.optimization_barrier((zero, v4))
    (b1,) = call(
        target_kernel, "target", [columns, halo_list], [blocks, ops, gops, zero], [rows],
        [partial(count), held(count)], 3,
    )
    sums, b1, v4 = lax.optimization_barrier((sums, b1, v4))
    while waiting is not None:
        sums, waiting = widening(sums, "sub", waiting, 4)

    (w5,) = call(
        third_kernel, "third", [columns, halo_list], [blocks, ops, gops, v4], [rows],
        [partial(count), held(count)], 4,
    )

    stored = [zero, v1, v2, v3, v4, w5, b1]
    first, fixed, rho, coefs, scales, up, down = call(
        fourth_kernel, "fourth", [columns, send_rows], [blocks, ops, sigma, *stored, *sums],
        [rows, rows, rows, shape(10, 8, 8, LANES), shape(3, 8, LANES), message, message], [partial(count)], 3,
    )
    (early,) = call(early_kernel, "early", [], [coefs, *stored], [shape(NBLK * EARLY, LANES)], [], 0.5)
    size = lax.axis_size("rhs")
    early = [early]
    if size == 4:
        early.append(lax.ppermute(early[0], "rhs", [(i, i ^ 2) for i in range(size)]))
    low, high = exchange(up, down)

    zeta, answer = call(
        answer_kernel, "answer", [], [ops, coefs, *stored],
        [shape(2, count, ROWS, LANES), rows], [held(count), *turned], 1.5,
    )
    early, low, high, zeta = lax.optimization_barrier((early, low, high, zeta))
    if size == 4:
        early = early + [lax.ppermute(part, "rhs", [(i, i ^ 1) for i in range(size)]) for part in early]
    else:
        early = all_of(early[0], "rhs")

    (late,) = call(
        fifth_kernel, "fifth", [columns, halo_list, send_rows, edge],
        [blocks, ops, gops, rho, fixed, zeta, scales, low, high],
        [shape(NBLK * LATE, LANES)], [partial(count), held(count), held(count)], 4,
    )
    if size == 4:
        late = [late] + [lax.ppermute(late, "rhs", [(i, i ^ d) for i in range(size)]) for d in (2, 1, 3)]
    else:
        late = all_of(late, "rhs")

    mixed, weights = call(
        mixed_kernel, "mixed", [], [*early, weight_cuts], [shape(NBLK, LANES, LANES), shape(NBLK, BS, LANES)], [], 3
    )
    (grad,) = call(
        grad_kernel, "grad", [], [*early, *late, mixed, weights], [shape(NBLK * CUTS, LANES)], [], 10,
        [pl.BlockSpec((WIDE * CUTS, LANES), lambda g: (g, 0))], (NBLK // WIDE,),
        [vmem()] * (len(early) + len(late) + 1) + [pl.BlockSpec((WIDE, BS, LANES), lambda g: (g, 0, 0))],
    )
    grad = grad.reshape(NBLK // 8, CUTS, 8, LANES).transpose(0, 2, 1, 3).reshape(NBLK, BS * BS)
    return answer[:, OFF:HIGH, :BS].reshape(count, NBLK * BS), grad


def solution(mesh):
    in_specs = (
        P("sub", None, None),
        P("sub", None),
        P("rhs", "sub"),
        P("rhs", "sub"),
        P("sub", None),
        P("sub", None),
        P("sub"),
    )
    out_specs = (P("rhs", "sub"), P("sub", None))
    return jax.shard_map(shards, mesh=mesh, in_specs=in_specs, out_specs=out_specs, check_vma=False)
```

```python
import functools

import jax
import jax.numpy as jnp
from jax import lax
from jax.experimental import pallas as pl
from jax.experimental.pallas import tpu as pltpu
from jax.sharding import PartitionSpec as P

BS = 96
K = 4
NBLK = 48
IF = 6
ITERS = 4
ALL = (0, 1, 2, 3, 4, 5, 6, 7)
USED = ((0, 1), (0, 1, 2), (0, 1, 2, 3), (0, 1, 2, 3, 4, 6), ALL, ALL, ALL, ALL, ALL, (0, 1, 2, 3))
EARLY = 16
LATE = 4
CUTS = BS * BS // 128
SPAN = 24
WIDE = 16
LANES = 128
OFF = 8
ROWS = 64
LOW = OFF - IF
HIGH = OFF + NBLK
CHUNK = 8
MIB = 1024 * 1024

highest = lax.Precision.HIGHEST
f32 = jnp.float32


def own(value):
    return value[:, OFF:HIGH]


def lane_ids():
    return lax.broadcasted_iota(jnp.int32, (BS, LANES), 1)


def diagonal():
    pos = lax.broadcasted_iota(jnp.int32, (BS, LANES), 0)
    row = (pos & ~31) + 4 * (pos & 7) + ((pos >> 3) & 3)
    return row == lane_ids()


def fold(prod):
    return jnp.sum(prod.reshape(BS // 8, 8, prod.shape[-1]), axis=0)


def unflatten(read):
    lane = lax.broadcasted_iota(jnp.int32, (8, LANES), 1)
    out = []
    for h in range(BS // 32):
        one, two, three = (read(24 * h + m) for m in range(3))
        out.append(jnp.where(lane < BS, one, 0.0))
        mixed = jnp.where(lane < 32, pltpu.roll(one, 32, 1), pltpu.roll(two, 32, 1))
        out.append(jnp.where(lane < BS, mixed, 0.0))
        mixed = jnp.where(lane < 64, pltpu.roll(two, 64, 1), pltpu.roll(three, 64, 1))
        out.append(jnp.where(lane < BS, mixed, 0.0))
        out.append(jnp.where(lane < BS, pltpu.roll(three, 96, 1), 0.0))
    return jnp.concatenate(out, axis=0)


def flatten(block):
    lane = lax.broadcasted_iota(jnp.int32, (8, LANES), 1)
    out = []
    for h in range(BS // 32):
        one, two, three, four = (block[32 * h + 8 * j : 32 * h + 8 * j + 8] for j in range(4))
        two = pltpu.roll(two, 96, 1)
        three = pltpu.roll(three, 64, 1)
        out.append(jnp.where(lane < BS, one, two))
        out.append(jnp.where(lane < 64, two, three))
        out.append(jnp.where(lane < 32, three, pltpu.roll(four, 32, 1)))
    return out


def make_operator(weights, gram_ref):
    gram = lax.dot_general(
        weights, weights, (((0,), (0,)), ((), ())), precision=highest, preferred_element_type=f32
    )
    gram_ref[...] = gram[:BS]
    rows = [gram_ref[pl.ds(32 * h + j, 8, stride=4), :] for h in range(BS // 32) for j in range(4)]
    return jnp.concatenate(rows, axis=0) + jnp.where(diagonal(), 1.0, 0.0)


def scatter_apply(blocks, op_ref, x_ref, y_ref, col_ref, column_ref):
    count = x_ref.shape[0]
    for k in range(1, K):
        for r in range(count):
            y_ref[k][r][...] = jnp.zeros_like(y_ref[k][r])

    def step(group, carry):
        base = pl.multiple_of(group * SPAN, CHUNK)
        tiles = [x_ref[r, pl.ds(base + OFF, SPAN), :] for r in range(count)]
        for i in range(SPAN):
            n = group * SPAN + i
            oper = op_ref[n]
            images = [jnp.sum(oper * tiles[r][i : i + 1, :], axis=1, keepdims=True) for r in range(count)]
            if column_ref is not None:
                for r in range(count):
                    column_ref[r] = jnp.where(lane_ids() == n + OFF, images[r], column_ref[r])
            for k in range(K):
                block = blocks[n, k]
                slot = n + OFF if k == 0 else col_ref[k, n] + LOW
                for r in range(count):
                    part = fold(block * images[r])
                    y_ref[k][r][slot] = part if k == 0 else y_ref[k][r][slot] + part
        return carry

    lax.fori_loop(0, NBLK // SPAN, step, 0)


def ghost_images(op_ref, x_ref, g_ref):
    count = x_ref.shape[0]
    mask = diagonal()
    g_ref[...] = jnp.zeros_like(g_ref)
    for first, side in ((LOW, 0), (HIGH, IF)):
        for j in range(IF):
            slot = first + j
            oper = op_ref[side + j]
            for r in range(count):
                image = jnp.sum(oper * x_ref[r, slot : slot + 1, :], axis=1, keepdims=True)
                line = jnp.sum(fold(jnp.where(mask, image, 0.0)), axis=0, keepdims=True)
                g_ref[r, slot : slot + 1, :] = line


def ghost_apply(blocks, g_ref, y_ref, col_ref, list_ref):
    count = g_ref.shape[0]
    mask = diagonal()

    def step(item, carry):
        for u in range(4):
            entry = list_ref[0, 1 + item * 4 + u]
            n = entry >> 2
            k = entry & 3
            slot = col_ref[k, n] + LOW
            block = blocks[n, k]
            for r in range(count):
                image = jnp.sum(block * g_ref[r, pl.ds(slot, 1), :], axis=1, keepdims=True)
                y_ref[0][r][n + OFF] = y_ref[0][r][n + OFF] + fold(jnp.where(mask, image, 0.0))
        return carry

    lax.fori_loop(0, (list_ref[0, 0] + 3) >> 2, step, 0)


def pack(y_ref, r):
    sub = lax.broadcasted_iota(jnp.int32, (8, LANES), 0)
    groups = []
    for g in range(ROWS // 8):
        total = jnp.zeros((8, LANES), f32)
        for i in range(8):
            slot = g * 8 + i
            line = y_ref[1][r][slot]
            for k in range(2, K):
                line = line + y_ref[k][r][slot]
            if OFF <= slot < HIGH:
                line = line + y_ref[0][r][slot]
            line = jnp.sum(line, axis=0, keepdims=True)
            total = jnp.where(sub == i, line, total)
        groups.append(total)
    return jnp.concatenate(groups, axis=0)


def unpack_columns(column_ref, square_ref, r):
    for h in range(BS // 32):
        for j in range(4):
            start = 32 * h + 8 * j
            square_ref[pl.ds(32 * h + j, 8, stride=4), :] = column_ref[r, start : start + 8, :]
    square_ref[BS:, :] = jnp.zeros((LANES - BS, LANES), f32)
    return square_ref[...].T[:ROWS]


def messages(up_ref, down_ref, v_ref, send_ref, extra_ref=None):
    for r in range(v_ref.shape[0]):
        for j in range(IF):
            low = pl.ds(send_ref[0, j] + OFF, 1)
            high = pl.ds(send_ref[0, IF + j] + OFF, 1)
            down_ref[r, j : j + 1, :] = v_ref[r, low, :]
            up_ref[r, j : j + 1, :] = v_ref[r, high, :]
            down_ref[r, 8 + j : 9 + j, :] = v_ref[r, LOW + j : LOW + j + 1, :]
            up_ref[r, 8 + j : 9 + j, :] = v_ref[r, HIGH + j : HIGH + j + 1, :]
            if extra_ref is not None:
                down_ref[r, 16 + j : 17 + j, :] = extra_ref[r, low, :]
                up_ref[r, 16 + j : 17 + j, :] = extra_ref[r, high, :]


def complete(v_ref, low_ref, high_ref, send_ref, edge_ref):
    for r in range(v_ref.shape[0]):
        for j in range(IF):
            for part, base, ghost, flag in ((low_ref, 0, LOW, 0), (high_ref, IF, HIGH, 1)):
                at = pl.ds(send_ref[0, base + j] + OFF, 1)
                v_ref[r, at, :] = v_ref[r, at, :] + part[r, 8 + j : 9 + j, :]
                slot = ghost + j
                summed = v_ref[r, slot : slot + 1, :] + part[r, j : j + 1, :]
                v_ref[r, slot : slot + 1, :] = jnp.where(edge_ref[flag] > 0, summed, 0.0)


def tile_sum(first, second):
    prod = first * second
    return jnp.sum(prod.reshape(prod.shape[0] // 8, 8, LANES), axis=0)


def whole_sum(tile):
    return jnp.sum(jnp.sum(tile, axis=0, keepdims=True), axis=1, keepdims=True)


def inner_rows():
    row = lax.broadcasted_iota(jnp.int32, (ROWS, LANES), 0)
    return (row >= OFF) & (row < HIGH)


def pack_kernel(send_ref, raw_ref, stiff_ref, base_ref, up_ref, down_ref):
    vectors = base_ref.shape[0]
    flat = lax.broadcasted_iota(jnp.int32, (CUTS, LANES), 0) * LANES
    flat = (flat + lax.broadcasted_iota(jnp.int32, (CUTS, LANES), 1)).astype(f32)
    step = float(BS + 1)
    mask = jnp.where(flat - step * jnp.floor((flat + 0.5) * (1.0 / step)) == 0.0, 1.0, 0.0)

    def gather(group, carry):
        squares, traces = carry
        for i in range(CUTS):
            tile = raw_ref[pl.ds(pl.multiple_of(group * (8 * CUTS) + 8 * i, 8), 8), :]
            squares = squares + tile * tile
        return squares, traces

    blank = jnp.zeros((8, LANES), f32)
    squares, traces = lax.fori_loop(0, NBLK // CHUNK, gather, (blank, blank))
    for i in range(CHUNK):
        for q in range(0, CUTS, 8):
            start = i * (CUTS * K) + K * q
            traces = traces + mask[q : q + 8] * stiff_ref[pl.ds(start, 8, stride=K), :]
    squares = jnp.sum(squares, axis=0, keepdims=True)
    traces = (NBLK // CHUNK) * jnp.sum(traces, axis=0, keepdims=True)
    for part, ref in ((0, down_ref), (IF, up_ref)):
        for j in range(IF):
            n = send_ref[0, part + j]
            start = (n >> 3) * (8 * CUTS) + (n & 7)
            for i in range(CUTS // 8):
                ref[j, 8 * i : 8 * i + 8, :] = raw_ref[pl.ds(start + 64 * i, 8, stride=8), :]
            ref[j, CUTS:, :] = jnp.zeros((8, LANES), f32)
            weights = unflatten(lambda q: raw_ref[pl.ds(start + 8 * q, 8, stride=24), :])
            for r in range(vectors):
                line = base_ref[r, pl.ds(n + OFF, 1), :]
                ref[j, CUTS + r : CUTS + r + 1, :] = line
                if r < vectors // 2:
                    inside = jnp.sum(weights * line, axis=1, keepdims=True)
                    image = line + jnp.sum(fold(weights * inside), axis=0, keepdims=True)
                    at = CUTS + vectors + r
                    ref[j, at : at + 1, :] = image
        ref[0, CUTS + 6 : CUTS + 7, :] = squares
        ref[0, CUTS + 7 : CUTS + 8, :] = traces


def operator_kernel(raw_ref, ops_ref, gram_ref):
    base = pl.program_id(0) * WIDE
    for i in range(WIDE):
        start = i // 8 * (8 * CUTS) + i % 8
        weights = unflatten(lambda q: raw_ref[pl.ds(start + 8 * q, 8, stride=24), :])
        ops_ref[base + i] = make_operator(weights, gram_ref.at[i & 3])


def blocks_kernel(col_ref, stiff_ref, blocks_ref, list_ref, count_ref):
    base = pl.program_id(0) * CHUNK

    @pl.when(base == 0)
    def _():
        count_ref[0] = 0

    count = count_ref[0]
    for i in range(CHUNK):
        for k in range(K):
            blocks_ref[base + i, k] = unflatten(lambda q: stiff_ref[pl.ds(i * (CUTS * K) + 4 * q + k, 8, stride=12), :])
            col = col_ref[k, base + i]
            list_ref[0, 1 + count] = (base + i) * K + k
            count = count + jnp.where((col < IF) | (col >= IF + NBLK), 1, 0)
    count_ref[0] = count
    list_ref[0, 0] = count
    for u in range(4):
        list_ref[0, 1 + count + u] = 0


def first_kernel(
    col_ref, list_ref, send_ref, count_ref,
    blocks, op_ref, base_ref, low_ref, high_ref,
    zero_ref, a1_ref, a2_ref, up_ref, down_ref,
    y_ref, g_ref,
):
    count = a1_ref.shape[0]
    zero_ref[...] = base_ref[...]
    g_ref[...] = jnp.zeros_like(g_ref)
    row = lax.broadcasted_iota(jnp.int32, (ROWS, LANES), 0)
    dead = (row >= count_ref[0] + OFF) & (row < HIGH)
    for r in range(count):
        zero_ref[r] = jnp.where(dead, 0.0, zero_ref[r])
        for part, first in ((low_ref, LOW), (high_ref, HIGH)):
            for j in range(IF):
                at = slice(first + j, first + j + 1)
                for s in (r, count + r):
                    zero_ref[s, at, :] = part[j, CUTS + s : CUTS + s + 1, :]
                g_ref[r, at, :] = part[j, CUTS + 2 * count + r : CUTS + 2 * count + r + 1, :]
    scatter_apply(blocks, op_ref, zero_ref.at[pl.ds(0, count)], y_ref, col_ref, None)
    ghost_apply(blocks, g_ref, y_ref, col_ref, list_ref)
    inner = inner_rows()
    for r in range(count):
        a1_ref[r] = jnp.where(inner, pack(y_ref, r), 0.0)
    scatter_apply(blocks, op_ref, a1_ref, y_ref, col_ref, None)
    for r in range(count):
        a2_ref[r] = pack(y_ref, r)
    messages(up_ref, down_ref, a2_ref, send_ref, a1_ref)


def operator_rows(op_ref, x_ref, out_ref, column_ref, square_ref):
    column_ref[...] = jnp.zeros_like(column_ref)
    lanes = lane_ids()
    for r in range(column_ref.shape[0]):
        for n in range(NBLK):
            image = jnp.sum(op_ref[n] * x_ref[r, n + OFF : n + OFF + 1, :], axis=1, keepdims=True)
            column_ref[r] = jnp.where(lanes == n + OFF, image, column_ref[r])
        out_ref[r] = unpack_columns(column_ref, square_ref, r)


def ghost_kernel(op_ref, zero_ref, a1_ref, low_ref, high_ref, gop_ref, k0_ref, k1_ref, gram_ref, column_ref, square_ref):
    for part, first in ((low_ref, 0), (high_ref, IF)):
        for j in range(IF):
            weights = unflatten(lambda q: part[j, pl.ds(q, 8, stride=3), :])
            gop_ref[first + j] = make_operator(weights, gram_ref.at[j & 1])
    operator_rows(op_ref, zero_ref, k0_ref, column_ref, square_ref)
    operator_rows(op_ref, a1_ref, k1_ref, column_ref, square_ref)


def target_kernel(col_ref, list_ref, blocks, op_ref, gop_ref, zero_ref, b1_ref, y_ref, g_ref):
    count = b1_ref.shape[0]
    target = zero_ref.at[pl.ds(count, count)]
    scatter_apply(blocks, op_ref, target, y_ref, col_ref, None)
    ghost_images(gop_ref, target, g_ref)
    ghost_apply(blocks, g_ref, y_ref, col_ref, list_ref)
    inner = inner_rows()
    for r in range(count):
        b1_ref[r] = jnp.where(inner, pack(y_ref, r), 0.0)


def second_kernel(
    col_ref, list_ref, send_ref, edge_ref,
    blocks, ops_ref, gop_ref, zero_ref, a1_ref, a2_in, k0_ref, k1_ref, low_ref, high_ref, stats_ref,
    v1_ref, v2_ref, v3_ref, v4_ref, k3_ref, dots_ref, sigma_ref, up_ref, down_ref,
    y_ref, column_ref, square_ref, g_ref,
):
    count = a1_ref.shape[0]
    inner = inner_rows()
    squares, traces = stats_ref[0, :1], stats_ref[0, 1:]
    for s in range(1, stats_ref.shape[0]):
        squares = squares + stats_ref[s, :1]
        traces = traces + stats_ref[s, 1:]
    scale = 1.0 / (lax.axis_size("sub") * NBLK * BS)
    sigma = (1.0 + scale * whole_sum(squares)) * (scale * whole_sum(traces))
    sigma_ref[...] = jnp.broadcast_to(sigma, sigma_ref.shape)
    column_ref[...] = jnp.zeros_like(column_ref)
    v2_ref[...] = a2_in[...]
    complete(v2_ref, low_ref, high_ref, send_ref, edge_ref)
    for r in range(count):
        v1_ref[r] = a1_ref[r]
        for part, ghost, flag in ((low_ref, LOW, 0), (high_ref, HIGH, 1)):
            for j in range(IF):
                v1_ref[r, ghost + j : ghost + j + 1, :] = part[r, 16 + j : 17 + j, :]
        v1 = v1_ref[r] - sigma * zero_ref[r]
        v2_ref[r] = v2_ref[r] - sigma * v1_ref[r] - sigma * v1
        v1 = jnp.where(inner, v1, 0.0)
        v1_ref[r] = v1
        v0 = jnp.where(inner, zero_ref[r], 0.0)
        target = jnp.where(inner, zero_ref[count + r], 0.0)
        second = k1_ref[r] - sigma * k0_ref[r]
        dots_ref[r, 0] = tile_sum(v0, k0_ref[r])
        dots_ref[r, 1] = tile_sum(v1, k0_ref[r])
        dots_ref[r, 2] = tile_sum(v1, second)
        dots_ref[r, 8] = tile_sum(target, k0_ref[r])
        dots_ref[r, 9] = tile_sum(target, second)
    scatter_apply(blocks, ops_ref, v2_ref, y_ref, col_ref, column_ref)
    ghost_images(gop_ref, v2_ref, g_ref)
    ghost_apply(blocks, g_ref, y_ref, col_ref, list_ref)
    for r in range(count):
        image = unpack_columns(column_ref, square_ref, r)
        v3 = jnp.where(inner, pack(y_ref, r) - sigma * v2_ref[r], 0.0)
        v3_ref[r] = v3
        dots_ref[r, 3] = tile_sum(v1_ref[r], image)
        dots_ref[r, 4] = tile_sum(jnp.where(inner, v2_ref[r], 0.0), image)
        dots_ref[r, 5] = tile_sum(v3, image)
        dots_ref[r, 10] = tile_sum(jnp.where(inner, zero_ref[count + r], 0.0), image)
    scatter_apply(blocks, ops_ref, v3_ref, y_ref, col_ref, column_ref)
    for r in range(count):
        image = unpack_columns(column_ref, square_ref, r)
        dots_ref[r, 6] = tile_sum(v3_ref[r], image)
        dots_ref[r, 7] = jnp.zeros((8, LANES), f32)
        dots_ref[r, 11] = tile_sum(jnp.where(inner, zero_ref[count + r], 0.0), image)
        k3_ref[r] = image
        v4_ref[r] = pack(y_ref, r) - sigma * v3_ref[r]
    messages(up_ref, down_ref, v4_ref, send_ref)


def moment_kernel(send_ref, edge_ref, v4_in, k3_ref, low_ref, high_ref, dots_in, v4_ref, dots_ref):
    v4_ref[...] = v4_in[...]
    complete(v4_ref, low_ref, high_ref, send_ref, edge_ref)
    lane = lax.broadcasted_iota(jnp.int32, (8, LANES), 1)
    sub = lax.broadcasted_iota(jnp.int32, (8, LANES), 0)
    total = jnp.zeros((8, LANES), f32)
    for r in range(v4_ref.shape[0]):
        for d in range(12):
            part = tile_sum(v4_ref[r], k3_ref[r]) if d == 7 else dots_in[r, d]
            total = jnp.where((lane == d) & (sub == r), whole_sum(part), total)
    dots_ref[...] = total


def third_kernel(col_ref, list_ref, blocks, ops_ref, gop_ref, v4_ref, w5_ref, y_ref, g_ref):
    scatter_apply(blocks, ops_ref, v4_ref, y_ref, col_ref, None)
    ghost_images(gop_ref, v4_ref, g_ref)
    ghost_apply(blocks, g_ref, y_ref, col_ref, list_ref)
    for r in range(v4_ref.shape[0]):
        w5_ref[r] = pack(y_ref, r)


def combine(coef_ref, parts, g, r):
    total = None
    for s in USED[g]:
        term = coef_ref[g, s, r : r + 1, :] * parts[s]
        total = term if total is None else total + term
    return total


def sources(zero_ref, stored, r, count):
    v1_ref, v2_ref, v3_ref, v4_ref, w5_ref, b1_ref = stored
    parts = [zero_ref[r], v1_ref[r], v2_ref[r], v3_ref[r], v4_ref[r], w5_ref[r], zero_ref[count + r], b1_ref[r]]
    inner = inner_rows()
    return [jnp.where(inner, part, 0.0) for part in parts]


def fourth_kernel(col_ref, send_ref, blocks, ops_ref, sigma_ref, zero_ref, *refs):
    stored, sums = refs[:6], [part[...] for part in refs[6:-8]]
    first_ref, base_ref, rho_ref, coef_ref, scale_ref, up_ref, down_ref, y_ref = refs[-8:]
    while len(sums) > 1:
        sums = [sums[i] + sums[i + 1] for i in range(0, len(sums), 2)]
    sums = sums[0]
    column = lambda d: jnp.broadcast_to(sums[:, d : d + 1], (8, LANES))
    combos, scales = scalars([column(d) for d in range(8)], [column(8 + d) for d in range(4)], sigma_ref[...])
    for g, value in enumerate(scales):
        scale_ref[g] = value
    for g, combo in enumerate(combos):
        for s, value in enumerate(combo):
            if s in USED[g]:
                coef_ref[g, s] = value
    count = rho_ref.shape[0]
    for r in range(count):
        parts = sources(zero_ref, stored, r, count)
        first_ref[r] = combine(coef_ref, parts, 5, r)
        base_ref[r] = combine(coef_ref, parts, 7, r)
    scatter_apply(blocks, ops_ref, first_ref, y_ref, col_ref, None)
    for r in range(count):
        rho_ref[r] = base_ref[r] - scale_ref[0, r : r + 1, :] * pack(y_ref, r)
    messages(up_ref, down_ref, rho_ref, send_ref)


def early_kernel(coef_ref, zero_ref, *refs):
    stored, early_ref = refs[:6], refs[6]
    count = zero_ref.shape[0] // 2
    for r in range(count):
        parts = sources(zero_ref, stored, r, count)
        early_ref[pl.ds(r, NBLK, stride=EARLY), :] = parts[0][OFF:HIGH]
        for g, slot in ((0, 2), (1, 4), (2, 6), (4, 12), (3, 14)):
            early_ref[pl.ds(slot + r, NBLK, stride=EARLY), :] = combine(coef_ref, parts, g, r)[OFF:HIGH]
        for slot in (8, 10):
            early_ref[pl.ds(slot + r, NBLK, stride=EARLY), :] = jnp.zeros((NBLK, LANES), f32)


def answer_kernel(ops_ref, coef_ref, zero_ref, *refs):
    stored, (zeta_ref, sol_ref, x_ref, column_ref, square_ref) = refs[:6], refs[6:]
    count = zeta_ref.shape[1]
    for r in range(count):
        parts = sources(zero_ref, stored, r, count)
        zeta_ref[0, r] = combine(coef_ref, parts, 8, r)
        zeta_ref[1, r] = combine(coef_ref, parts, 6, r)
        x_ref[r] = combine(coef_ref, parts, 9, r)
    operator_rows(ops_ref, x_ref, sol_ref, column_ref, square_ref)


def fifth_kernel(
    col_ref, list_ref, send_ref, edge_ref,
    blocks, ops_ref, gop_ref, rho_in, base_ref, zeta_ref, scale_ref, low_ref, high_ref,
    late_ref, y_ref, rho_ref, g_ref,
):
    count = rho_in.shape[0]
    rho_ref[...] = rho_in[...]
    complete(rho_ref, low_ref, high_ref, send_ref, edge_ref)
    scatter_apply(blocks, ops_ref, rho_ref, y_ref, col_ref, None)
    ghost_images(gop_ref, rho_ref, g_ref)
    ghost_apply(blocks, g_ref, y_ref, col_ref, list_ref)
    for r in range(count):
        change = rho_ref[r] - base_ref[r]
        first = zeta_ref[0, r] + scale_ref[1, r : r + 1, :] * change - scale_ref[2, r : r + 1, :] * pack(y_ref, r)
        second = zeta_ref[1, r] + change
        late_ref[pl.ds(r, NBLK, stride=LATE), :] = first[OFF:HIGH]
        late_ref[pl.ds(2 + r, NBLK, stride=LATE), :] = second[OFF:HIGH]


def split(value):
    high = value.astype(jnp.bfloat16)
    return high, (value - high.astype(f32)).astype(jnp.bfloat16)


def product(first, second, dim):
    (fh, fl), (sh, sl) = split(first), split(second)
    left = jnp.concatenate([fh, fl, fh], axis=dim)
    right = jnp.concatenate([sh, sh, sl], axis=0)
    return lax.dot_general(left, right, (((dim,), (0,)), ((), ())), preferred_element_type=f32)


def mixed_kernel(*refs):
    early, (raw_ref, mixed_ref, weights_ref) = refs[:-3], refs[-3:]

    def step(group, carry):
        for i in range(CHUNK):
            at = pl.multiple_of((group * CHUNK + i) * EARLY, EARLY)
            resid = [ref[pl.ds(at, 8), :] for ref in early]
            zeta = [ref[pl.ds(at + 8, 8), :] for ref in early]
            left = jnp.concatenate(resid + zeta, axis=0)
            right = jnp.concatenate(zeta + resid, axis=0)
            mixed_ref[group * CHUNK + i] = product(left, right, 0)
            start = group * (8 * CUTS) + i
            weights_ref[group * CHUNK + i] = unflatten(lambda q: raw_ref[pl.ds(start + 8 * q, 8, stride=24), :])
        return carry

    lax.fori_loop(0, NBLK // CHUNK, step, 0)


def grad_kernel(*refs):
    peers = (len(refs) - 4) // 2
    early, late, mixed_ref, weights_ref, grad_ref, turn_ref = refs[:peers], refs[peers : 2 * peers], *refs[-4:]
    first = pl.program_id(0) * WIDE
    upper = lax.broadcasted_iota(jnp.int32, (8, LANES), 0) < LATE

    def join(tiles):
        out = []
        for q in range(0, len(tiles), 2):
            other = pltpu.roll(tiles[q + 1], LATE, 0) if q + 1 < len(tiles) else jnp.zeros((8, LANES), f32)
            out.append(jnp.where(upper, tiles[q], other))
        return out

    for i in range(WIDE):
        n = first + i
        at = pl.multiple_of(n * EARLY, EARLY)
        pair = pl.ds(pl.multiple_of(first * LATE + 8 * (i // 2), 8), 8)
        resid = join([ref[pl.ds(at, 8), :] for ref in early])
        zeta = [ref[pair, :] for ref in late]
        zeta = join([pltpu.roll(tile, LATE, 0) for tile in zeta] if i % 2 else zeta)
        left = jnp.concatenate(resid + zeta, axis=0)
        right = jnp.concatenate(zeta + resid, axis=0)
        grad = product(weights_ref[i], mixed_ref[n] + product(left, right, 0), 1)
        for t, tile in enumerate(flatten(grad)):
            turn_ref[i * CUTS + 8 * t : i * CUTS + 8 * t + 8, :] = tile
        if i % 8 == 7:
            for q in range(CUTS):
                start = (i - 7) * CUTS + 8 * (3 * (q // 24) + q % 3) + q % 24 // 3
                at = i // 8 * (8 * CUTS) + 8 * q
                grad_ref[at : at + 8, :] = turn_ref[pl.ds(start, 8, stride=CUTS), :]


def widening(parts, axis, step, most):
    if step is None:
        return parts, None
    size = lax.axis_size(axis)
    if size & (size - 1):
        return [lax.psum(parts[0], axis)], None
    step = step or 1
    while len(parts) > 1:
        parts = [parts[i] + parts[i + 1] for i in range(0, len(parts), 2)]
    width = min(most, size // step)
    total = parts[0]
    parts = [total] + [lax.ppermute(total, axis, [(i, i ^ (d * step)) for i in range(size)]) for d in range(1, width)]
    step *= width
    return parts, step if step < size else None


def all_of(values, axis):
    size = lax.axis_size(axis)
    return [values] + [
        lax.ppermute(values, axis, [(i, (i + d) % size) for i in range(size)]) for d in range(1, size)
    ]


def exchange(up, down):
    size = lax.axis_size("sub")
    rising = [(i, i + 1) for i in range(size - 1)]
    falling = [(j, i) for i, j in rising]
    return lax.ppermute(up, "sub", rising), lax.ppermute(down, "sub", falling)


def plus(first, second):
    if first is None:
        return second
    return first if second is None else first + second


def times(first, second):
    return None if first is None or second is None else first * second


def add(first, second, scale):
    size = max(len(first), len(second))
    first = list(first) + [None] * (size - len(first))
    second = list(second) + [None] * (size - len(second))
    return [plus(a, times(scale, b)) for a, b in zip(first, second)]


def scaled(first, scale):
    return [times(scale, a) for a in first]


def scalars(moments, products, sigma):
    one = jnp.ones_like(sigma)

    def inner(first, second):
        weights = [None] * (len(first) + len(second) - 1)
        for i, a in enumerate(first):
            for j, b in enumerate(second):
                weights[i + j] = plus(weights[i + j], a * b)
        total = None
        for weight, moment in zip(weights, moments):
            total = plus(total, weight * moment)
        return total

    def apply(poly):
        out = [None] * (len(poly) + 1)
        for j, value in enumerate(poly):
            out[j] = plus(out[j], sigma * value)
            out[j + 1] = plus(out[j + 1], value)
        return out

    resid = [[one]]
    direc = [[one]]
    image = []
    step, ratio, norm, curv = [], [None], [moments[0]], []
    for i in range(ITERS):
        image.append(apply(direc[i]))
        curv.append(inner(direc[i], image[i]))
        step.append(norm[i] / curv[i])
        if i + 1 < ITERS:
            resid.append(add(resid[i], image[i], -step[i]))
            norm.append(inner(resid[i + 1], resid[i + 1]))
            ratio.append(norm[i + 1] / norm[i])
            direc.append(add(resid[i + 1], direc[i], ratio[i + 1]))
    cot = []
    for i in range(ITERS):
        total = None
        for j, value in enumerate(resid[i]):
            total = plus(total, value * products[j])
        cot.append(total)
    along = [cot[0]]
    for i in range(1, ITERS):
        along.append(cot[i] + ratio[i] * along[i - 1])

    def row(poly):
        return list(poly) + [None] * (8 - len(poly))

    target = [None] * 6 + [one, None]
    resid_rows = [row(poly) for poly in resid]
    image_rows = [row(poly) for poly in image]
    inverse = [1.0 / value for value in step]

    def resid_prod(i):
        return [norm[l] if l == i else None for l in range(ITERS)]

    def image_prod(i):
        out = [None] * ITERS
        out[i] = norm[i] * inverse[i]
        if i + 1 < ITERS:
            out[i + 1] = -norm[i + 1] * inverse[i]
        return out

    def along_dir(prod, i):
        total = prod[0]
        for l in range(1, i + 1):
            total = plus(prod[l], times(ratio[l], total))
        return total

    def operator_prod(prod):
        out = []
        for l in range(ITERS - 1):
            value = times(add([prod[l]], [prod[l + 1]], -one)[0], inverse[l])
            if l > 0:
                back = times(add([prod[l - 1]], [prod[l]], -one)[0], inverse[l - 1])
                value = add([value], [back], -ratio[l])[0]
            out.append(value)
        return out + [None]

    last = ITERS - 1
    step_bar = along[last]
    curv_bar = -step_bar * step[last] / curv[last]
    dir_row = add(scaled(target, step[last]), image_rows[last], 2 * curv_bar)
    dir_prod = add(scaled(cot, step[last]), image_prod(last), 2 * curv_bar)
    norm_bar = step_bar / curv[last]
    rho_row = [None] * 8
    rho_prod = [None] * ITERS
    zetas = [None] * ITERS
    rho_rows = []
    for i in (2, 1, 0):
        ratio_bar = along_dir(dir_prod, i)
        full = norm_bar + ratio_bar / norm[i]
        zetas[i + 1] = add(dir_row, resid_rows[i + 1], full)
        rho_row = add(add(rho_row, zetas[i + 1], one), resid_rows[i + 1], full)
        rho_prod = add(add(rho_prod, dir_prod, one), resid_prod(i + 1), 2 * full)
        rho_rows.append(rho_row)
        step_bar = along[i] - (rho_prod[i] - rho_prod[i + 1]) * inverse[i]
        curv_bar = -step_bar * step[i] / curv[i]
        oper = [None] * 8
        if i == 2:
            for k in range(5):
                if k < 4:
                    oper[k] = plus(oper[k], times(sigma, rho_row[k]))
                    oper[k + 1] = plus(oper[k + 1], rho_row[k])
                else:
                    oper[5] = plus(oper[5], rho_row[4])
            oper[7] = rho_row[6]
        kept = add(scaled(dir_row, ratio[i + 1]), target, step[i])
        kept = add(kept, image_rows[i], 2 * curv_bar)
        dir_row = add(kept, oper, -step[i])
        dir_prod = add(add(scaled(dir_prod, ratio[i + 1]), cot, step[i]), image_prod(i), 2 * curv_bar)
        dir_prod = add(dir_prod, operator_prod(rho_prod), -step[i])
        norm_bar = step_bar / curv[i] - ratio_bar * norm[i + 1] / (norm[i] * norm[i])
    zetas[0] = add(dir_row, resid_rows[0], norm_bar)
    answer = [None] * 8
    for i in range(ITERS):
        answer = add(answer, row(direc[i]), step[i])
    combos = [resid_rows[1], resid_rows[2], resid_rows[3], zetas[3], zetas[2], rho_rows[1], zetas[1], rho_rows[2], zetas[0], answer]
    return combos, [step[1], ratio[1], step[0]]


def vmem():
    return pl.BlockSpec(memory_space=pltpu.VMEM)


def hbm():
    return pl.BlockSpec(memory_space=pltpu.HBM)


def smem():
    return pl.BlockSpec(memory_space=pltpu.SMEM)


def shards(stiffness, precond, rhs_vec, cotangent, col_index, send_rows, counts):
    count = rhs_vec.shape[0]
    sub = lax.axis_index("sub")
    size = lax.axis_size("sub")
    edge = jnp.stack([sub > 0, sub + 1 < size]).astype(jnp.int32)
    columns = col_index.T
    stiff_cuts = stiffness.reshape(NBLK, K, CUTS, LANES).transpose(0, 2, 1, 3).reshape(NBLK * K * CUTS, LANES)
    weight_cuts = precond.reshape(NBLK // 8, 8, CUTS, LANES).transpose(0, 2, 1, 3).reshape(NBLK * CUTS, LANES)
    base = jnp.concatenate([rhs_vec, cotangent], axis=0).reshape(2 * count, NBLK, BS)
    base = jnp.pad(base, ((0, 0), (OFF, ROWS - HIGH), (0, LANES - BS)))

    def shape(*dims):
        return jax.ShapeDtypeStruct(dims, f32)

    def call(kernel, name, scalars_in, arrays_in, outs, scratch, expected, specs=None, grid=(), in_specs=None):
        return pl.pallas_call(
            kernel,
            grid=grid,
            in_specs=in_specs or [smem()] * len(scalars_in) + [vmem()] * len(arrays_in),
            out_specs=specs or [vmem()] * len(outs),
            out_shape=outs,
            scratch_shapes=scratch,
            compiler_params=pltpu.CompilerParams(vmem_limit_bytes=8 * MIB),
            cost_estimate=pl.CostEstimate(flops=MIB, bytes_accessed=int(expected * 3.2e6), transcendentals=0),
            name=name,
        )(*scalars_in, *arrays_in)

    rows = shape(count, ROWS, LANES)
    message = shape(count, 16, LANES)
    longer = shape(count, 24, LANES)
    ghost_message = shape(IF, CUTS + 8, LANES)
    partial = lambda r: [[pltpu.VMEM((ROWS, 8, LANES), f32)] * r] * K
    turned = [pltpu.VMEM((count, BS, LANES), f32), pltpu.VMEM((LANES, LANES), f32)]
    held = lambda r: pltpu.VMEM((r, ROWS, LANES), f32)
    grams = pltpu.VMEM((4, BS, LANES), f32)

    up, down = call(
        pack_kernel, "pack", [send_rows], [weight_cuts, lax.slice_in_dim(stiff_cuts, 0, CHUNK * CUTS * K), base], [ghost_message] * 2, [], 3
    )
    near, far = exchange(up, down)

    (ops,) = call(
        operator_kernel, "operators", [], [weight_cuts], [shape(NBLK, BS, LANES)],
        [grams], 4, [vmem()], (NBLK // WIDE,),
        [pl.BlockSpec((WIDE * CUTS, LANES), lambda g: (g, 0))],
    )
    stats, partner = up[0, CUTS + 6 :], jnp.where(sub % 2 == 0, far[0, CUTS + 6 :], near[0, CUTS + 6 :])
    if size > 1 and size & (size - 1) == 0:
        stats, waiting = [stats + partner], 2
    else:
        stats, waiting = [stats], 0
    blocks, halo_list = call(
        blocks_kernel, "blocks", [columns], [stiff_cuts],
        [shape(NBLK, K, BS, LANES), jax.ShapeDtypeStruct((1, NBLK * K + 8), jnp.int32)],
        [pltpu.SMEM((1,), jnp.int32)], 5, [vmem(), smem()], (NBLK // CHUNK,),
        [smem(), pl.BlockSpec((CHUNK * CUTS * K, LANES), lambda g: (g, 0))],
    )

    near, far, blocks, stats = lax.optimization_barrier((near, far, blocks, stats))
    zero, a1, a2, up, down = call(
        first_kernel, "first", [columns, halo_list, send_rows, counts], [blocks, ops, base, near, far],
        [shape(2 * count, ROWS, LANES), rows, rows, longer, longer],
        [partial(count), held(count)], 6,
    )
    stats, a2 = lax.optimization_barrier((stats, a2))
    while waiting is not None and waiting < size:
        stats, waiting = widening(stats, "sub", waiting, 4)
    low, high = exchange(up, down)
    stats = jnp.stack(stats)

    gops, k0, k1 = call(
        ghost_kernel, "ghosts", [], [ops, zero, a1, near, far],
        [shape(2 * IF, BS, LANES), rows, rows], [grams, *turned], 3,
    )

    v1, v2, v3, v4, k3, dots, sigma, up, down = call(
        second_kernel, "second", [columns, halo_list, send_rows, edge],
        [blocks, ops, gops, zero, a1, a2, k0, k1, low, high, stats],
        [rows, rows, rows, rows, rows, shape(count, 12, 8, LANES), shape(8, LANES), message, message],
        [partial(count), *turned, held(count)], 7,
    )
    low, high = exchange(up, down)

    v4, dots = call(
        moment_kernel, "moments", [send_rows, edge], [v4, k3, low, high, dots], [rows, shape(8, LANES)], [], 0.8
    )
    sums, waiting = widening([dots], "sub", 0, 2)
    zero, v4 = lax.optimization_barrier((zero, v4))
    (b1,) = call(
        target_kernel, "target", [columns, halo_list], [blocks, ops, gops, zero], [rows],
        [partial(count), held(count)], 3,
    )
    sums, b1, v4 = lax.optimization_barrier((sums, b1, v4))
    while waiting is not None:
        sums, waiting = widening(sums, "sub", waiting, 4)

    (w5,) = call(
        third_kernel, "third", [columns, halo_list], [blocks, ops, gops, v4], [rows],
        [partial(count), held(count)], 4,
    )

    stored = [zero, v1, v2, v3, v4, w5, b1]
    first, fixed, rho, coefs, scales, up, down = call(
        fourth_kernel, "fourth", [columns, send_rows], [blocks, ops, sigma, *stored, *sums],
        [rows, rows, rows, shape(10, 8, 8, LANES), shape(3, 8, LANES), message, message], [partial(count)], 3,
    )
    (early,) = call(early_kernel, "early", [], [coefs, *stored], [shape(NBLK * EARLY, LANES)], [], 0.5)
    size = lax.axis_size("rhs")
    early = [early]
    if size == 4:
        early.append(lax.ppermute(early[0], "rhs", [(i, i ^ 2) for i in range(size)]))
    low, high = exchange(up, down)

    zeta, answer = call(
        answer_kernel, "answer", [], [ops, coefs, *stored],
        [shape(2, count, ROWS, LANES), rows], [held(count), *turned], 1.5,
    )
    early, low, high, zeta = lax.optimization_barrier((early, low, high, zeta))
    if size == 4:
        early = early + [lax.ppermute(part, "rhs", [(i, i ^ 1) for i in range(size)]) for part in early]
    else:
        early = all_of(early[0], "rhs")

    (late,) = call(
        fifth_kernel, "fifth", [columns, halo_list, send_rows, edge],
        [blocks, ops, gops, rho, fixed, zeta, scales, low, high],
        [shape(NBLK * LATE, LANES)], [partial(count), held(count), held(count)], 4,
    )
    if size == 4:
        late = [late] + [lax.ppermute(late, "rhs", [(i, i ^ d) for i in range(size)]) for d in (2, 1, 3)]
    else:
        late = all_of(late, "rhs")

    mixed, weights = call(
        mixed_kernel, "mixed", [], [*early, weight_cuts], [shape(NBLK, LANES, LANES), shape(NBLK, BS, LANES)], [], 3
    )
    (grad,) = call(
        grad_kernel, "grad", [], [*early, *late, mixed, weights], [shape(NBLK * CUTS, LANES)],
        [pltpu.VMEM((WIDE * CUTS, LANES), f32)], 10,
        [pl.BlockSpec((WIDE * CUTS, LANES), lambda g: (g, 0))], (NBLK // WIDE,),
        [vmem()] * (len(early) + len(late) + 1) + [pl.BlockSpec((WIDE, BS, LANES), lambda g: (g, 0, 0))],
    )
    grad = grad.reshape(NBLK // 8, CUTS, 8, LANES).transpose(0, 2, 1, 3).reshape(NBLK, BS * BS)
    return answer[:, OFF:HIGH, :BS].reshape(count, NBLK * BS), grad


def solution(mesh):
    in_specs = (
        P("sub", None, None),
        P("sub", None),
        P("rhs", "sub"),
        P("rhs", "sub"),
        P("sub", None),
        P("sub", None),
        P("sub"),
    )
    out_specs = (P("rhs", "sub"), P("sub", None))
    return jax.shard_map(shards, mesh=mesh, in_specs=in_specs, out_specs=out_specs, check_vma=False)
```
